32 devices in a mesh: dp: 8 (over z, x), tensor: 4 (over y, core).
Axes of the slice: x: 2, y: 2, z: 4, core: 2. Of those that a mesh axis runs over, the one named last changes fastest.
Arguments:
- frames: bfloat16 [48, 1024, 256], P('dp', 'tensor'), may hold values from -6 to 6
- lengths: int32 [48], P('dp'), may hold values from 513 to 1024, as said below
- w_qkv: bfloat16 [256, 768], replicated, may hold values from -0.375 to 0.375
- w_out: bfloat16 [256, 256], replicated, may hold values from -6 to 6
- b_out: float32 [256], replicated, may hold values from -2 to 2
- gain_one: float32 [256], replicated, may hold values from 0.5 to 1.5
- shift_one: float32 [256], replicated, may hold values from -3 to 3
- w_conv: bfloat16 [9, 256, 1024], P(None, None, 'tensor'), may hold values from -0.125 to 0.125
- b_conv: float32 [1024], P('tensor'), may hold values from -2 to 2
- w_proj: bfloat16 [1024, 256], P('tensor'), may hold values from -0.1875 to 0.1875
- b_proj: float32 [256], replicated, may hold values from -2 to 2
- gain_two: float32 [256], replicated, may hold values from 0.5 to 1.5
- shift_two: float32 [256], replicated, may hold values from -3 to 3
- cotangent: bfloat16 [48, 1024, 256], P('dp', 'tensor'), may hold values from -6 to 6
Outputs:
- output: bfloat16 [48, 1024, 256], P('dp', 'tensor')
- grad_frames: float32 [48, 1024, 256], P('dp', 'tensor')
- grad_qkv: float32 [256, 768], replicated
- grad_out: float32 [256, 256], replicated
- grad_b_out: float32 [256], replicated
- grad_gain_one: float32 [256], replicated
- grad_shift_one: float32 [256], replicated
- grad_conv: float32 [9, 256, 1024], P(None, None, 'tensor')
- grad_b_conv: float32 [1024], P('tensor')
- grad_proj: float32 [1024, 256], P('tensor')
- grad_b_proj: float32 [256], replicated
- grad_gain_two: float32 [256], replicated
- grad_shift_two: float32 [256], replicated
The draws below stay inside these ranges and needn't reach their ends.
Inputs may be any that keep to these rules, and one draw needn't show every extreme that they name: `lengths`: in each block of 6 utterances of one index of dp, one utterance has exactly 1024 frames.
All inputs are finite; a program needn't handle non-finite values.
Results may differ from the reference program's by a relative error of at most 0.017.
Values may be sent and summed in bfloat16 or wider, within the bound.
No kernel may reach another device: no remote copies, remote signals or barrier semaphores. Data moves between devices by JAX's collectives and lax.ppermute only.
A program may use at most 192 MiB of HBM per device.

```python
import jax
import jax.numpy as jnp
from jax import lax

D = 256
FF = 1024
KERNEL = 9
LEN = 1024
UTT_DEV = 6
UTT = 48


def draw_lengths(key, part):
    key = jax.random.fold_in(key, 11)
    base = jax.random.randint(key, (UTT,), LEN // 2 + 1, LEN + 1)
    chosen = jax.random.randint(jax.random.fold_in(key, 1), (UTT // UTT_DEV,), 0, UTT_DEV)
    slots = jnp.arange(UTT, dtype=jnp.int32)
    owner = slots // UTT_DEV
    picked = slots % UTT_DEV == chosen[owner]
    return jnp.where(picked, LEN, base).astype(jnp.int32)


def steps_of(stream_key, dims, split, smallest, high):
    level, own = 1.0, jax.random.fold_in(stream_key, 6)
    for position, blocks in split:
        draws = jnp.exp(jax.random.uniform(jax.random.fold_in(own, position), (blocks,), jnp.float32, smallest / len(split), high / len(split)))
        level = level * jnp.repeat(draws, dims[position] // blocks).reshape([-1 if axis == position else 1 for axis in range(len(dims))])
    return level


def normal_values(rng, dims, scale, most, pieces=(), kind=jnp.bfloat16):
    entries = jax.random.normal(rng, dims, jnp.float32) * scale
    if len(pieces) > 0:
        entries = steps_of(rng, dims, pieces, -0.22, 0.18) * entries
    return jnp.clip(entries, min=-most, max=most).astype(kind)


def setup_inputs(seed: int = 0) -> dict:
    seeds = jax.random.split(jax.random.key(seed), 15)
    return {
        "frames": normal_values(seeds[0], (UTT, LEN, D), 1.0, 6.0, ((0, 8), (1, 4))),
        "lengths": draw_lengths(jax.random.fold_in(seeds[14], 71), 0),
        "w_qkv": normal_values(seeds[2], (D, 3 * D), D ** -0.5, 0.375),
        "w_out": normal_values(seeds[3], (D, D), (max(1, D * 4 // LEN)) ** -0.5, 6.0),
        "b_out": normal_values(seeds[4], (D,), 0.3, 2.0, (), jnp.float32),
        "gain_one": jnp.clip(1.0 + 0.1 * jax.random.normal(seeds[5], (D,), jnp.float32), 0.5, 1.5),
        "shift_one": normal_values(seeds[6], (D,), 0.5, 3.0, (), jnp.float32),
        "w_conv": normal_values(seeds[7], (KERNEL, D, FF), (KERNEL * D) ** -0.5, 0.125, ((2, 4),)),
        "b_conv": normal_values(seeds[8], (FF,), 0.3, 2.0, ((0, 4),), jnp.float32),
        "w_proj": normal_values(seeds[9], (FF, D), FF ** -0.5, 0.1875, ((0, 4),)),
        "b_proj": normal_values(seeds[10], (D,), 0.3, 2.0, (), jnp.float32),
        "gain_two": jnp.clip(1.0 + 0.1 * jax.random.normal(seeds[11], (D,), jnp.float32), 0.5, 1.5),
        "shift_two": normal_values(seeds[12], (D,), 0.5, 3.0, (), jnp.float32),
        "cotangent": normal_values(seeds[13], (UTT, LEN, D), 1.0, 6.0, ((0, 8), (1, 4))),
    }


precise = lax.Precision.HIGHEST
epsilon = 1e-05

@jax.custom_vjp
def low(v):
    return lax.optimization_barrier(v.astype(jnp.bfloat16)).astype(jnp.float32)

@jax.custom_vjp
def low_back(v):
    return v

def low_keep(v):
    return (low(v), None)

def low_pass(kept, grad):
    return (grad,)

def back_keep(v):
    return (v, None)

def back_low(kept, grad):
    return (low(grad),)
low.defvjp(low_keep, low_pass)
low_back.defvjp(back_keep, back_low)

def layer_norm(inputs, gain, shift):
    centred = inputs - lax.optimization_barrier(jnp.mean(inputs, axis=-1, keepdims=True))
    variance = lax.optimization_barrier(jnp.mean(centred * centred, axis=-1, keepdims=True))
    return centred * lax.rsqrt(variance + epsilon) * gain + shift

def block_forward(frames, valid, w_qkv, w_out, b_out, gain_one, shift_one, w_conv, b_conv, w_proj, b_proj, gain_two, shift_two):
    length, width = frames.shape
    head_dim = width // 2
    projected = jnp.dot(frames, w_qkv, precision=precise)
    query_matrix = low(low_back(projected[:, :width])).reshape(length, 2, head_dim)
    key_matrix = low(low_back(projected[:, width:2 * width])).reshape(length, 2, head_dim)
    value_matrix = low(low_back(projected[:, 2 * width:])).reshape(length, 2, head_dim)
    scores = jnp.einsum('qhe,khe->hqk', query_matrix, key_matrix, precision=precise) * head_dim ** (-0.5)
    scores = low_back(scores)
    scores = jnp.where(valid[None, None, :] > 0.5, scores, -1000000000.0)
    weights = jax.nn.softmax(scores, axis=-1)
    mixture_output = jnp.einsum('hqk,khe->qhe', low(weights), value_matrix, precision=precise).reshape(length, width)
    mixture_output = low(low_back(mixture_output))
    attended = low_back(jnp.dot(mixture_output, w_out, precision=precise)) + b_out
    first = layer_norm(frames + attended, gain_one, shift_one) * valid[:, None]
    reach = w_conv.shape[0] // 2
    padded = jnp.pad(low(first), ((reach, reach), (0, 0)))
    conv_sum = jnp.zeros((length, w_conv.shape[2]), jnp.float32)
    for offset in range(w_conv.shape[0]):
        conv_sum = conv_sum + jnp.dot(padded[offset:offset + length], w_conv[offset], precision=precise)
    hidden = low_back(conv_sum) + b_conv
    active = low(jax.nn.gelu(hidden))
    branch = low_back(jnp.dot(active, w_proj, precision=precise)) + b_proj
    return layer_norm(first + branch, gain_two, shift_two) * valid[:, None]

def reference(frames, lengths, w_qkv, w_out, b_out, gain_one, shift_one, w_conv, b_conv, w_proj, b_proj, gain_two, shift_two, cotangent):
    params = (w_qkv.astype(jnp.float32), w_out.astype(jnp.float32), b_out, gain_one, shift_one, w_conv.astype(jnp.float32), b_conv, w_proj.astype(jnp.float32), b_proj, gain_two, shift_two)
    positions = jnp.arange(frames.shape[1], dtype=jnp.int32)

    def utterance(totals, inputs):
        rows, length, seed_grad = inputs
        valid = (positions < length).astype(jnp.float32)

        def apply(rows_in, *weights_in):
            return block_forward(rows_in, valid, *weights_in)
        output, pullback = jax.vjp(apply, rows.astype(jnp.float32), *params)
        gradients = pullback(seed_grad.astype(jnp.float32))
        totals = tuple((summed + gradient for summed, gradient in zip(totals, gradients[1:])))
        return (totals, (output.astype(jnp.bfloat16), gradients[0]))
    start = tuple((jnp.zeros_like(member) for member in params))
    totals, (outputs, input_grads) = lax.scan(utterance, start, (frames, lengths, cotangent))
    return (outputs, input_grads) + totals
```

```python
import functools
import itertools

import jax
import jax.experimental.pallas as pl
import jax.experimental.pallas.tpu as pltpu
import jax.numpy as jnp
import numpy as np
from jax import lax
from jax.sharding import PartitionSpec as P


EPSILON = 1e-05
F32 = jnp.float32
BF16 = jnp.bfloat16
HALO = 16
BLOCK = 256
MASKED = -1e30
GELU_A = float(np.sqrt(2.0 / np.pi))
GELU_B = 0.044715
LOG2E = float(np.log2(np.e))
VMEM_LIMIT = 58 * 2**20
SMALL_ROWS = 64


def params(**more):
    return pltpu.CompilerParams(vmem_limit_bytes=VMEM_LIMIT, **more)


def cost(flops, size):
    return pl.CostEstimate(flops=int(flops), bytes_accessed=int(size), transcendentals=0)


def dot(a, b):
    return jnp.dot(a, b, preferred_element_type=F32)


def dot_nt(a, b):
    return lax.dot_general(a, b, (((1,), (1,)), ((), ())), preferred_element_type=F32)


def dot_tn(a, b):
    return lax.dot_general(a, b, (((0,), (0,)), ((), ())), preferred_element_type=F32)


def at(start, size, step=HALO):
    return pl.ds(pl.multiple_of(start, step), size)


def up(value, step=HALO):
    return ((value + (step - 1)) // step) * step


def choose(index, options):
    result = options[-1]
    for i, option in enumerate(options[:-1]):
        result = jnp.where(index == i, option, result)
    return result


def plan(lengths):
    keys = [lengths[i] * 8 + i for i in range(6)]
    best, triples = None, None
    for pair in itertools.combinations(range(1, 6), 2):
        mine = (0,) + pair
        rest = tuple(i for i in range(6) if i not in mine)
        gap = jnp.abs(sum(lengths[i] for i in mine) - sum(lengths[i] for i in rest))
        option = [keys[i] for i in mine + rest]
        if best is None:
            best, triples = gap, option
        else:
            better = gap < best
            best = jnp.where(better, gap, best)
            triples = [jnp.where(better, new, old) for new, old in zip(option, triples)]
    whole, shared = [], []
    for a, b, c in (triples[:3], triples[3:]):
        a, b = jnp.maximum(a, b), jnp.minimum(a, b)
        a, c = jnp.maximum(a, c), jnp.minimum(a, c)
        b, c = jnp.maximum(b, c), jnp.minimum(b, c)
        whole += [a, b]
        shared.append(c)
    return whole, shared


class Rows:
    def __init__(self, lengths, length):
        self.member = lax.axis_index("tensor")
        whole, shared = plan(lengths)
        self.whole, self.shared = whole, shared
        role = self.member % 2
        second = self.member >= 2
        key_a = choose(self.member, whole)
        self.len_a = key_a // 8
        self.len_c = jnp.where(second, shared[1], shared[0]) // 8
        first_len = jnp.where(second, whole[2], whole[0]) // 8
        other_len = jnp.where(second, whole[3], whole[1]) // 8
        split = (other_len + self.len_c - first_len) // 2
        split = jnp.maximum((split + HALO // 2) // HALO * HALO, HALO)
        starts = role == 0
        self.own_from = jnp.where(starts, 0, split)
        self.own_to = jnp.where(starts, split, length)
        self.window = jnp.where(starts, 0, split - HALO)
        self.end = jnp.where(starts, jnp.minimum(split + HALO, self.len_c), self.len_c)
        self.rows_a = up(self.len_a) + HALO
        self.rows_c = jnp.maximum(up(self.end) - self.window, 0)
        self.tiles_a = (self.len_a + BLOCK - 1) // BLOCK
        self.tiles_c = (self.rows_c + BLOCK - 1) // BLOCK
        self.blocks = (self.rows_a + self.rows_c + BLOCK - 1) // BLOCK
        self.halo = self.rows_a + jnp.where(starts, split, 0)

    def masks(self, start, size):
        row = start + lax.broadcasted_iota(jnp.int32, (size, 1), 0)
        in_a = row < self.rows_a
        frame = jnp.where(in_a, row, row - self.rows_a + self.window)
        live = frame < jnp.where(in_a, self.len_a, self.end)
        inside = (frame >= self.own_from) & (frame < self.own_to)
        return live, live & (in_a | inside)

    def frames_at(self, part, index):
        return at(BLOCK * index + (self.window if part else 0), BLOCK)

    def base(self, part, index):
        return BLOCK * index + (self.rows_a if part else 0)


def place(member, pieces, target, part=None):
    quarter = pieces[0].shape[1]
    for distance, piece in enumerate(pieces):
        rows = at((member ^ distance) * quarter, quarter, quarter)
        if part is None:
            target[:, rows, :] = piece[...]
        else:
            target[rows, :] = piece[part]


def pick(lengths, frames, cotangent, *rest):
    targets, sems = rest[:-1], rest[-1]
    member = lax.axis_index("tensor")
    whole, shared = plan(lengths)
    copies = []
    for kind, source in enumerate((frames, cotangent)):
        for distance in range(4):
            there = member ^ distance
            for part in range(2):
                key = jnp.where(there >= 2, shared[1], shared[0]) if part else choose(there, whole)
                copies.append(
                    pltpu.make_async_copy(
                        source.at[key % 8], targets[4 * kind + distance].at[part], sems.at[len(copies)]
                    )
                )
                copies[-1].start()
    for copy in copies:
        copy.wait()


def softmax_parts(rows, part, length):
    return (rows.len_c if part else rows.len_a), lax.broadcasted_iota(jnp.int32, (1, length), 1)


def mask_keys(scores, column, limit):
    half = scores.shape[1] // 2
    tail = jnp.where(column[:, half:] < limit, scores[:, half:], MASKED)
    return jnp.concatenate([scores[:, :half], tail], axis=1)


def attention_forward(
    lengths, r0, r1, r2, r3, w_qkv, w_out, b_out, normed, stats, mixed, placed, qkv, valued
):
    quarter = r0.shape[1]
    length = 4 * quarter
    width = r0.shape[2]
    head = width // 2
    scale = head ** (-0.5) * LOG2E
    rows = Rows(lengths, length)
    spare = placed.shape[1] - length
    placed[:, length:, :] = jnp.zeros((2, spare, width), BF16)
    place(rows.member, (r0, r1, r2, r3), placed)
    mixed[...] = jnp.zeros(mixed.shape, BF16)
    for part in range(2):
        for h in range(2):
            valued[part, h, :, head:] = jnp.ones((length, head), BF16)

    def project(index, carry):
        here = at(index * BLOCK, BLOCK, BLOCK)
        for part in range(2):
            value = dot(placed[part, here, :], w_qkv[...]).astype(BF16)
            qkv[part, here, :] = value[:, : 2 * width]
            for h in range(2):
                valued[part, h, here, :head] = value[:, 2 * width + h * head : 2 * width + (h + 1) * head]
        return carry

    lax.fori_loop(0, length // BLOCK, project, 0)
    qkv[:, length:, :] = jnp.zeros((2, spare, 2 * width), BF16)
    lane = lax.broadcasted_iota(jnp.int32, (1, 128), 1)

    def tile(part, index, carry):
        frames_at = rows.frames_at(part, index)
        here = at(rows.base(part, index), BLOCK)
        limit, column = softmax_parts(rows, part, length)
        mixtures, logs = [], []
        for h in range(2):
            low, high = h * head, (h + 1) * head
            scores = dot_nt(qkv[part, frames_at, low:high], qkv[part, :length, width + low : width + high])
            scores = mask_keys(scores, column, limit)
            highest = jnp.max(scores, axis=-1, keepdims=True) * scale
            exponent = jnp.exp2(scores * scale - highest).astype(BF16)
            summed = dot(exponent, valued[part, h])
            total = summed[:, head : head + 1]
            mixtures.append((summed[:, :head] / total).astype(BF16))
            logs.append(highest + jnp.log2(total))
        mixture = jnp.concatenate(mixtures, axis=1)
        mixed[here, :] = mixture
        residual = placed[part, frames_at, :].astype(F32) + dot(mixture, w_out[...]) + b_out[...]
        centred = residual - jnp.mean(residual, axis=-1, keepdims=True)
        inverse = lax.rsqrt(jnp.mean(centred * centred, axis=-1, keepdims=True) + EPSILON)
        normed[here, :] = centred * inverse
        stats[here, :] = jnp.where(lane == 0, logs[0], jnp.where(lane == 1, logs[1], inverse))
        return carry

    lax.fori_loop(0, rows.tiles_a, functools.partial(tile, 0), 0)
    lax.fori_loop(0, rows.tiles_c, functools.partial(tile, 1), 0)


def gelu_pair(x):
    square = x * x
    t = jnp.tanh(GELU_A * x * (1.0 + GELU_B * square))
    half = 0.5 * (1.0 + t)
    slope = half + (0.5 * GELU_A) * x * (1.0 - t * t) * (1.0 + 3.0 * GELU_B * square)
    return x * half, slope


def load_filters(near, far, target, sems):
    width = near[0].shape[1]
    piece = near[0].shape[0] // 4
    shift = lax.axis_index("dp") % 4
    copies = []
    for j, source in enumerate(near):
        copies.append((source, target.at[:, pl.ds(j * width, width)]))
    for j, source in enumerate(far):
        for i in range(4):
            there = at((shift ^ i) * piece, piece)
            part = pl.ds((2 + j) * width, width)
            copies.append((source.at[pl.ds(i * piece, piece)], target.at[there, part]))
    copies = [
        pltpu.make_async_copy(source, there, sems.at[i]) for i, (source, there) in enumerate(copies)
    ]
    for copy in copies:
        copy.start()
    return copies


FILTER_COPIES = 10


def feed_forward(
    lengths,
    normed,
    c0,
    c1,
    c2,
    c3,
    pack0,
    pack1,
    far0,
    far1,
    gain_one,
    shift_one,
    b_proj,
    gain_two,
    shift_two,
    o0,
    o1,
    o2,
    o3,
    kept0,
    kept1,
    kept2,
    sent0,
    sent1,
    sent2,
    d_hidden,
    dz_two,
    small,
    conv_bias,
    weights,
    first,
    columns,
    slope,
    active,
    d_branch,
    cot_frames,
    cot_rows,
    out_rows,
    out_c,
    sems,
):
    quarter, width = c0.shape[1:]
    length = 4 * quarter
    filters = weights.shape[1]
    taps = columns.shape[1] // width
    depth = taps * width
    reach = taps // 2
    loads = load_filters((pack0, pack1), (far0, far1), weights, sems)
    rows = Rows(lengths, length)
    blocks = rows.blocks
    place(rows.member, (c0, c1, c2, c3), cot_frames)
    cot_frames[:, length:, :] = jnp.zeros((2, cot_frames.shape[1] - length, width), BF16)
    cot_rows[0:length, :] = cot_frames[0, 0:length, :]

    def gather_cot(index, carry):
        cot_rows[at(rows.base(1, index), BLOCK), :] = cot_frames[1, rows.frames_at(1, index), :]
        return carry

    lax.fori_loop(0, rows.tiles_c, gather_cot, 0)
    out_rows[...] = jnp.zeros(out_rows.shape, BF16)
    small[...] = jnp.zeros(small.shape, F32)
    conv_bias[...] = jnp.zeros(conv_bias.shape, F32)

    first[0:HALO, :] = jnp.zeros((HALO, width), F32)

    def make_first(index, carry):
        base = index * BLOCK
        live, _ = rows.masks(base, BLOCK)
        value = normed[at(base, BLOCK), :] * gain_one[...] + shift_one[...]
        first[at(base + HALO, BLOCK), :] = jnp.where(live, value, 0.0)
        return carry

    lax.fori_loop(0, blocks, make_first, 0)
    first[at(blocks * BLOCK + HALO, HALO), :] = jnp.zeros((HALO, width), F32)
    for copy in loads:
        copy.wait()

    def block(index, carry):
        base = index * BLOCK
        here = at(base, BLOCK, BLOCK)
        live, own = rows.masks(base, BLOCK)
        around = first[at(base + HALO - 8, BLOCK + 16, 8), :]
        for k in range(taps):
            columns[here, k * width : (k + 1) * width] = around[8 - reach + k : 8 - reach + k + BLOCK].astype(BF16)
        branch = jnp.zeros((BLOCK, width), F32)
        for j in range(filters // width):
            part = slice(j * width, (j + 1) * width)
            bias = weights[depth + width : depth + width + 1, part].astype(F32) + weights[
                depth + width + 16 : depth + width + 17, part
            ].astype(F32)
            hidden = dot(columns[here, :], weights[0:depth, part]) + bias
            value, derivative = gelu_pair(hidden)
            value = value.astype(BF16)
            active[here, part] = value
            slope[here, part] = derivative
            branch = branch + dot(value, weights[depth : depth + width, part])
        residual = first[at(base + HALO, BLOCK), :] + branch + b_proj[...]
        centred = residual - jnp.mean(residual, axis=-1, keepdims=True)
        inverse = lax.rsqrt(jnp.mean(centred * centred, axis=-1, keepdims=True) + EPSILON)
        normed_two = centred * inverse
        out_rows[here, :] = jnp.where(own, normed_two * gain_two[...] + shift_two[...], 0.0).astype(BF16)
        upstream = jnp.where(live, cot_rows[here, :].astype(F32), 0.0)
        counted = jnp.where(own, upstream, 0.0)
        scaled = upstream * gain_two[...]
        dz = inverse * (
            scaled
            - jnp.mean(scaled, axis=-1, keepdims=True)
            - normed_two * jnp.mean(scaled * normed_two, axis=-1, keepdims=True)
        )
        dz_two[here, :] = dz
        small[3:4, :] += jnp.sum(jnp.where(own, dz, 0.0), axis=0, keepdims=True)
        small[4:5, :] += jnp.sum(counted * normed_two, axis=0, keepdims=True)
        small[5:6, :] += jnp.sum(counted, axis=0, keepdims=True)
        low = dz.astype(BF16)
        d_branch[here, :] = jnp.where(own, low, jnp.zeros_like(low))
        for j in range(filters // width):
            part = slice(j * width, (j + 1) * width)
            grad = dot_nt(low, weights[depth : depth + width, part]) * slope[here, part]
            conv_bias[0:1, part] += jnp.sum(jnp.where(own, grad, 0.0), axis=0, keepdims=True)
            d_hidden[here, part] = grad.astype(BF16)
        return carry

    lax.fori_loop(0, blocks, block, 0)

    columns[at(rows.halo, HALO), :] = jnp.zeros((HALO, columns.shape[1]), BF16)

    kept, sent = (kept0, kept1, kept2), (sent0, sent1, sent2)
    per_chunk = taps // 3
    for count in range(2, active.shape[0] // BLOCK + 1):

        @pl.when(blocks == count)
        def _():
            n = count * BLOCK
            for chunk in range(3):

                def tap(k, carry):
                    here = at((chunk * per_chunk + k) * width, width, width)
                    grads = dot_tn(columns[0:n, here], d_hidden[0:n, :]).astype(BF16)
                    there = at(k * width, width, width)
                    for j in range(filters // width):
                        (kept, sent)[j % 2][chunk][j // 2, there, :] = grads[:, j * width : (j + 1) * width]
                    return carry

                lax.fori_loop(0, per_chunk, tap, 0)
            grads = dot_tn(active[0:n, :], d_branch[0:n, :]).astype(BF16)
            for j in range(filters // width):
                (kept, sent)[j % 2][2][j // 2, per_chunk * width :, :] = grads[j * width : (j + 1) * width, :]

    out_c[...] = jnp.zeros(out_c.shape, BF16)

    def scatter_out(index, carry):
        out_c[rows.frames_at(1, index), :] = out_rows[at(rows.base(1, index), BLOCK), :]
        return carry

    lax.fori_loop(0, rows.tiles_c, scatter_out, 0)
    for distance, target in enumerate((o0, o1, o2, o3)):
        start = (rows.member ^ distance) * quarter
        there = at(start, quarter, quarter)
        row = start + lax.broadcasted_iota(jnp.int32, (quarter, 1), 0)
        value = out_rows[there, :]
        target[0, :, :] = jnp.where(row < rows.len_a, value, jnp.zeros_like(value))
        target[1, :, :] = out_c[there, :]


def conv_backward(
    lengths,
    d_hidden,
    pack0,
    pack1,
    far0,
    far1,
    dz_two,
    normed,
    stats,
    mixed,
    w_out,
    gain_one,
    small_two,
    dz_one,
    d_mixed,
    soft,
    grad_out,
    small,
    weights,
    spread,
    sems,
):
    width = normed.shape[1]
    head = width // 2
    taps = spread.shape[1] // width
    reach = taps // 2
    loads = load_filters((pack0, pack1), (far0, far1), weights, sems)
    rows = Rows(lengths, 4 * width)
    blocks = rows.blocks
    dz_one[...] = jnp.zeros(dz_one.shape, F32)
    d_mixed[...] = jnp.zeros(d_mixed.shape, BF16)
    soft[...] = jnp.full(soft.shape, -MASKED, F32)
    small[...] = small_two[...]
    grad_out[...] = jnp.zeros(grad_out.shape, F32)
    spread[0:HALO, :] = jnp.zeros((HALO, spread.shape[1]), F32)
    spread[at(blocks * BLOCK + HALO, HALO), :] = jnp.zeros((HALO, spread.shape[1]), F32)
    for copy in loads:
        copy.wait()

    def back(index, carry):
        base = index * BLOCK
        value = d_hidden[at(base, BLOCK, BLOCK), :]
        for k in range(taps):
            part = slice(k * width, (k + 1) * width)
            spread[at(base + HALO, BLOCK), part] = dot_nt(value, weights[part, :])
        return carry

    lax.fori_loop(0, blocks, back, 0)
    lane = lax.broadcasted_iota(jnp.int32, (1, 128), 1)

    def block(index, carry):
        base = index * BLOCK
        here = at(base, BLOCK, BLOCK)
        _, own = rows.masks(base, BLOCK)
        total = dz_two[here, :]
        for k in range(taps):
            around = spread[at(base + HALO - 8, BLOCK + 16, 8), k * width : (k + 1) * width]
            total = total + around[8 + reach - k : 8 + reach - k + BLOCK]
        total = jnp.where(own, total, 0.0)
        unit = jnp.where(own, normed[here, :], 0.0)
        kept = stats[here, :]
        inverse = kept[:, 2:3]
        scaled = total * gain_one[...]
        dz = inverse * (
            scaled
            - jnp.mean(scaled, axis=-1, keepdims=True)
            - unit * jnp.mean(scaled * unit, axis=-1, keepdims=True)
        )
        dz = jnp.where(own, dz, 0.0)
        dz_one[here, :] = dz
        small[0:1, :] += jnp.sum(dz, axis=0, keepdims=True)
        small[1:2, :] += jnp.sum(total * unit, axis=0, keepdims=True)
        small[2:3, :] += jnp.sum(total, axis=0, keepdims=True)
        low = dz.astype(BF16)
        upstream = dot_nt(low, w_out[...]).astype(BF16)
        d_mixed[here, :] = upstream
        mixture = mixed[here, :]
        grad_out[...] += dot_tn(mixture, low)
        product = upstream.astype(F32) * mixture.astype(F32)
        means = [jnp.sum(product[:, h * head : (h + 1) * head], axis=-1, keepdims=True) for h in range(2)]
        soft[here, :] = jnp.where(
            lane < 2, jnp.where(own, kept, -MASKED), jnp.where(lane == 2, means[0], means[1])
        )
        return carry

    lax.fori_loop(0, blocks, block, 0)


def attention_backward(part, ties, *refs):
    (lengths, r0, r1, r2, r3, d_mixed, soft, dz_one, w_qkv), refs = refs[:9], refs[9:]
    extra = 4 * part
    inputs, refs = refs[:extra], refs[extra + ties :]
    targets, refs = refs[:4], refs[4:]
    if part:
        (late_kept, late_sent), refs = refs[:2], refs[2:]
    else:
        grad_qkv, refs = refs[0], refs[1:]
    placed, qkv, d_proj, keys, values, frame_grads = refs[:6]
    quarter = r0.shape[1]
    length = 4 * quarter
    width = r0.shape[2]
    head = width // 2
    scale = head ** (-0.5)
    rows = Rows(lengths, length)
    spare = placed.shape[0] - length
    placed[length:, :] = jnp.zeros((spare, width), BF16)
    place(rows.member, (r0, r1, r2, r3), placed, part)
    d_proj[...] = jnp.zeros(d_proj.shape, BF16)
    keys[...] = jnp.zeros(keys.shape, F32)
    values[...] = jnp.zeros(values.shape, F32)

    def project(index, carry):
        here = at(index * BLOCK, BLOCK, BLOCK)
        qkv[here, :] = dot(placed[here, :], w_qkv[...]).astype(BF16)
        return carry

    lax.fori_loop(0, length // BLOCK, project, 0)
    qkv[length:, :] = jnp.zeros((spare, 3 * width), BF16)

    def tile(index, carry):
        frames_at = rows.frames_at(part, index)
        base = rows.base(part, index)
        here = at(base, BLOCK)
        limit, column = softmax_parts(rows, part, length)
        inside = base + lax.broadcasted_iota(jnp.int32, (BLOCK, 1), 0) < rows.rows_a
        for h in range(2):
            low, high = h * head, (h + 1) * head
            query = qkv[frames_at, low:high]
            key = qkv[:length, width + low : width + high]
            value = qkv[:length, 2 * width + low : 2 * width + high]
            upstream = d_mixed[here, low:high]
            shift = soft[here, h : h + 1]
            mean = soft[here, 2 + h : 3 + h]
            if part == 0:
                shift = jnp.where(inside, shift, -MASKED)
            scores = mask_keys(dot_nt(query, key), column, limit)
            weights = jnp.exp2(scores * (scale * LOG2E) - shift)
            d_weights = dot_nt(upstream, value)
            d_scores = (weights * (d_weights - mean)).astype(BF16)
            d_proj[frames_at, low:high] = (dot(d_scores, key) * scale).astype(BF16)
            keys[:, low:high] += dot_tn(d_scores, query)
            values[:, low:high] += dot_tn(weights.astype(BF16), upstream)
        return carry

    lax.fori_loop(0, rows.tiles_c if part else rows.tiles_a, tile, 0)
    d_proj[0:length, width : 2 * width] = (keys[...] * scale).astype(BF16)
    d_proj[0:length, 2 * width : 3 * width] = values[...].astype(BF16)
    if part == 0:
        row = lax.broadcasted_iota(jnp.int32, (length, 1), 0)
        frame_grads[0:length, :] = jnp.where(row < rows.len_a, dz_one[0:length, :], 0.0)
    else:
        frame_grads[...] = jnp.zeros(frame_grads.shape, F32)

        def scatter(index, carry):
            frame_grads[rows.frames_at(1, index), :] = dz_one[at(rows.base(1, index), BLOCK), :]
            return carry

        lax.fori_loop(0, rows.tiles_c, scatter, 0)
    for distance, target in enumerate(targets):
        here = at((rows.member ^ distance) * quarter, quarter, quarter)
        target[...] = (frame_grads[here, :] + dot_nt(d_proj[here, :], w_qkv[...])).astype(BF16)
    grads = dot_tn(placed[0:length, :], d_proj[0:length, :])
    if part == 0:
        grad_qkv[...] = grads
        return
    blocks = refs[6]
    grad_before, grad_out, small, conv_bias = inputs
    grads = (grads + grad_before[...]).astype(BF16)
    for q in range(3):
        blocks[q, :, :] = grads[:, q * width : (q + 1) * width]
    blocks[3, :, :] = grad_out[...].astype(BF16)
    line = lax.broadcasted_iota(jnp.int32, (8, 1), 0)
    for j in range(4):
        target = (late_kept, late_sent)[j % 2]
        target[j // 2, 0:width, :] = blocks[rows.member ^ j]
        bias = conv_bias[0:1, j * width : (j + 1) * width]
        tail = jnp.where(line == 6, bias, small[...])
        tail = jnp.concatenate([tail, jnp.zeros((SMALL_ROWS - 8, width), F32)], axis=0)
        target[j // 2, width : width + SMALL_ROWS, :] = tail.astype(BF16)


def collect(paired, lengths, *refs):
    pieces, result = refs[:-1], refs[-1]
    if paired:
        whole_parts = [piece[0] for piece in pieces]
        shared_parts = [piece[1] for piece in pieces]
    else:
        whole_parts = [piece[...] for piece in pieces[:4]]
        shared_parts = [piece[...] for piece in pieces[4:]]
    member = lax.axis_index("tensor")
    whole, shared = plan(lengths)
    for distance in range(4):
        slot = choose(member ^ distance, whole) % 8
        result[slot] = whole_parts[distance].astype(result.dtype)
    for side in range(2):
        second = (member >= 2) == (side == 0)
        slot = jnp.where(second, shared[1], shared[0]) % 8
        total = shared_parts[2 * side].astype(F32) + shared_parts[2 * side + 1].astype(F32)
        result[slot] = total.astype(result.dtype)


def finish_late(own, p1, p2, p3, *refs):
    grad_qkv, grad_out = refs[:2]
    vectors, blocks = refs[2:-1], refs[-1]
    width = grad_out.shape[0]
    member = lax.axis_index("tensor")
    for distance, piece in enumerate((own, p1, p2, p3)):
        blocks[member ^ distance] = piece[0:width, :].astype(F32)
    for q in range(3):
        grad_qkv[:, q * width : (q + 1) * width] = blocks[q]
    grad_out[...] = blocks[3]
    tail = own[width : width + 16, :].astype(F32)
    for i, vector in enumerate(vectors):
        vector[...] = tail[i : i + 1, :]


def finish_filters(steps, *refs):
    parts, (grad_conv, grad_proj, work) = refs[:-3], refs[-3:]
    where = lax.axis_index("dp")
    depth = grad_conv.shape[0]
    start = 0
    for step, value, other in zip(steps, parts[::2], parts[1::2]):
        half = value.shape[0]
        bit = (where // step) % 2
        work[at(start + bit * half, half), :] = value[...]
        work[at(start + (1 - bit) * half, half), :] = other[...]
        start += 2 * half
    grad_conv[...] = work[0:depth, :].astype(F32)
    grad_proj[...] = work[depth:, :].astype(F32)


def shards(
    frames,
    lengths,
    w_qkv,
    w_out,
    b_out,
    gain_one,
    shift_one,
    w_conv,
    b_conv,
    w_proj,
    b_proj,
    gain_two,
    shift_two,
    cotangent,
):
    count, quarter, width = frames.shape
    length = 4 * quarter
    taps = w_conv.shape[0]
    depth = taps * width
    filters = 4 * w_conv.shape[2]
    padded = length + BLOCK
    space = 2 * length
    limit = 7 * BLOCK
    smem = pl.BlockSpec(memory_space=pltpu.SMEM)
    vmem = pl.BlockSpec(memory_space=pltpu.VMEM)
    anywhere = pl.BlockSpec(memory_space=pl.ANY)
    shape = jax.ShapeDtypeStruct
    dp_size = lax.axis_size("dp")
    dp_place = lax.axis_index("dp")
    b_out, gain_one, shift_one, b_proj, gain_two, shift_two = [
        v[None] for v in (b_out, gain_one, shift_one, b_proj, gain_two, shift_two)
    ]

    def hop(value, distance):
        return lax.ppermute(value, "tensor", [(i, i ^ distance) for i in range(4)])

    def dp_hop(value, distance):
        return lax.ppermute(value, "dp", [(i, i ^ distance) for i in range(dp_size)])

    def after(value, *others):
        return lax.optimization_barrier((value,) + others)[0]

    picked = pl.pallas_call(
        pick,
        out_shape=[shape((2, quarter, width), BF16)] * 8,
        in_specs=[smem, anywhere, anywhere],
        out_specs=[anywhere] * 8,
        scratch_shapes=[pltpu.SemaphoreType.DMA((16,))],
        compiler_params=params(),
        name="pick",
    )(lengths, frames, cotangent)
    frame_parts = [picked[0]] + [hop(picked[d], d) for d in (1, 2, 3)]

    b_high = b_conv.astype(BF16)
    b_low = (b_conv - b_high.astype(F32)).astype(BF16)
    pack = jnp.concatenate(
        [
            w_conv.reshape(depth, width),
            w_proj,
            jnp.broadcast_to(b_high[None], (16, width)),
            jnp.broadcast_to(b_low[None], (48, width)),
        ]
    )
    piece = pack.shape[0] // 4
    mine = lax.dynamic_slice_in_dim(pack, (dp_place % 4) * piece, piece, 0)
    far0 = hop(mine, 2)
    near_pack = hop(pack, 1)
    far0 = after(far0, *frame_parts)
    far1, far2 = dp_hop(far0, 1), dp_hop(far0, 2)

    cot_ready = [after(picked[4 + d], near_pack, *frame_parts) for d in range(4)]
    cot_parts = [cot_ready[0]] + [hop(cot_ready[d], d) for d in (1, 2, 3)]

    rows = length + length // 2
    normed, stats, mixed = pl.pallas_call(
        attention_forward,
        out_shape=(
            shape((space, width), F32),
            shape((space, 128), F32),
            shape((space, width), BF16),
        ),
        in_specs=[smem] + [vmem] * 7,
        out_specs=[vmem] * 3,
        scratch_shapes=[
            pltpu.VMEM((2, padded, width), BF16),
            pltpu.VMEM((2, padded, 2 * width), BF16),
            pltpu.VMEM((2, 2, length, width), BF16),
        ],
        compiler_params=params(),
        cost_estimate=cost(2 * rows * 2.5e6, 10e6),
        name="attention_forward",
    )(lengths, *frame_parts, w_qkv, w_out, b_out)

    far1, far2 = after((far1, far2), normed)
    far3 = jnp.concatenate([dp_hop(far2[: piece // 2], 1), dp_hop(far1[piece // 2 :], 2)])
    far_pack = jnp.concatenate([far0, far1, far2, far3])
    far_near_pack = hop(far_pack, 1)
    packs = (pack, near_pack, far_pack, far_near_pack)

    per_chunk = depth // 3
    sizes = [per_chunk, per_chunk, per_chunk + width]
    result = pl.pallas_call(
        feed_forward,
        out_shape=[shape((2, quarter, width), BF16)] * 4
        + [shape((2, n, width), BF16) for n in sizes] * 2
        + [
            shape((limit, filters), BF16),
            shape((limit, width), F32),
            shape((8, width), F32),
            shape((8, filters), F32),
        ],
        in_specs=[smem] + [vmem] * 5 + [anywhere] * 4 + [vmem] * 5,
        out_specs=[vmem] * 14,
        scratch_shapes=[
            pltpu.VMEM((pack.shape[0], filters), BF16),
            pltpu.VMEM((space + 2 * HALO, width), F32),
            pltpu.VMEM((limit, depth), BF16),
            pltpu.VMEM((limit, filters), F32),
            pltpu.VMEM((limit, filters), BF16),
            pltpu.VMEM((limit, width), BF16),
            pltpu.VMEM((2, padded, width), BF16),
            pltpu.VMEM((space, width), BF16),
            pltpu.VMEM((space, width), BF16),
            pltpu.VMEM((padded, width), BF16),
            pltpu.SemaphoreType.DMA((FILTER_COPIES,)),
        ],
        compiler_params=params(),
        cost_estimate=cost(2 * rows * 6e6, 30e6),
        name="feed_forward",
    )(lengths, normed, *cot_parts, *packs, gain_one, shift_one, b_proj, gain_two, shift_two)
    outputs, kept, sent = result[:4], result[4:7], result[7:10]
    d_hidden, dz_two, small_two, conv_bias = result[10:]

    def add(a, b):
        return (a.astype(F32) + b.astype(F32)).astype(BF16)

    def halves(value, step):
        half = value.shape[-2] // 2
        bit = (dp_place // step) % 2
        axis = value.ndim - 2
        parts = value.reshape(value.shape[:-2] + (2, half, width))
        keep = lax.dynamic_index_in_dim(parts, bit, axis, keepdims=False)
        send = lax.dynamic_index_in_dim(parts, 1 - bit, axis, keepdims=False)
        return keep, dp_hop(send, step)

    def halve(value, step):
        return add(*halves(value, step))

    def double(value, step):
        bit = (dp_place // step) % 2
        other = dp_hop(value, step)
        return jnp.where(bit == 0, jnp.concatenate([value, other]), jnp.concatenate([other, value]))

    def begin(value, step):
        return (value[0], hop(value[1], 2)) if step == 0 else halves(value, step)

    def spread_out(parts):
        return [parts[0]] + [hop(parts[d], d) for d in (1, 2, 3)]

    def collected(parts, dtype, name):
        return pl.pallas_call(
            functools.partial(collect, len(parts) == 4),
            out_shape=shape((count, quarter, width), dtype),
            in_specs=[smem] + [vmem] * len(parts),
            out_specs=vmem,
            compiler_params=params(),
            name=name,
        )(lengths, *parts)

    more = [2**i for i in range(2, 20) if 2**i < dp_size]
    orders = [[1, 2, 0] + more, [2, 0, 1] + more, [0, 1, 2] + more]
    moving = [(kept[c], hop(sent[c], 1)) for c in range(3)]
    out_parts = spread_out(outputs)

    dz_one, d_mixed, soft, grad_out, small = pl.pallas_call(
        conv_backward,
        out_shape=(
            shape((space, width), F32),
            shape((space, width), BF16),
            shape((space, 128), F32),
            shape((width, width), F32),
            shape((8, width), F32),
        ),
        in_specs=[smem, vmem] + [anywhere] * 4 + [vmem] * 7,
        out_specs=[vmem] * 5,
        scratch_shapes=[
            pltpu.VMEM((pack.shape[0], filters), BF16),
            pltpu.VMEM((limit + 2 * HALO, depth), F32),
            pltpu.SemaphoreType.DMA((FILTER_COPIES,)),
        ],
        compiler_params=params(),
        cost_estimate=cost(2 * rows * 2.5e6, 15e6),
        name="conv_backward",
    )(lengths, d_hidden, *packs, dz_two, normed, stats, mixed, w_out, gain_one, small_two)

    def attention_back(part, inputs, ties):
        late_rows = width + SMALL_ROWS
        more_outs = [shape((2, late_rows, width), BF16)] * 2 if part else [shape((width, 3 * width), F32)]
        return pl.pallas_call(
            functools.partial(attention_backward, part, len(ties)),
            out_shape=[shape((quarter, width), BF16)] * 4 + more_outs,
            in_specs=[smem] + [vmem] * (8 + len(inputs)) + [anywhere] * len(ties),
            out_specs=[vmem] * (4 + len(more_outs)),
            scratch_shapes=[
                pltpu.VMEM((padded, width), BF16),
                pltpu.VMEM((padded, 3 * width), BF16),
                pltpu.VMEM((padded, 3 * width), BF16),
                pltpu.VMEM((length, width), F32),
                pltpu.VMEM((length, width), F32),
                pltpu.VMEM((padded, width), F32),
            ]
            + [pltpu.VMEM((4, width, width), BF16)] * part,
            compiler_params=params(),
            cost_estimate=cost(rows * 4e6, 8e6),
            name=f"attention_backward_{'ac'[part]}",
        )(lengths, *frame_parts, d_mixed, soft, dz_one, w_qkv, *inputs, *ties)

    moving = [(keep, after(other, dz_one)) for keep, other in moving]
    state = [add(*pair) for pair in moving]
    moving = [begin(value, order[0]) for value, order in zip(state, orders)]
    *grads_a, grad_qkv = attention_back(0, [], state)
    moving = [(keep, after(other, grad_qkv)) for keep, other in moving]
    state = [add(*pair) for pair in moving]
    moving = [begin(value, order[1]) for value, order in zip(state, orders)]
    a_parts = spread_out(grads_a)
    *grads_c, late_kept, late_sent = attention_back(1, [grad_qkv, grad_out, small, conv_bias], state)
    moving = [(keep, after(other, late_kept)) for keep, other in moving]
    state = [add(*pair) for pair in moving]
    for stage in range(2, len(orders[0])):
        state = [add(*begin(value, order[stage])) for value, order in zip(state, orders)]
    backs = [[step for step in reversed(order) if step] for order in orders]
    for stage in range(len(backs[0]) - 1):
        state = [double(value, back[stage]) for value, back in zip(state, backs)]
    last = [back[-1] for back in backs]
    others = [dp_hop(value, step) for value, step in zip(state, last)]
    grad_conv, grad_proj = pl.pallas_call(
        functools.partial(finish_filters, last),
        out_shape=(shape((depth, width), F32), shape((width, width), F32)),
        in_specs=[vmem] * 6,
        out_specs=[vmem] * 2,
        scratch_shapes=[pltpu.VMEM((depth + width, width), BF16)],
        compiler_params=params(),
        name="finish_filters",
    )(*[part for pair in zip(state, others) for part in pair])
    output = collected(out_parts, BF16, "collect_output")
    d_frames = collected(a_parts + spread_out(grads_c), F32, "collect_grad")

    late = add(late_kept, hop(late_sent, 1))
    late = add(late[0], hop(late[1], 2))
    steps = [1, 2] + more
    for step in steps:
        late = halve(late, step)
    for step in reversed(steps):
        late = double(late, step)
    body = late[:width]
    grad_qkv, grad_out, *vectors = pl.pallas_call(
        finish_late,
        out_shape=[shape((width, 3 * width), F32), shape((width, width), F32)] + [shape((1, width), F32)] * 7,
        in_specs=[vmem] * 4,
        out_specs=[vmem] * 9,
        scratch_shapes=[pltpu.VMEM((4, width, width), F32)],
        compiler_params=params(),
        name="finish_late",
    )(late, *[hop(body, d) for d in (1, 2, 3)])
    vectors = [v.reshape(width) for v in vectors]
    return (
        output,
        d_frames,
        grad_qkv,
        grad_out,
        vectors[0],
        vectors[1],
        vectors[2],
        grad_conv.reshape(w_conv.shape),
        vectors[6],
        grad_proj,
        vectors[3],
        vectors[4],
        vectors[5],
    )


def solution(mesh):
    return jax.shard_map(
        shards,
        mesh=mesh,
        in_specs=(
            P("dp", "tensor", None),
            P("dp"),
            P(),
            P(),
            P(),
            P(),
            P(),
            P(None, None, "tensor"),
            P("tensor"),
            P("tensor", None),
            P(),
            P(),
            P(),
            P("dp", "tensor", None),
        ),
        out_specs=(
            P("dp", "tensor", None),
            P("dp", "tensor", None),
            P(),
            P(),
            P(),
            P(),
            P(),
            P(None, None, "tensor"),
            P("tensor"),
            P("tensor", None),
            P(),
            P(),
            P(),
        ),
        check_vma=False,
    )
```

```python
import functools
import itertools

import jax
import jax.experimental.pallas as pl
import jax.experimental.pallas.tpu as pltpu
import jax.numpy as jnp
import numpy as np
from jax import lax
from jax.sharding import PartitionSpec as P


EPSILON = 1e-05
F32 = jnp.float32
BF16 = jnp.bfloat16
HALO = 16
BLOCK = 256
MASKED = -1e30
GELU_A = float(np.sqrt(2.0 / np.pi))
GELU_B = 0.044715
LOG2E = float(np.log2(np.e))
VMEM_LIMIT = 58 * 2**20
SMALL_ROWS = 64


def params(**more):
    return pltpu.CompilerParams(vmem_limit_bytes=VMEM_LIMIT, **more)


def cost(flops, size):
    return pl.CostEstimate(flops=int(flops), bytes_accessed=int(size), transcendentals=0)


def dot(a, b):
    return jnp.dot(a, b, preferred_element_type=F32)


def dot_nt(a, b):
    return lax.dot_general(a, b, (((1,), (1,)), ((), ())), preferred_element_type=F32)


def dot_tn(a, b):
    return lax.dot_general(a, b, (((0,), (0,)), ((), ())), preferred_element_type=F32)


def at(start, size, step=HALO):
    return pl.ds(pl.multiple_of(start, step), size)


def up(value, step=HALO):
    return ((value + (step - 1)) // step) * step


def choose(index, options):
    result = options[-1]
    for i, option in enumerate(options[:-1]):
        result = jnp.where(index == i, option, result)
    return result


def plan(lengths):
    keys = [lengths[i] * 8 + i for i in range(6)]
    best, triples = None, None
    for pair in itertools.combinations(range(1, 6), 2):
        mine = (0,) + pair
        rest = tuple(i for i in range(6) if i not in mine)
        gap = jnp.abs(sum(lengths[i] for i in mine) - sum(lengths[i] for i in rest))
        option = [keys[i] for i in mine + rest]
        if best is None:
            best, triples = gap, option
        else:
            better = gap < best
            best = jnp.where(better, gap, best)
            triples = [jnp.where(better, new, old) for new, old in zip(option, triples)]
    whole, shared = [], []
    for a, b, c in (triples[:3], triples[3:]):
        a, b = jnp.maximum(a, b), jnp.minimum(a, b)
        a, c = jnp.maximum(a, c), jnp.minimum(a, c)
        b, c = jnp.maximum(b, c), jnp.minimum(b, c)
        whole += [a, b]
        shared.append(c)
    return whole, shared


def tied(kernel, inputs, ties):
    return lambda *refs: kernel(*refs[:inputs], *refs[inputs + ties :])


class Rows:
    def __init__(self, lengths, length):
        self.member = lax.axis_index("tensor")
        whole, shared = plan(lengths)
        self.whole, self.shared = whole, shared
        role = self.member % 2
        second = self.member >= 2
        key_a = choose(self.member, whole)
        self.len_a = key_a // 8
        self.len_c = jnp.where(second, shared[1], shared[0]) // 8
        first_len = jnp.where(second, whole[2], whole[0]) // 8
        other_len = jnp.where(second, whole[3], whole[1]) // 8
        split = (other_len + self.len_c - first_len) // 2
        split = jnp.maximum((split + HALO // 2) // HALO * HALO, HALO)
        starts = role == 0
        self.own_from = jnp.where(starts, 0, split)
        self.own_to = jnp.where(starts, split, length)
        self.window = jnp.where(starts, 0, split - HALO)
        self.end = jnp.where(starts, jnp.minimum(split + HALO, self.len_c), self.len_c)
        self.rows_a = up(self.len_a) + HALO
        self.rows_c = jnp.maximum(up(self.end) - self.window, 0)
        self.tiles_a = (self.len_a + BLOCK - 1) // BLOCK
        self.tiles_c = (self.rows_c + BLOCK - 1) // BLOCK
        self.blocks = (self.rows_a + self.rows_c + BLOCK - 1) // BLOCK
        self.halo = self.rows_a + jnp.where(starts, split, 0)

    def masks(self, start, size):
        row = start + lax.broadcasted_iota(jnp.int32, (size, 1), 0)
        in_a = row < self.rows_a
        frame = jnp.where(in_a, row, row - self.rows_a + self.window)
        live = frame < jnp.where(in_a, self.len_a, self.end)
        inside = (frame >= self.own_from) & (frame < self.own_to)
        return live, live & (in_a | inside)

    def frames_at(self, part, index):
        return at(BLOCK * index + (self.window if part else 0), BLOCK)

    def base(self, part, index):
        return BLOCK * index + (self.rows_a if part else 0)


def place(member, pieces, target, part=None):
    quarter = pieces[0].shape[1]
    for distance, piece in enumerate(pieces):
        rows = at((member ^ distance) * quarter, quarter, quarter)
        if part is None:
            target[:, rows, :] = piece[...]
        else:
            target[rows, :] = piece[part]


def pick(lengths, source, *targets):
    member = lax.axis_index("tensor")
    whole, shared = plan(lengths)
    for distance, target in enumerate(targets):
        there = member ^ distance
        target[0] = source[choose(there, whole) % 8]
        target[1] = source[jnp.where(there >= 2, shared[1], shared[0]) % 8]


def softmax_parts(rows, part, length):
    return (rows.len_c if part else rows.len_a), lax.broadcasted_iota(jnp.int32, (1, length), 1)


def mask_keys(scores, column, limit):
    half = scores.shape[1] // 2
    tail = jnp.where(column[:, half:] < limit, scores[:, half:], MASKED)
    return jnp.concatenate([scores[:, :half], tail], axis=1)


def attention_forward(
    lengths, r0, r1, r2, r3, w_qkv, w_out, b_out, normed, stats, mixed, placed, qkv, valued, n_out, s_out, m_out, sems
):
    quarter = r0.shape[1]
    length = 4 * quarter
    width = r0.shape[2]
    head = width // 2
    scale = head ** (-0.5) * LOG2E
    rows = Rows(lengths, length)
    spare = placed.shape[1] - length
    placed[:, length:, :] = jnp.zeros((2, spare, width), BF16)
    place(rows.member, (r0, r1, r2, r3), placed)
    for part in range(2):
        for h in range(2):
            valued[part, h, :, head:] = jnp.ones((length, head), BF16)

    def project(index, carry):
        here = at(index * BLOCK, BLOCK, BLOCK)
        for part in range(2):
            value = dot(placed[part, here, :], w_qkv[...]).astype(BF16)
            qkv[part, here, :] = value[:, : 2 * width]
            for h in range(2):
                valued[part, h, here, :head] = value[:, 2 * width + h * head : 2 * width + (h + 1) * head]
        return carry

    lax.fori_loop(0, length // BLOCK, project, 0)
    qkv[:, length:, :] = jnp.zeros((2, spare, 2 * width), BF16)
    lane = lax.broadcasted_iota(jnp.int32, (1, 128), 1)

    def copies(part, index):
        there = at(rows.base(part, index), BLOCK)
        here = at(index * BLOCK, BLOCK, BLOCK)
        pairs = ((n_out, normed), (s_out, stats), (m_out, mixed))
        return [
            pltpu.make_async_copy(source.at[part, here], target.at[there], sems.at[part, i, index])
            for i, (source, target) in enumerate(pairs)
        ]

    def tile(part, index, carry):
        frames_at = rows.frames_at(part, index)
        here = at(index * BLOCK, BLOCK, BLOCK)
        limit, column = softmax_parts(rows, part, length)
        mixtures, logs = [], []
        for h in range(2):
            low, high = h * head, (h + 1) * head
            scores = dot_nt(qkv[part, frames_at, low:high], qkv[part, :length, width + low : width + high])
            scores = mask_keys(scores, column, limit)
            highest = jnp.max(scores, axis=-1, keepdims=True) * scale
            exponent = jnp.exp2(scores * scale - highest).astype(BF16)
            summed = dot(exponent, valued[part, h])
            total = summed[:, head : head + 1]
            mixtures.append((summed[:, :head] / total).astype(BF16))
            logs.append(highest + jnp.log2(total))
        mixture = jnp.concatenate(mixtures, axis=1)
        m_out[part, here, :] = mixture
        residual = placed[part, frames_at, :].astype(F32) + dot(mixture, w_out[...]) + b_out[...]
        centred = residual - jnp.mean(residual, axis=-1, keepdims=True)
        inverse = lax.rsqrt(jnp.mean(centred * centred, axis=-1, keepdims=True) + EPSILON)
        n_out[part, here, :] = centred * inverse
        s_out[part, here, :] = jnp.where(lane == 0, logs[0], jnp.where(lane == 1, logs[1], inverse))
        for copy in copies(part, index):
            copy.start()
        return carry

    def finish(part, index, carry):
        for copy in copies(part, index):
            copy.wait()
        return carry

    for part, count in enumerate((rows.tiles_a, rows.tiles_c)):
        lax.fori_loop(0, count, functools.partial(tile, part), 0)
        lax.fori_loop(0, count, functools.partial(finish, part), 0)


def gelu_pair(x):
    square = x * x
    t = jnp.tanh(GELU_A * x * (1.0 + GELU_B * square))
    half = 0.5 * (1.0 + t)
    slope = half + (0.5 * GELU_A) * x * (1.0 - t * t) * (1.0 + 3.0 * GELU_B * square)
    return x * half, slope


def load_filters(near, far, target, sems):
    width = near[0].shape[1]
    piece = near[0].shape[0] // 4
    shift = lax.axis_index("dp") % 4
    copies = []
    for j, source in enumerate(near):
        copies.append((source, target.at[:, pl.ds(j * width, width)]))
    for j, source in enumerate(far):
        for i in range(4):
            there = at((shift ^ i) * piece, piece)
            part = pl.ds((2 + j) * width, width)
            copies.append((source.at[pl.ds(i * piece, piece)], target.at[there, part]))
    copies = [
        pltpu.make_async_copy(source, there, sems.at[i]) for i, (source, there) in enumerate(copies)
    ]
    for copy in copies:
        copy.start()
    return copies


FILTER_COPIES = 10


def feed_forward(
    lengths,
    normed,
    c0,
    c1,
    c2,
    c3,
    pack0,
    pack1,
    far0,
    far1,
    gain_one,
    shift_one,
    b_proj,
    gain_two,
    shift_two,
    o0,
    o1,
    o2,
    o3,
    kept0,
    kept1,
    sent0,
    sent1,
    d_hidden_out,
    dz_out,
    conv_out,
    small,
    conv_bias,
    weights,
    units,
    first,
    columns,
    hidden,
    slope,
    active,
    d_branch,
    d_hidden,
    dz_two,
    grads,
    cot_frames,
    cot_rows,
    out_rows,
    out_c,
    load_sems,
    unit_sems,
    out_sems,
    grad_sems,
    conv_sem,
):
    quarter, width = c0.shape[1:]
    length = 4 * quarter
    filters = weights.shape[1]
    taps = columns.shape[1] // width
    depth = taps * width
    reach = taps // 2
    loads = load_filters((pack0, pack1), (far0, far1), weights, load_sems)
    rows = Rows(lengths, length)
    blocks = rows.blocks

    def unit_copy(index):
        here = at(index * BLOCK, BLOCK, BLOCK)
        return pltpu.make_async_copy(normed.at[here], units.at[here], unit_sems.at[index])

    def start_unit(index, carry):
        unit_copy(index).start()
        return carry

    lax.fori_loop(0, blocks, start_unit, 0)
    place(rows.member, (c0, c1, c2, c3), cot_frames)
    cot_frames[:, length:, :] = jnp.zeros((2, cot_frames.shape[1] - length, width), BF16)
    cot_rows[0:length, :] = cot_frames[0, 0:length, :]

    def gather_cot(index, carry):
        cot_rows[at(rows.base(1, index), BLOCK), :] = cot_frames[1, rows.frames_at(1, index), :]
        return carry

    lax.fori_loop(0, rows.tiles_c, gather_cot, 0)
    out_rows[...] = jnp.zeros(out_rows.shape, BF16)
    small[...] = jnp.zeros(small.shape, F32)
    conv_bias[...] = jnp.zeros(conv_bias.shape, F32)

    first[0:HALO, :] = jnp.zeros((HALO, width), F32)

    def make_first(index, carry):
        base = index * BLOCK
        unit_copy(index).wait()
        live, _ = rows.masks(base, BLOCK)
        value = units[at(base, BLOCK), :] * gain_one[...] + shift_one[...]
        first[at(base + HALO, BLOCK), :] = jnp.where(live, value, 0.0)
        return carry

    lax.fori_loop(0, blocks, make_first, 0)
    first[at(blocks * BLOCK + HALO, HALO), :] = jnp.zeros((HALO, width), F32)

    def make_columns(index, carry):
        base = index * BLOCK
        around = first[at(base + HALO - 8, BLOCK + 16, 8), :]
        for k in range(taps):
            columns[at(base, BLOCK, BLOCK), k * width : (k + 1) * width] = around[
                8 - reach + k : 8 - reach + k + BLOCK
            ].astype(BF16)
        return carry

    lax.fori_loop(0, blocks, make_columns, 0)
    for copy in loads:
        copy.wait()
    conv_copy = pltpu.make_async_copy(weights.at[pl.ds(0, depth)], conv_out, conv_sem.at[0])
    conv_copy.start()

    def out_copies(index):
        here = at(index * BLOCK, BLOCK, BLOCK)
        return [
            pltpu.make_async_copy(d_hidden.at[here], d_hidden_out.at[here], out_sems.at[0, index]),
            pltpu.make_async_copy(dz_two.at[here], dz_out.at[here], out_sems.at[1, index]),
        ]

    def conv(index, target):
        target[...] = dot(columns[at(index * BLOCK, BLOCK, BLOCK), :], weights[0:depth, :])

    def rest(index, source):
        base = index * BLOCK
        here = at(base, BLOCK, BLOCK)
        live, own = rows.masks(base, BLOCK)
        branch = jnp.zeros((BLOCK, width), F32)
        for j in range(filters // width):
            part = slice(j * width, (j + 1) * width)
            bias = weights[depth + width : depth + width + 1, part].astype(F32) + weights[
                depth + width + 16 : depth + width + 17, part
            ].astype(F32)
            value, derivative = gelu_pair(source[:, part] + bias)
            value = value.astype(BF16)
            active[here, part] = value
            slope[:, part] = derivative
            branch = branch + dot(value, weights[depth : depth + width, part])
        residual = first[at(base + HALO, BLOCK), :] + branch + b_proj[...]
        centred = residual - jnp.mean(residual, axis=-1, keepdims=True)
        inverse = lax.rsqrt(jnp.mean(centred * centred, axis=-1, keepdims=True) + EPSILON)
        normed_two = centred * inverse
        out_rows[here, :] = jnp.where(own, normed_two * gain_two[...] + shift_two[...], 0.0).astype(BF16)
        upstream = jnp.where(live, cot_rows[here, :].astype(F32), 0.0)
        counted = jnp.where(own, upstream, 0.0)
        scaled = upstream * gain_two[...]
        dz = inverse * (
            scaled
            - jnp.mean(scaled, axis=-1, keepdims=True)
            - normed_two * jnp.mean(scaled * normed_two, axis=-1, keepdims=True)
        )
        dz_two[here, :] = dz
        small[3:4, :] += jnp.sum(jnp.where(own, dz, 0.0), axis=0, keepdims=True)
        small[4:5, :] += jnp.sum(counted * normed_two, axis=0, keepdims=True)
        small[5:6, :] += jnp.sum(counted, axis=0, keepdims=True)
        low = dz.astype(BF16)
        d_branch[here, :] = jnp.where(own, low, jnp.zeros_like(low))
        for j in range(filters // width):
            part = slice(j * width, (j + 1) * width)
            grad = dot_nt(low, weights[depth : depth + width, part]) * slope[:, part]
            conv_bias[0:1, part] += jnp.sum(jnp.where(own, grad, 0.0), axis=0, keepdims=True)
            d_hidden[here, part] = grad.astype(BF16)
        for copy in out_copies(index):
            copy.start()

    even, odd = hidden.at[0], hidden.at[1]
    conv(0, even)

    def step(pair, carry):
        index = 2 * pair
        conv(index + 1, odd)
        rest(index, even)
        conv(index + 2, even)
        rest(index + 1, odd)
        return carry

    lax.fori_loop(0, (blocks - 1) // 2, step, 0)

    @pl.when(blocks % 2 == 1)
    def _():
        rest(blocks - 1, even)

    @pl.when(blocks % 2 == 0)
    def _():
        conv(blocks - 1, odd)
        rest(blocks - 2, even)
        rest(blocks - 1, odd)

    columns[at(rows.halo, HALO), :] = jnp.zeros((HALO, columns.shape[1]), BF16)

    kept, sent = (kept0, kept1), (sent0, sent1)
    per_chunk = (taps + 1) // 2

    def grad_copies(k, chunk):
        here = at(k * width, width, width)
        there = at((k - chunk * per_chunk) * width, width, width)
        return [
            pltpu.make_async_copy(
                grads.at[j, here], (kept, sent)[j % 2][chunk].at[j // 2, there], grad_sems.at[k, j]
            )
            for j in range(filters // width)
        ]

    for count in range(3, active.shape[0] // BLOCK + 1):

        @pl.when(blocks == count)
        def _():
            n = count * BLOCK

            def tap(k, carry):
                here = at(k * width, width, width)
                value = dot_tn(columns[0:n, here], d_hidden[0:n, :]).astype(BF16)
                for j in range(filters // width):
                    grads[j, here, :] = value[:, j * width : (j + 1) * width]
                for chunk in range(2):

                    @pl.when(k // per_chunk == chunk)
                    def _():
                        for copy in grad_copies(k, chunk):
                            copy.start()

                return carry

            lax.fori_loop(0, taps, tap, 0)
            value = dot_tn(active[0:n, :], d_branch[0:n, :]).astype(BF16)
            for j in range(filters // width):
                grads[j, depth:, :] = value[j * width : (j + 1) * width, :]
            for copy in grad_copies(taps, 1):
                copy.start()

    out_c[...] = jnp.zeros(out_c.shape, BF16)

    def scatter_out(index, carry):
        out_c[rows.frames_at(1, index), :] = out_rows[at(rows.base(1, index), BLOCK), :]
        return carry

    lax.fori_loop(0, rows.tiles_c, scatter_out, 0)
    for distance, target in enumerate((o0, o1, o2, o3)):
        start = (rows.member ^ distance) * quarter
        there = at(start, quarter, quarter)
        row = start + lax.broadcasted_iota(jnp.int32, (quarter, 1), 0)
        value = out_rows[there, :]
        target[0, :, :] = jnp.where(row < rows.len_a, value, jnp.zeros_like(value))
        target[1, :, :] = out_c[there, :]

    conv_copy.wait()

    def finish(index, carry):
        for copy in out_copies(index):
            copy.wait()
        return carry

    lax.fori_loop(0, blocks, finish, 0)

    def finish_grads(chunk, k, carry):
        for copy in grad_copies(k, chunk):
            copy.wait()
        return carry

    lax.fori_loop(0, per_chunk, functools.partial(finish_grads, 0), 0)
    lax.fori_loop(per_chunk, 2 * per_chunk, functools.partial(finish_grads, 1), 0)


def conv_backward(
    lengths,
    d_hidden_in,
    conv,
    dz_in,
    normed_in,
    stats_in,
    mixed_in,
    w_out,
    gain_one,
    small_two,
    dz_out,
    d_mixed_out,
    soft_out,
    grad_out,
    small,
    weights,
    d_hidden,
    dz_two,
    normed,
    stats,
    mixed,
    dz_one,
    d_mixed,
    soft,
    spread,
    conv_sems,
    in_sems,
    out_sems,
):
    width = normed.shape[1]
    head = width // 2
    taps = spread.shape[1] // width
    reach = taps // 2
    rows = Rows(lengths, 4 * width)
    blocks = rows.blocks

    def block_copies(pairs, sems, index):
        here = at(index * BLOCK, BLOCK, BLOCK)
        return [
            pltpu.make_async_copy(source.at[here], target.at[here], sems.at[i, index])
            for i, (source, target) in enumerate(pairs)
        ]

    conv_copies = [
        pltpu.make_async_copy(
            conv.at[pl.ds(k * width, width)], weights.at[pl.ds(k * width, width)], conv_sems.at[k]
        )
        for k in range(taps)
    ]
    into = ((d_hidden_in, d_hidden), (dz_in, dz_two), (normed_in, normed), (stats_in, stats), (mixed_in, mixed))
    onto = ((dz_one, dz_out), (d_mixed, d_mixed_out), (soft, soft_out))
    conv_copies[0].start()

    def start_hidden(index, carry):
        block_copies(into, in_sems, index)[0].start()
        return carry

    def start_rest(index, carry):
        for copy in block_copies(into, in_sems, index)[1:]:
            copy.start()
        return carry

    lax.fori_loop(0, blocks, start_hidden, 0)
    for copy in conv_copies[1:]:
        copy.start()
    lax.fori_loop(0, blocks, start_rest, 0)
    small[...] = small_two[...]
    grad_out[...] = jnp.zeros(grad_out.shape, F32)
    spread[0:HALO, :] = jnp.zeros((HALO, spread.shape[1]), F32)
    spread[at(blocks * BLOCK + HALO, HALO), :] = jnp.zeros((HALO, spread.shape[1]), F32)

    group = 9
    for k in range(0, taps, group):
        for copy in conv_copies[k : k + group]:
            copy.wait()

        def back(index, carry):
            base = index * BLOCK
            if k == 0:
                block_copies(into, in_sems, index)[0].wait()
            for tap in range(k, k + group):
                part = slice(tap * width, (tap + 1) * width)
                spread[at(base + HALO, BLOCK), part] = dot_nt(d_hidden[at(base, BLOCK, BLOCK), :], weights[part, :])
            return carry

        lax.fori_loop(0, blocks, back, 0)
    lane = lax.broadcasted_iota(jnp.int32, (1, 128), 1)

    def block(index, carry):
        base = index * BLOCK
        here = at(base, BLOCK, BLOCK)
        for copy in block_copies(into, in_sems, index)[1:]:
            copy.wait()
        _, own = rows.masks(base, BLOCK)
        total = dz_two[here, :]
        for k in range(taps):
            around = spread[at(base + HALO - 8, BLOCK + 16, 8), k * width : (k + 1) * width]
            total = total + around[8 + reach - k : 8 + reach - k + BLOCK]
        total = jnp.where(own, total, 0.0)
        unit = jnp.where(own, normed[here, :], 0.0)
        kept = stats[here, :]
        inverse = kept[:, 2:3]
        scaled = total * gain_one[...]
        dz = inverse * (
            scaled
            - jnp.mean(scaled, axis=-1, keepdims=True)
            - unit * jnp.mean(scaled * unit, axis=-1, keepdims=True)
        )
        dz = jnp.where(own, dz, 0.0)
        dz_one[here, :] = dz
        small[0:1, :] += jnp.sum(dz, axis=0, keepdims=True)
        small[1:2, :] += jnp.sum(total * unit, axis=0, keepdims=True)
        small[2:3, :] += jnp.sum(total, axis=0, keepdims=True)
        low = dz.astype(BF16)
        upstream = dot_nt(low, w_out[...]).astype(BF16)
        d_mixed[here, :] = upstream
        mixture = mixed[here, :]
        mixture = jnp.where(own, mixture, jnp.zeros_like(mixture))
        grad_out[...] += dot_tn(mixture, low)
        product = upstream.astype(F32) * mixture.astype(F32)
        means = [jnp.sum(product[:, h * head : (h + 1) * head], axis=-1, keepdims=True) for h in range(2)]
        soft[here, :] = jnp.where(
            lane < 2, jnp.where(own, kept, -MASKED), jnp.where(lane == 2, means[0], means[1])
        )
        for copy in block_copies(onto, out_sems, index):
            copy.start()
        return carry

    lax.fori_loop(0, blocks, block, 0)

    def finish(index, carry):
        for copy in block_copies(onto, out_sems, index):
            copy.wait()
        return carry

    lax.fori_loop(0, blocks, finish, 0)


def attention_backward(part, *refs):
    (lengths, r0, r1, r2, r3, d_mixed_in, soft_in, dz_in, w_qkv), refs = refs[:9], refs[9:]
    extra = 4 * part
    inputs, refs = refs[:extra], refs[extra:]
    targets, refs = refs[:4], refs[4:]
    if part:
        (late_kept, late_sent), refs = refs[:2], refs[2:]
    else:
        grad_qkv, refs = refs[0], refs[1:]
    placed, qkv, d_proj, keys, values, frame_grads, d_mixed, soft, dz_one, place_sems, in_sems = refs[:11]
    quarter = r0.shape[1]
    length = 4 * quarter
    width = r0.shape[2]
    head = width // 2
    scale = head ** (-0.5)
    rows = Rows(lengths, length)
    tiles = rows.tiles_c if part else rows.tiles_a
    spare = placed.shape[0] - length
    places = [
        pltpu.make_async_copy(
            piece.at[part], placed.at[at((rows.member ^ distance) * quarter, quarter, quarter)], place_sems.at[distance]
        )
        for distance, piece in enumerate((r0, r1, r2, r3))
    ]
    for copy in places:
        copy.start()

    def copies(index):
        there = at(rows.base(part, index), BLOCK)
        here = at(index * BLOCK, BLOCK, BLOCK)
        pairs = ((d_mixed_in, d_mixed), (soft_in, soft), (dz_in, dz_one))
        return [
            pltpu.make_async_copy(source.at[there], target.at[here], in_sems.at[i, index])
            for i, (source, target) in enumerate(pairs)
        ]

    def start(index, carry):
        for copy in copies(index):
            copy.start()
        return carry

    lax.fori_loop(0, tiles, start, 0)
    placed[length:, :] = jnp.zeros((spare, width), BF16)
    d_proj[...] = jnp.zeros(d_proj.shape, BF16)
    keys[...] = jnp.zeros(keys.shape, F32)
    values[...] = jnp.zeros(values.shape, F32)
    frame_grads[...] = jnp.zeros(frame_grads.shape, F32)
    for copy in places:
        copy.wait()

    def project(index, carry):
        here = at(index * BLOCK, BLOCK, BLOCK)
        qkv[here, :] = dot(placed[here, :], w_qkv[...]).astype(BF16)
        return carry

    lax.fori_loop(0, length // BLOCK, project, 0)
    qkv[length:, :] = jnp.zeros((spare, 3 * width), BF16)

    def tile(index, carry):
        frames_at = rows.frames_at(part, index)
        here = at(index * BLOCK, BLOCK, BLOCK)
        for copy in copies(index):
            copy.wait()
        limit, column = softmax_parts(rows, part, length)
        inside = BLOCK * index + lax.broadcasted_iota(jnp.int32, (BLOCK, 1), 0)
        inside = inside < (rows.rows_c if part else rows.rows_a)
        frame_grads[frames_at, :] = jnp.where(inside, dz_one[here, :], 0.0)
        for h in range(2):
            low, high = h * head, (h + 1) * head
            query = qkv[frames_at, low:high]
            key = qkv[:length, width + low : width + high]
            value = qkv[:length, 2 * width + low : 2 * width + high]
            upstream = d_mixed[here, low:high]
            upstream = jnp.where(inside, upstream, jnp.zeros_like(upstream))
            shift = jnp.where(inside, soft[here, h : h + 1], -MASKED)
            mean = jnp.where(inside, soft[here, 2 + h : 3 + h], 0.0)
            scores = mask_keys(dot_nt(query, key), column, limit)
            weights = jnp.exp2(scores * (scale * LOG2E) - shift)
            d_weights = dot_nt(upstream, value)
            d_scores = (weights * (d_weights - mean)).astype(BF16)
            d_proj[frames_at, low:high] = (dot(d_scores, key) * scale).astype(BF16)
            keys[:, low:high] += dot_tn(d_scores, query)
            values[:, low:high] += dot_tn(weights.astype(BF16), upstream)
        return carry

    lax.fori_loop(0, tiles, tile, 0)
    d_proj[0:length, width : 2 * width] = (keys[...] * scale).astype(BF16)
    d_proj[0:length, 2 * width : 3 * width] = values[...].astype(BF16)
    for distance, target in enumerate(targets):
        here = at((rows.member ^ distance) * quarter, quarter, quarter)
        target[...] = (frame_grads[here, :] + dot_nt(d_proj[here, :], w_qkv[...])).astype(BF16)
    grads = dot_tn(placed[0:length, :], d_proj[0:length, :])
    if part == 0:
        grad_qkv[...] = grads
        return
    blocks = refs[11]
    grad_before, grad_out, small, conv_bias = inputs
    grads = (grads + grad_before[...]).astype(BF16)
    for q in range(3):
        blocks[q, :, :] = grads[:, q * width : (q + 1) * width]
    blocks[3, :, :] = grad_out[...].astype(BF16)
    line = lax.broadcasted_iota(jnp.int32, (8, 1), 0)
    for j in range(4):
        target = (late_kept, late_sent)[j % 2]
        target[j // 2, 0:width, :] = blocks[rows.member ^ j]
        bias = conv_bias[0:1, j * width : (j + 1) * width]
        tail = jnp.where(line == 6, bias, small[...])
        tail = jnp.concatenate([tail, jnp.zeros((SMALL_ROWS - 8, width), F32)], axis=0)
        target[j // 2, width : width + SMALL_ROWS, :] = tail.astype(BF16)


def collect(paired, lengths, *refs):
    pieces, result = refs[:-1], refs[-1]
    if paired:
        whole_parts = [piece[0] for piece in pieces]
        shared_parts = [piece[1] for piece in pieces]
    else:
        whole_parts = [piece[...] for piece in pieces[:4]]
        shared_parts = [piece[...] for piece in pieces[4:]]
    member = lax.axis_index("tensor")
    whole, shared = plan(lengths)
    for distance in range(4):
        slot = choose(member ^ distance, whole) % 8
        result[slot] = whole_parts[distance].astype(result.dtype)
    for side in range(2):
        second = (member >= 2) == (side == 0)
        slot = jnp.where(second, shared[1], shared[0]) % 8
        total = shared_parts[2 * side].astype(F32) + shared_parts[2 * side + 1].astype(F32)
        result[slot] = total.astype(result.dtype)


def finish_late(own, p1, p2, p3, *refs):
    grad_qkv, grad_out = refs[:2]
    vectors, blocks = refs[2:-1], refs[-1]
    width = grad_out.shape[0]
    member = lax.axis_index("tensor")
    for distance, piece in enumerate((own, p1, p2, p3)):
        blocks[member ^ distance] = piece[0:width, :].astype(F32)
    for q in range(3):
        grad_qkv[:, q * width : (q + 1) * width] = blocks[q]
    grad_out[...] = blocks[3]
    tail = own[width : width + 16, :].astype(F32)
    for i, vector in enumerate(vectors):
        vector[...] = tail[i : i + 1, :]


def finish_filters(steps, *refs):
    parts, (grad_conv, grad_proj, work) = refs[:-3], refs[-3:]
    where = lax.axis_index("dp")
    depth = grad_conv.shape[0]
    start = 0
    for step, value, other in zip(steps, parts[::2], parts[1::2]):
        half = value.shape[0]
        bit = (where // step) % 2
        work[at(start + bit * half, half), :] = value[...]
        work[at(start + (1 - bit) * half, half), :] = other[...]
        start += 2 * half
    grad_conv[...] = work[0:depth, :].astype(F32)
    grad_proj[...] = work[depth:, :].astype(F32)


def shards(
    frames,
    lengths,
    w_qkv,
    w_out,
    b_out,
    gain_one,
    shift_one,
    w_conv,
    b_conv,
    w_proj,
    b_proj,
    gain_two,
    shift_two,
    cotangent,
):
    count, quarter, width = frames.shape
    length = 4 * quarter
    taps = w_conv.shape[0]
    depth = taps * width
    filters = 4 * w_conv.shape[2]
    padded = length + BLOCK
    space = 2 * length
    limit = 7 * BLOCK
    smem = pl.BlockSpec(memory_space=pltpu.SMEM)
    vmem = pl.BlockSpec(memory_space=pltpu.VMEM)
    anywhere = pl.BlockSpec(memory_space=pl.ANY)
    shape = jax.ShapeDtypeStruct
    dp_size = lax.axis_size("dp")
    dp_place = lax.axis_index("dp")
    b_out, gain_one, shift_one, b_proj, gain_two, shift_two = [
        v[None] for v in (b_out, gain_one, shift_one, b_proj, gain_two, shift_two)
    ]

    def hop(value, distance):
        return lax.ppermute(value, "tensor", [(i, i ^ distance) for i in range(4)])

    def dp_hop(value, distance):
        return lax.ppermute(value, "dp", [(i, i ^ distance) for i in range(dp_size)])

    def after(value, *others):
        return lax.optimization_barrier((value,) + others)[0]

    def picked(array, name):
        return pl.pallas_call(
            pick,
            out_shape=[shape((2, quarter, width), BF16)] * 4,
            in_specs=[smem, vmem],
            out_specs=[vmem] * 4,
            compiler_params=params(),
            name=name,
        )(lengths, array)

    def spread_out(parts):
        return [parts[0]] + [hop(parts[d], d) for d in (1, 2, 3)]

    b_high = b_conv.astype(BF16)
    b_low = (b_conv - b_high.astype(F32)).astype(BF16)
    pack = jnp.concatenate(
        [
            w_conv.reshape(depth, width),
            w_proj,
            jnp.broadcast_to(b_high[None], (16, width)),
            jnp.broadcast_to(b_low[None], (48, width)),
        ]
    )
    piece = pack.shape[0] // 4
    far0 = hop(lax.dynamic_slice_in_dim(pack, (dp_place % 4) * piece, piece, 0), 2)
    near_pack = hop(pack, 1)
    frame_picks = picked(frames, "pick_frames")
    frame_parts = spread_out(frame_picks)
    cot_picks = picked(after(cotangent, *frame_picks), "pick_cotangent")
    far0, near_pack, *cot_picks = lax.optimization_barrier((far0, near_pack, *cot_picks))
    far1, far2, *frame_parts = lax.optimization_barrier((dp_hop(far0, 1), dp_hop(far0, 2), *frame_parts))
    last = [dp_hop(far2[: piece // 2], 1), dp_hop(far1[piece // 2 :], 2)]
    cot_parts = spread_out([after(part, *frame_parts) for part in cot_picks])

    rows = length + length // 2
    normed, stats, mixed = pl.pallas_call(
        tied(attention_forward, 8, 1),
        out_shape=(
            shape((space, width), F32),
            shape((space, 128), F32),
            shape((space, width), BF16),
        ),
        in_specs=[smem] + [vmem] * 7 + [anywhere] * 1,
        out_specs=[anywhere] * 3,
        scratch_shapes=[
            pltpu.VMEM((2, padded, width), BF16),
            pltpu.VMEM((2, padded, 2 * width), BF16),
            pltpu.VMEM((2, 2, length, width), BF16),
            pltpu.VMEM((2, length, width), F32),
            pltpu.VMEM((2, length, 128), F32),
            pltpu.VMEM((2, length, width), BF16),
            pltpu.SemaphoreType.DMA((2, 3, length // BLOCK)),
        ],
        compiler_params=params(),
        cost_estimate=cost(1e6, 1e5),
        name="attention_forward",
    )(lengths, *frame_parts, w_qkv, w_out, b_out, near_pack)

    last = [after(part, normed, *cot_parts) for part in last]
    far_pack = jnp.concatenate([far0, far1, far2] + last)
    far_near_pack = hop(far_pack, 1)
    packs = (pack, near_pack, far_pack, far_near_pack)

    chunk_rows = (depth + width) // 2
    block_count = limit // BLOCK
    result = pl.pallas_call(
        feed_forward,
        out_shape=[shape((2, quarter, width), BF16)] * 4
        + [shape((2, chunk_rows, width), BF16)] * 4
        + [
            shape((limit, filters), BF16),
            shape((limit, width), F32),
            shape((depth, filters), BF16),
            shape((8, width), F32),
            shape((8, filters), F32),
        ],
        in_specs=[smem, anywhere] + [vmem] * 4 + [anywhere] * 4 + [vmem] * 5,
        out_specs=[vmem] * 4 + [anywhere] * 7 + [vmem] * 2,
        scratch_shapes=[
            pltpu.VMEM((pack.shape[0], filters), BF16),
            pltpu.VMEM((limit, width), F32),
            pltpu.VMEM((limit + 2 * HALO, width), F32),
            pltpu.VMEM((limit, depth), BF16),
            pltpu.VMEM((2, BLOCK, filters), F32),
            pltpu.VMEM((BLOCK, filters), F32),
            pltpu.VMEM((limit, filters), BF16),
            pltpu.VMEM((limit, width), BF16),
            pltpu.VMEM((limit, filters), BF16),
            pltpu.VMEM((limit, width), F32),
            pltpu.VMEM((4, depth + width, width), BF16),
            pltpu.VMEM((2, padded, width), BF16),
            pltpu.VMEM((space, width), BF16),
            pltpu.VMEM((space, width), BF16),
            pltpu.VMEM((padded, width), BF16),
            pltpu.SemaphoreType.DMA((FILTER_COPIES,)),
            pltpu.SemaphoreType.DMA((block_count,)),
            pltpu.SemaphoreType.DMA((2, block_count)),
            pltpu.SemaphoreType.DMA((taps + 1, 4)),
            pltpu.SemaphoreType.DMA((1,)),
        ],
        compiler_params=params(),
        cost_estimate=cost(1e6, 1e5),
        name="feed_forward",
    )(lengths, normed, *cot_parts, *packs, gain_one, shift_one, b_proj, gain_two, shift_two)
    outputs, kept, sent = result[:4], result[4:6], result[6:8]
    d_hidden, dz_two, conv, small_two, conv_bias = result[8:]

    def add(a, b):
        return (a.astype(F32) + b.astype(F32)).astype(BF16)

    def halves(value, step):
        half = value.shape[-2] // 2
        bit = (dp_place // step) % 2
        axis = value.ndim - 2
        parts = value.reshape(value.shape[:-2] + (2, half, width))
        keep = lax.dynamic_index_in_dim(parts, bit, axis, keepdims=False)
        send = lax.dynamic_index_in_dim(parts, 1 - bit, axis, keepdims=False)
        return keep, dp_hop(send, step)

    def joined(value, other, step):
        bit = (dp_place // step) % 2
        return jnp.where(bit == 0, jnp.concatenate([value, other]), jnp.concatenate([other, value]))

    def begin(value, step):
        return (value[0], hop(value[1], 2)) if step == 0 else halves(value, step)

    def collected(parts, dtype, name):
        return pl.pallas_call(
            functools.partial(collect, len(parts) == 4),
            out_shape=shape((count, quarter, width), dtype),
            in_specs=[smem] + [vmem] * len(parts),
            out_specs=vmem,
            compiler_params=params(),
            name=name,
        )(lengths, *parts)

    more = [2**i for i in range(2, 20) if 2**i < dp_size]
    orders = [[1, 0, 2], [0, 2, 1]]
    moving = [(kept[c], hop(sent[c], 1)) for c in range(2)]
    out_parts = spread_out(outputs)

    dz_one, d_mixed, soft, grad_out, small = pl.pallas_call(
        conv_backward,
        out_shape=(
            shape((space, width), F32),
            shape((space, width), BF16),
            shape((space, 128), F32),
            shape((width, width), F32),
            shape((8, width), F32),
        ),
        in_specs=[smem] + [anywhere] * 6 + [vmem] * 3,
        out_specs=[anywhere] * 3 + [vmem] * 2,
        scratch_shapes=[
            pltpu.VMEM((depth, filters), BF16),
            pltpu.VMEM((limit, filters), BF16),
            pltpu.VMEM((limit, width), F32),
            pltpu.VMEM((limit, width), F32),
            pltpu.VMEM((limit, 128), F32),
            pltpu.VMEM((limit, width), BF16),
            pltpu.VMEM((limit, width), F32),
            pltpu.VMEM((limit, width), BF16),
            pltpu.VMEM((limit, 128), F32),
            pltpu.VMEM((limit + 2 * HALO, depth), F32),
            pltpu.SemaphoreType.DMA((taps,)),
            pltpu.SemaphoreType.DMA((5, block_count)),
            pltpu.SemaphoreType.DMA((3, block_count)),
        ],
        compiler_params=params(),
        cost_estimate=cost(1e6, 1e5),
        name="conv_backward",
    )(lengths, d_hidden, conv, dz_two, normed, stats, mixed, w_out, gain_one, small_two)

    def attention_back(part, inputs, ties):
        late_rows = width + SMALL_ROWS
        more_outs = [shape((2, late_rows, width), BF16)] * 2 if part else [shape((width, 3 * width), F32)]
        return pl.pallas_call(
            tied(functools.partial(attention_backward, part), 9 + len(inputs), len(ties)),
            out_shape=[shape((quarter, width), BF16)] * 4 + more_outs,
            in_specs=[smem] + [anywhere] * 7 + [vmem] * (1 + len(inputs)) + [anywhere] * len(ties),
            out_specs=[vmem] * (4 + len(more_outs)),
            scratch_shapes=[
                pltpu.VMEM((padded, width), BF16),
                pltpu.VMEM((padded, 3 * width), BF16),
                pltpu.VMEM((padded, 3 * width), BF16),
                pltpu.VMEM((length, width), F32),
                pltpu.VMEM((length, width), F32),
                pltpu.VMEM((padded, width), F32),
                pltpu.VMEM((length, width), BF16),
                pltpu.VMEM((length, 128), F32),
                pltpu.VMEM((length, width), F32),
                pltpu.SemaphoreType.DMA((4,)),
                pltpu.SemaphoreType.DMA((3, length // BLOCK)),
            ]
            + [pltpu.VMEM((4, width, width), BF16)] * part,
            compiler_params=params(),
            cost_estimate=cost(1e6, 1e5),
            name=f"attention_backward_{'ac'[part]}",
        )(lengths, *frame_parts, d_mixed, soft, dz_one, w_qkv, *inputs, *ties)

    moving = [(keep, after(other, dz_one)) for keep, other in moving]
    state = [add(*pair) for pair in moving]
    moving = [begin(value, order[0]) for value, order in zip(state, orders)]
    output = collected(out_parts, BF16, "collect_output")
    *grads_a, grad_qkv = attention_back(0, [], state + [output])
    moving = [(keep, after(other, grad_qkv)) for keep, other in moving]
    state = [add(*pair) for pair in moving]
    moving = [begin(value, order[1]) for value, order in zip(state, orders)]
    a_far = [hop(grads_a[d], d) for d in (2, 3)]
    *grads_c, late_kept, late_sent = attention_back(1, [grad_qkv, grad_out, small, conv_bias], state)
    moving = [(keep, after(other, late_kept, *a_far)) for keep, other in moving]
    state = [add(*pair) for pair in moving]
    near_grads = hop(after(jnp.stack([grads_a[1], grads_c[1]]), *state), 1)
    c_far = [hop(after(grads_c[d], *state), d) for d in (2, 3)]
    d_frames = collected(
        [grads_a[0], near_grads[0]] + a_far + [grads_c[0], near_grads[1]] + c_far, F32, "collect_grad"
    )

    moving = [begin(value, order[2]) for value, order in zip(state, orders)]
    late = add(late_kept, hop(after(late_sent, *state), 1))
    late_far = hop(late[1], 2)
    state = [add(keep, after(other, late)) for keep, other in moving]
    others = [dp_hop(value, 4) for value in state] if dp_size > 4 else []
    late = add(late[0], late_far)
    late_parts = [dp_hop(late, step) for step in (1, 2, 3)]
    if others:
        others = list(lax.optimization_barrier((*others, *late_parts, d_frames)))[:-1]
        others, late_parts = others[: len(state)], others[len(state) :]
        state = [add(value, other) for value, other in zip(state, others)]
    late = sum((part.astype(F32) for part in late_parts), late.astype(F32)).astype(BF16)
    for step in more[1:]:
        state = [add(value, dp_hop(value, step)) for value in state]
    backs = [[step for step in reversed(order) if step] for order in orders]
    others = [dp_hop(value, back[0]) for value, back in zip(state, backs)]
    for step in more:
        late = add(late, dp_hop(late, step))
    state = [joined(value, after(other, late), back[0]) for value, other, back in zip(state, others, backs)]
    last = [back[-1] for back in backs]
    others = [dp_hop(value, step) for value, step in zip(state, last)]
    grad_conv, grad_proj = pl.pallas_call(
        functools.partial(finish_filters, last),
        out_shape=(shape((depth, width), F32), shape((width, width), F32)),
        in_specs=[vmem] * 4,
        out_specs=[vmem] * 2,
        scratch_shapes=[pltpu.VMEM((depth + width, width), BF16)],
        compiler_params=params(),
        name="finish_filters",
    )(*[part for pair in zip(state, others) for part in pair])
    body = late[:width]
    grad_qkv, grad_out, *vectors = pl.pallas_call(
        finish_late,
        out_shape=[shape((width, 3 * width), F32), shape((width, width), F32)] + [shape((1, width), F32)] * 7,
        in_specs=[vmem] * 4,
        out_specs=[vmem] * 9,
        scratch_shapes=[pltpu.VMEM((4, width, width), F32)],
        compiler_params=params(),
        name="finish_late",
    )(late, *[hop(body, d) for d in (1, 2, 3)])
    vectors = [v.reshape(width) for v in vectors]
    return (
        output,
        d_frames,
        grad_qkv,
        grad_out,
        vectors[0],
        vectors[1],
        vectors[2],
        grad_conv.reshape(w_conv.shape),
        vectors[6],
        grad_proj,
        vectors[3],
        vectors[4],
        vectors[5],
    )


def solution(mesh):
    return jax.shard_map(
        shards,
        mesh=mesh,
        in_specs=(
            P("dp", "tensor", None),
            P("dp"),
            P(),
            P(),
            P(),
            P(),
            P(),
            P(None, None, "tensor"),
            P("tensor"),
            P("tensor", None),
            P(),
            P(),
            P(),
            P("dp", "tensor", None),
        ),
        out_specs=(
            P("dp", "tensor", None),
            P("dp", "tensor", None),
            P(),
            P(),
            P(),
            P(),
            P(),
            P(None, None, "tensor"),
            P("tensor"),
            P("tensor", None),
            P(),
            P(),
            P(),
        ),
        check_vma=False,
    )
```

```python
import functools
import itertools

import jax
import jax.experimental.pallas as pl
import jax.experimental.pallas.tpu as pltpu
import jax.numpy as jnp
import numpy as np
from jax import lax
from jax.sharding import PartitionSpec as P


EPSILON = 1e-05
F32 = jnp.float32
BF16 = jnp.bfloat16
HALO = 16
BLOCK = 256
MASKED = -1e30
GELU_A = float(np.sqrt(2.0 / np.pi))
GELU_B = 0.044715
LOG2E = float(np.log2(np.e))
VMEM_LIMIT = 58 * 2**20
SMALL_ROWS = 16


def near(*arrays):
    return [pltpu.with_memory_space_constraint(array, pltpu.VMEM) for array in arrays]


def params(**more):
    return pltpu.CompilerParams(vmem_limit_bytes=VMEM_LIMIT, **more)


def cost(flops, size):
    return pl.CostEstimate(flops=int(flops), bytes_accessed=int(size), transcendentals=0)


def dot(a, b):
    return jnp.dot(a, b, preferred_element_type=F32)


def dot_nt(a, b):
    return lax.dot_general(a, b, (((1,), (1,)), ((), ())), preferred_element_type=F32)


def dot_tn(a, b):
    return lax.dot_general(a, b, (((0,), (0,)), ((), ())), preferred_element_type=F32)


def at(start, size, step=HALO):
    return pl.ds(pl.multiple_of(start, step), size)


def up(value, step=HALO):
    return ((value + (step - 1)) // step) * step


def choose(index, options):
    result = options[-1]
    for i, option in enumerate(options[:-1]):
        result = jnp.where(index == i, option, result)
    return result


def plan(lengths):
    keys = [lengths[i] * 8 + i for i in range(6)]
    best, triples = None, None
    for pair in itertools.combinations(range(1, 6), 2):
        mine = (0,) + pair
        rest = tuple(i for i in range(6) if i not in mine)
        gap = jnp.abs(sum(lengths[i] for i in mine) - sum(lengths[i] for i in rest))
        option = [keys[i] for i in mine + rest]
        if best is None:
            best, triples = gap, option
        else:
            better = gap < best
            best = jnp.where(better, gap, best)
            triples = [jnp.where(better, new, old) for new, old in zip(option, triples)]
    whole, shared = [], []
    for a, b, c in (triples[:3], triples[3:]):
        a, b = jnp.maximum(a, b), jnp.minimum(a, b)
        a, c = jnp.maximum(a, c), jnp.minimum(a, c)
        b, c = jnp.maximum(b, c), jnp.minimum(b, c)
        whole += [a, b]
        shared.append(c)
    return whole, shared


class Rows:
    def __init__(self, lengths, length):
        self.member = lax.axis_index("tensor")
        whole, shared = plan(lengths)
        self.whole, self.shared = whole, shared
        role = self.member % 2
        second = self.member >= 2
        key_a = choose(self.member, whole)
        self.len_a = key_a // 8
        self.len_c = jnp.where(second, shared[1], shared[0]) // 8
        first_len = jnp.where(second, whole[2], whole[0]) // 8
        other_len = jnp.where(second, whole[3], whole[1]) // 8
        split = (other_len + self.len_c - first_len) // 2
        split = jnp.maximum((split + HALO // 2) // HALO * HALO, HALO)
        starts = role == 0
        self.own_from = jnp.where(starts, 0, split)
        self.own_to = jnp.where(starts, split, length)
        self.window = jnp.where(starts, 0, split - HALO)
        self.end = jnp.where(starts, jnp.minimum(split + HALO, self.len_c), self.len_c)
        self.rows_a = up(self.len_a) + HALO
        self.rows_c = jnp.maximum(up(self.end) - self.window, 0)
        self.tiles_a = (self.len_a + BLOCK - 1) // BLOCK
        self.tiles_c = (self.rows_c + BLOCK - 1) // BLOCK
        self.blocks = (self.rows_a + self.rows_c + BLOCK - 1) // BLOCK
        self.halo = self.rows_a + jnp.where(starts, split, 0)

    def masks(self, start, size):
        row = start + lax.broadcasted_iota(jnp.int32, (size, 1), 0)
        in_a = row < self.rows_a
        frame = jnp.where(in_a, row, row - self.rows_a + self.window)
        live = frame < jnp.where(in_a, self.len_a, self.end)
        inside = (frame >= self.own_from) & (frame < self.own_to)
        return live, live & (in_a | inside)

    def frames_at(self, part, index):
        return at(BLOCK * index + (self.window if part else 0), BLOCK)

    def base(self, part, index):
        return BLOCK * index + (self.rows_a if part else 0)


def piece_index(piece, part):
    return part if piece.shape[0] == 2 else 2 - part


def place(member, pieces, target):
    quarter = pieces[0].shape[1]
    for distance, piece in enumerate(pieces):
        rows = at((member ^ distance) * quarter, quarter, quarter)
        for part in range(2):
            target[part, rows, :] = piece[piece_index(piece, part)]


def pick(lengths, source, *targets):
    member = lax.axis_index("tensor")
    whole, shared = plan(lengths)
    for distance, target in enumerate(targets):
        there = member ^ distance
        if target.shape[0] == 3:
            target[0] = source[choose(there ^ 1, whole) % 8]
        target[piece_index(target, 0)] = source[choose(there, whole) % 8]
        target[piece_index(target, 1)] = source[jnp.where(there >= 2, shared[1], shared[0]) % 8]


def begin_group(lengths, source, w_conv, w_proj, b_conv, pack, p0, p1, p2, part):
    depth, width = w_conv.shape
    pack[0:depth, :] = w_conv[...]
    pack[depth : depth + width, :] = w_proj[...]
    high = b_conv[...].astype(BF16)
    rest = (b_conv[...] - high.astype(F32)).astype(BF16)
    last = depth + width
    pack[last : last + HALO, :] = jnp.broadcast_to(high, (HALO, width))
    pack[last + HALO :, :] = jnp.broadcast_to(rest, (pack.shape[0] - last - HALO, width))
    piece = part.shape[0]
    part[...] = pack[at((lax.axis_index("dp") % 4) * piece, piece), :]
    pick(lengths, source, p0, p1, p2)


def softmax_parts(rows, part, length):
    return (rows.len_c if part else rows.len_a), lax.broadcasted_iota(jnp.int32, (1, length), 1)


def mask_keys(scores, column, limit):
    half = scores.shape[1] // 2
    tail = jnp.where(column[:, half:] < limit, scores[:, half:], MASKED)
    return jnp.concatenate([scores[:, :half], tail], axis=1)


def attention_forward(
    lengths, r0, r1, r2, r3, w_qkv, w_out, b_out, normed, stats, mixed, placed, qkv, valued, n_out, s_out, m_out, sems
):
    quarter = r0.shape[1]
    length = 4 * quarter
    width = r0.shape[2]
    head = width // 2
    scale = head ** (-0.5) * LOG2E
    rows = Rows(lengths, length)
    spare = placed.shape[1] - length
    placed[:, length:, :] = jnp.zeros((2, spare, width), BF16)
    place(rows.member, (r0, r1, r2, r3), placed)
    for part in range(2):
        for h in range(2):
            valued[part, h, :, head:] = jnp.ones((length, head), BF16)

    def project(index, carry):
        here = at(index * BLOCK, BLOCK, BLOCK)
        for part in range(2):
            value = dot(placed[part, here, :], w_qkv[...]).astype(BF16)
            qkv[part, here, :] = value[:, : 2 * width]
            for h in range(2):
                valued[part, h, here, :head] = value[:, 2 * width + h * head : 2 * width + (h + 1) * head]
        return carry

    lax.fori_loop(0, length // BLOCK, project, 0)
    qkv[:, length:, :] = jnp.zeros((2, spare, 2 * width), BF16)
    lane = lax.broadcasted_iota(jnp.int32, (1, 128), 1)

    def copies(part, index):
        there = at(rows.base(part, index), BLOCK)
        here = at(index * BLOCK, BLOCK, BLOCK)
        pairs = ((n_out, normed), (s_out, stats), (m_out, mixed))
        return [
            pltpu.make_async_copy(source.at[part, here], target.at[there], sems.at[part, i, index])
            for i, (source, target) in enumerate(pairs)
        ]

    def tile(part, index, carry):
        frames_at = rows.frames_at(part, index)
        here = at(index * BLOCK, BLOCK, BLOCK)
        limit, column = softmax_parts(rows, part, length)
        mixtures, logs = [], []
        for h in range(2):
            low, high = h * head, (h + 1) * head
            scores = dot_nt(qkv[part, frames_at, low:high], qkv[part, :length, width + low : width + high])
            scores = mask_keys(scores, column, limit)
            highest = jnp.max(scores, axis=-1, keepdims=True) * scale
            exponent = jnp.exp2(scores * scale - highest).astype(BF16)
            summed = dot(exponent, valued[part, h])
            total = summed[:, head : head + 1]
            mixtures.append((summed[:, :head] / total).astype(BF16))
            logs.append(highest + jnp.log2(total))
        mixture = jnp.concatenate(mixtures, axis=1)
        m_out[part, here, :] = mixture
        residual = placed[part, frames_at, :].astype(F32) + dot(mixture, w_out[...]) + b_out[...]
        centred = residual - jnp.mean(residual, axis=-1, keepdims=True)
        inverse = lax.rsqrt(jnp.mean(centred * centred, axis=-1, keepdims=True) + EPSILON)
        n_out[part, here, :] = centred * inverse
        s_out[part, here, :] = jnp.where(lane == 0, logs[0], jnp.where(lane == 1, logs[1], inverse))
        for copy in copies(part, index):
            copy.start()
        return carry

    def finish(part, index, carry):
        for copy in copies(part, index):
            copy.wait()
        return carry

    for part, count in enumerate((rows.tiles_a, rows.tiles_c)):
        lax.fori_loop(0, count, functools.partial(tile, part), 0)
        lax.fori_loop(0, count, functools.partial(finish, part), 0)


def gelu_pair(x):
    square = x * x
    t = jnp.tanh(GELU_A * x * (1.0 + GELU_B * square))
    half = 0.5 * (1.0 + t)
    slope = half + (0.5 * GELU_A) * x * (1.0 - t * t) * (1.0 + 3.0 * GELU_B * square)
    return x * half, slope


def load_filters(near, far, target, sems):
    width = near[0].shape[1]
    piece = near[0].shape[0] // 4
    shift = lax.axis_index("dp") % 4
    copies = []
    for j, source in enumerate(near):
        copies.append((source, target.at[:, pl.ds(j * width, width)]))
    for j, source in enumerate(far):
        for i in range(4):
            there = at((shift ^ i) * piece, piece)
            part = pl.ds((2 + j) * width, width)
            copies.append((source.at[pl.ds(i * piece, piece)], target.at[there, part]))
    copies = [
        pltpu.make_async_copy(source, there, sems.at[i]) for i, (source, there) in enumerate(copies)
    ]
    for copy in copies:
        copy.start()
    return copies


FILTER_COPIES = 10


def feed_forward(
    lengths,
    normed,
    c0,
    c1,
    c2,
    c3,
    pack0,
    pack1,
    far0,
    far1,
    gain_one,
    shift_one,
    b_proj,
    gain_two,
    shift_two,
    o0,
    o1,
    o2,
    o3,
    kept0,
    kept1,
    sent0,
    sent1,
    d_hidden_out,
    dz_out,
    conv_out,
    small,
    conv_bias,
    weights,
    units,
    first,
    columns,
    hidden,
    slope,
    active,
    d_branch,
    d_hidden,
    dz_two,
    grads,
    cot_frames,
    cot_rows,
    out_rows,
    out_c,
    load_sems,
    unit_sems,
    out_sems,
    grad_sems,
    conv_sem,
):
    quarter, width = c0.shape[1:]
    length = 4 * quarter
    filters = weights.shape[1]
    taps = columns.shape[1] // width
    depth = taps * width
    reach = taps // 2
    loads = load_filters((pack0, pack1), (far0, far1), weights, load_sems)
    rows = Rows(lengths, length)
    blocks = rows.blocks

    def unit_copy(index):
        here = at(index * BLOCK, BLOCK, BLOCK)
        return pltpu.make_async_copy(normed.at[here], units.at[here], unit_sems.at[index])

    def start_unit(index, carry):
        unit_copy(index).start()
        return carry

    lax.fori_loop(0, blocks, start_unit, 0)
    place(rows.member, (c0, c1, c2, c3), cot_frames)
    cot_frames[:, length:, :] = jnp.zeros((2, cot_frames.shape[1] - length, width), BF16)
    cot_rows[0:length, :] = cot_frames[0, 0:length, :]

    def gather_cot(index, carry):
        cot_rows[at(rows.base(1, index), BLOCK), :] = cot_frames[1, rows.frames_at(1, index), :]
        return carry

    lax.fori_loop(0, rows.tiles_c, gather_cot, 0)
    out_rows[...] = jnp.zeros(out_rows.shape, BF16)
    small[...] = jnp.zeros(small.shape, F32)
    conv_bias[...] = jnp.zeros(conv_bias.shape, F32)

    first[0:HALO, :] = jnp.zeros((HALO, width), F32)

    def make_first(index, carry):
        base = index * BLOCK
        unit_copy(index).wait()
        live, _ = rows.masks(base, BLOCK)
        value = units[at(base, BLOCK), :] * gain_one[...] + shift_one[...]
        first[at(base + HALO, BLOCK), :] = jnp.where(live, value, 0.0)
        return carry

    lax.fori_loop(0, blocks, make_first, 0)
    first[at(blocks * BLOCK + HALO, HALO), :] = jnp.zeros((HALO, width), F32)

    def make_columns(index, carry):
        base = index * BLOCK
        around = first[at(base + HALO - 8, BLOCK + 16, 8), :]
        for k in range(taps):
            columns[at(base, BLOCK, BLOCK), k * width : (k + 1) * width] = around[
                8 - reach + k : 8 - reach + k + BLOCK
            ].astype(BF16)
        return carry

    lax.fori_loop(0, blocks, make_columns, 0)
    for copy in loads:
        copy.wait()
    conv_copy = pltpu.make_async_copy(weights.at[pl.ds(0, depth)], conv_out, conv_sem.at[0])
    conv_copy.start()

    def out_copies(index):
        here = at(index * BLOCK, BLOCK, BLOCK)
        return [
            pltpu.make_async_copy(d_hidden.at[here], d_hidden_out.at[here], out_sems.at[0, index]),
            pltpu.make_async_copy(dz_two.at[here], dz_out.at[here], out_sems.at[1, index]),
        ]

    def conv(index, target):
        target[...] = dot(columns[at(index * BLOCK, BLOCK, BLOCK), :], weights[0:depth, :])

    def rest(index, source):
        base = index * BLOCK
        here = at(base, BLOCK, BLOCK)
        live, own = rows.masks(base, BLOCK)
        branch = jnp.zeros((BLOCK, width), F32)
        for j in range(filters // width):
            part = slice(j * width, (j + 1) * width)
            bias = weights[depth + width : depth + width + 1, part].astype(F32) + weights[
                depth + width + 16 : depth + width + 17, part
            ].astype(F32)
            value, derivative = gelu_pair(source[:, part] + bias)
            value = value.astype(BF16)
            active[here, part] = value
            slope[:, part] = derivative
            branch = branch + dot(value, weights[depth : depth + width, part])
        residual = first[at(base + HALO, BLOCK), :] + branch + b_proj[...]
        centred = residual - jnp.mean(residual, axis=-1, keepdims=True)
        inverse = lax.rsqrt(jnp.mean(centred * centred, axis=-1, keepdims=True) + EPSILON)
        normed_two = centred * inverse
        out_rows[here, :] = jnp.where(own, normed_two * gain_two[...] + shift_two[...], 0.0).astype(BF16)
        upstream = jnp.where(live, cot_rows[here, :].astype(F32), 0.0)
        counted = jnp.where(own, upstream, 0.0)
        scaled = upstream * gain_two[...]
        dz = inverse * (
            scaled
            - jnp.mean(scaled, axis=-1, keepdims=True)
            - normed_two * jnp.mean(scaled * normed_two, axis=-1, keepdims=True)
        )
        dz_two[here, :] = dz
        small[3:4, :] += jnp.sum(jnp.where(own, dz, 0.0), axis=0, keepdims=True)
        small[4:5, :] += jnp.sum(counted * normed_two, axis=0, keepdims=True)
        small[5:6, :] += jnp.sum(counted, axis=0, keepdims=True)
        low = dz.astype(BF16)
        d_branch[here, :] = jnp.where(own, low, jnp.zeros_like(low))
        for j in range(filters // width):
            part = slice(j * width, (j + 1) * width)
            grad = dot_nt(low, weights[depth : depth + width, part]) * slope[:, part]
            conv_bias[0:1, part] += jnp.sum(jnp.where(own, grad, 0.0), axis=0, keepdims=True)
            d_hidden[here, part] = grad.astype(BF16)
        for copy in out_copies(index):
            copy.start()

    even, odd = hidden.at[0], hidden.at[1]
    conv(0, even)

    def step(pair, carry):
        index = 2 * pair
        conv(index + 1, odd)
        rest(index, even)
        conv(index + 2, even)
        rest(index + 1, odd)
        return carry

    lax.fori_loop(0, (blocks - 1) // 2, step, 0)

    @pl.when(blocks % 2 == 1)
    def _():
        rest(blocks - 1, even)

    @pl.when(blocks % 2 == 0)
    def _():
        conv(blocks - 1, odd)
        rest(blocks - 2, even)
        rest(blocks - 1, odd)

    columns[at(rows.halo, HALO), :] = jnp.zeros((HALO, columns.shape[1]), BF16)

    kept, sent = (kept0, kept1), (sent0, sent1)
    per_chunk = (taps + 1) // 2

    def grad_copies(k, chunk):
        here = at(k * width, width, width)
        there = at((k - chunk * per_chunk) * width, width, width)
        return [
            pltpu.make_async_copy(
                grads.at[j, here], (kept, sent)[j % 2][chunk].at[j // 2, there], grad_sems.at[k, j]
            )
            for j in range(filters // width)
        ]

    for count in range(4, active.shape[0] // BLOCK + 1):

        @pl.when(blocks == count)
        def _():
            n = count * BLOCK

            def tap(k, carry):
                here = at(k * width, width, width)
                value = dot_tn(columns[0:n, here], d_hidden[0:n, :]).astype(BF16)
                for j in range(filters // width):
                    grads[j, here, :] = value[:, j * width : (j + 1) * width]
                for chunk in range(2):

                    @pl.when(k // per_chunk == chunk)
                    def _():
                        for copy in grad_copies(k, chunk):
                            copy.start()

                return carry

            lax.fori_loop(0, taps, tap, 0)
            value = dot_tn(active[0:n, :], d_branch[0:n, :]).astype(BF16)
            for j in range(filters // width):
                grads[j, depth:, :] = value[j * width : (j + 1) * width, :]
            for copy in grad_copies(taps, 1):
                copy.start()

    out_c[...] = jnp.zeros(out_c.shape, BF16)

    def scatter_out(index, carry):
        out_c[rows.frames_at(1, index), :] = out_rows[at(rows.base(1, index), BLOCK), :]
        return carry

    lax.fori_loop(0, rows.tiles_c, scatter_out, 0)
    for distance, target in enumerate((o0, o1, o2, o3)):
        start = (rows.member ^ distance) * quarter
        there = at(start, quarter, quarter)
        row = start + lax.broadcasted_iota(jnp.int32, (quarter, 1), 0)
        value = out_rows[there, :]
        target[0, :, :] = jnp.where(row < rows.len_a, value, jnp.zeros_like(value))
        target[1, :, :] = out_c[there, :]

    conv_copy.wait()

    def finish(index, carry):
        for copy in out_copies(index):
            copy.wait()
        return carry

    lax.fori_loop(0, blocks, finish, 0)

    def finish_grads(chunk, k, carry):
        for copy in grad_copies(k, chunk):
            copy.wait()
        return carry

    lax.fori_loop(0, per_chunk, functools.partial(finish_grads, 0), 0)
    lax.fori_loop(per_chunk, 2 * per_chunk, functools.partial(finish_grads, 1), 0)


def block_copies(pairs, sems, index):
    here = at(index * BLOCK, BLOCK, BLOCK)
    return [
        pltpu.make_async_copy(source.at[here], target.at[here], sems.at[i, index])
        for i, (source, target) in enumerate(pairs)
    ]


def conv_backward(
    lengths, d_hidden_in, conv, dz_in, d_first_out, weights, d_hidden, dz_two, d_first, sums, conv_sems, in_sems, out_sems
):
    width = dz_two.shape[1]
    taps = conv.shape[0] // width
    reach = taps // 2
    blocks = Rows(lengths, 4 * width).blocks
    conv_copies = [
        pltpu.make_async_copy(
            conv.at[pl.ds(k * width, width)], weights.at[pl.ds(k * width, width)], conv_sems.at[k]
        )
        for k in range(taps)
    ]
    into = ((d_hidden_in, d_hidden), (dz_in, dz_two))
    onto = ((d_first, d_first_out),)
    for copy in conv_copies:
        copy.start()

    def start(index, carry):
        for copy in block_copies(into, in_sems, index):
            copy.start()
        return carry

    lax.fori_loop(0, blocks, start, 0)
    sums[0:HALO, :] = jnp.zeros((HALO, width), F32)
    for copy in conv_copies:
        copy.wait()

    def back(index, carry):
        base = index * BLOCK
        for copy in block_copies(into, in_sems, index):
            copy.wait()
        value = d_hidden[at(base, BLOCK, BLOCK), :]
        total = jnp.zeros((BLOCK + HALO, width), F32)
        for k in range(taps):
            part = dot_nt(value, weights[k * width : (k + 1) * width, :])
            part = jnp.concatenate([part, jnp.zeros((HALO, width), F32)], axis=0)
            total = total + pltpu.roll(part, 8 - reach + k, axis=0)
        sums[at(base, HALO), :] += total[0:HALO]
        sums[at(base + HALO, BLOCK), :] = total[HALO:]
        return carry

    lax.fori_loop(0, blocks, back, 0)

    def finish(index, carry):
        base = index * BLOCK
        here = at(base, BLOCK, BLOCK)
        d_first[here, :] = dz_two[here, :] + sums[at(base + 8, BLOCK, 8), :]
        block_copies(onto, out_sems, index)[0].start()
        return carry

    lax.fori_loop(0, blocks, finish, 0)

    def drain(index, carry):
        block_copies(onto, out_sems, index)[0].wait()
        return carry

    lax.fori_loop(0, blocks, drain, 0)


def first_norm_backward(rows, ins, outs, blocks_in, blocks_out, in_sems, out_sems, w_out, gain_one, small, grad_out):
    d_first, normed, stats, mixed = blocks_in
    dz_one, d_mixed, soft = blocks_out
    into, onto = tuple(zip(ins, blocks_in)), tuple(zip(blocks_out, outs))
    width = normed.shape[1]
    head = width // 2
    lane = lax.broadcasted_iota(jnp.int32, (1, 128), 1)

    def block(index, carry):
        base = index * BLOCK
        here = at(base, BLOCK, BLOCK)
        for copy in block_copies(into, in_sems, index):
            copy.wait()
        _, own = rows.masks(base, BLOCK)
        total = jnp.where(own, d_first[here, :], 0.0)
        unit = jnp.where(own, normed[here, :], 0.0)
        kept = stats[here, :]
        inverse = kept[:, 2:3]
        scaled = total * gain_one[...]
        dz = inverse * (
            scaled
            - jnp.mean(scaled, axis=-1, keepdims=True)
            - unit * jnp.mean(scaled * unit, axis=-1, keepdims=True)
        )
        dz = jnp.where(own, dz, 0.0)
        dz_one[here, :] = dz
        small[0:1, :] += jnp.sum(dz, axis=0, keepdims=True)
        small[1:2, :] += jnp.sum(total * unit, axis=0, keepdims=True)
        small[2:3, :] += jnp.sum(total, axis=0, keepdims=True)
        low = dz.astype(BF16)
        upstream = dot_nt(low, w_out[...]).astype(BF16)
        d_mixed[here, :] = upstream
        mixture = mixed[here, :]
        mixture = jnp.where(own, mixture, jnp.zeros_like(mixture))
        grad_out[...] += dot_tn(mixture, low)
        product = upstream.astype(F32) * mixture.astype(F32)
        means = [jnp.sum(product[:, h * head : (h + 1) * head], axis=-1, keepdims=True) for h in range(2)]
        soft[here, :] = jnp.where(
            lane < 2, jnp.where(own, kept, -MASKED), jnp.where(lane == 2, means[0], means[1])
        )
        for copy in block_copies(onto, out_sems, index):
            copy.start()
        return carry

    lax.fori_loop(0, rows.blocks, block, 0)

    def finish(index, carry):
        for copy in block_copies(onto, out_sems, index):
            copy.wait()
        return carry

    return finish


def attention_backward(part, *refs):
    (lengths, r0, r1, r2, r3, w_qkv), refs = refs[:6], refs[6:]
    if part:
        in_refs, refs = refs[:3], refs[3:]
        inputs, refs = refs[:4], refs[4:]
        targets, refs = refs[:4], refs[4:]
        late, refs = refs[:4], refs[4:]
    else:
        in_refs, refs = refs[:4], refs[4:]
        (w_out, gain_one, small_two), refs = refs[:3], refs[3:]
        targets, refs = refs[:4], refs[4:]
        grad_qkv, refs = refs[0], refs[1:]
        out_refs, refs = refs[:3], refs[3:]
        (grad_out, small), refs = refs[:2], refs[2:]
    placed, qkv, d_proj, keys, values, frame_grads, dz_one, d_mixed, soft, place_sems, in_sems = refs[:11]
    quarter = r0.shape[1]
    length = 4 * quarter
    width = r0.shape[2]
    head = width // 2
    scale = head ** (-0.5)
    rows = Rows(lengths, length)
    tiles = rows.tiles_c if part else rows.tiles_a
    spare = placed.shape[0] - length
    places = [
        pltpu.make_async_copy(
            piece.at[piece_index(piece, part)],
            placed.at[at((rows.member ^ distance) * quarter, quarter, quarter)],
            place_sems.at[distance],
        )
        for distance, piece in enumerate((r0, r1, r2, r3))
    ]

    def copies(index):
        there = at(rows.base(part, index), BLOCK)
        here = at(index * BLOCK, BLOCK, BLOCK)
        return [
            pltpu.make_async_copy(source.at[there], target.at[here], in_sems.at[i, index])
            for i, (source, target) in enumerate(zip(in_refs, (dz_one, d_mixed, soft)))
        ]

    if part:

        def start(index, carry):
            for copy in copies(index):
                copy.start()
            return carry

        lax.fori_loop(0, tiles, start, 0)
    else:
        blocks_in, out_sems = refs[11:15], refs[15]

        def start(index, carry):
            for copy in block_copies(tuple(zip(in_refs, blocks_in)), in_sems, index):
                copy.start()
            return carry

        lax.fori_loop(0, rows.blocks, start, 0)
    for copy in places:
        copy.start()
    placed[length:, :] = jnp.zeros((spare, width), BF16)
    d_proj[...] = jnp.zeros(d_proj.shape, BF16)
    keys[...] = jnp.zeros(keys.shape, F32)
    values[...] = jnp.zeros(values.shape, F32)
    frame_grads[...] = jnp.zeros(frame_grads.shape, F32)
    if not part:
        small[...] = small_two[...]
        grad_out[...] = jnp.zeros(grad_out.shape, F32)
        finish = first_norm_backward(
            rows, in_refs, out_refs, blocks_in, (dz_one, d_mixed, soft), in_sems, out_sems, w_out, gain_one, small, grad_out
        )
    for copy in places:
        copy.wait()

    def project(index, carry):
        here = at(index * BLOCK, BLOCK, BLOCK)
        qkv[here, :] = dot(placed[here, :], w_qkv[...]).astype(BF16)
        return carry

    lax.fori_loop(0, length // BLOCK, project, 0)
    qkv[length:, :] = jnp.zeros((spare, 3 * width), BF16)

    def tile(index, carry):
        frames_at = rows.frames_at(part, index)
        here = at(index * BLOCK, BLOCK, BLOCK)
        if part:
            for copy in copies(index):
                copy.wait()
        limit, column = softmax_parts(rows, part, length)
        inside = BLOCK * index + lax.broadcasted_iota(jnp.int32, (BLOCK, 1), 0)
        inside = inside < (rows.rows_c if part else rows.rows_a)
        frame_grads[frames_at, :] = jnp.where(inside, dz_one[here, :], 0.0)
        for h in range(2):
            low, high = h * head, (h + 1) * head
            query = qkv[frames_at, low:high]
            key = qkv[:length, width + low : width + high]
            value = qkv[:length, 2 * width + low : 2 * width + high]
            upstream = d_mixed[here, low:high]
            upstream = jnp.where(inside, upstream, jnp.zeros_like(upstream))
            shift = jnp.where(inside, soft[here, h : h + 1], -MASKED)
            mean = jnp.where(inside, soft[here, 2 + h : 3 + h], 0.0)
            scores = mask_keys(dot_nt(query, key), column, limit)
            weights = jnp.exp2(scores * (scale * LOG2E) - shift)
            d_weights = dot_nt(upstream, value)
            d_scores = (weights * (d_weights - mean)).astype(BF16)
            d_proj[frames_at, low:high] = (dot(d_scores, key) * scale).astype(BF16)
            keys[:, low:high] += dot_tn(d_scores, query)
            values[:, low:high] += dot_tn(weights.astype(BF16), upstream)
        return carry

    lax.fori_loop(0, tiles, tile, 0)
    d_proj[0:length, width : 2 * width] = (keys[...] * scale).astype(BF16)
    d_proj[0:length, 2 * width : 3 * width] = values[...].astype(BF16)
    for distance, target in enumerate(targets):
        here = at((rows.member ^ distance) * quarter, quarter, quarter)
        target[...] = (frame_grads[here, :] + dot_nt(d_proj[here, :], w_qkv[...])).astype(BF16)
    grads = dot_tn(placed[0:length, :], d_proj[0:length, :])
    if part == 0:
        grad_qkv[...] = grads
        lax.fori_loop(0, rows.blocks, finish, 0)
        return
    blocks = refs[11]
    grad_before, grad_out, small, conv_bias = inputs
    grads = (grads + grad_before[...]).astype(BF16)
    for q in range(3):
        blocks[q, :, :] = grads[:, q * width : (q + 1) * width]
    blocks[3, :, :] = grad_out[...].astype(BF16)
    line = lax.broadcasted_iota(jnp.int32, (8, 1), 0)
    for j, target in enumerate(late):
        target[0:width, :] = blocks[rows.member ^ j]
        bias = conv_bias[0:1, j * width : (j + 1) * width]
        tail = jnp.where(line == 6, bias, small[...])
        tail = jnp.concatenate([tail, jnp.zeros((SMALL_ROWS - 8, width), F32)], axis=0)
        target[width : width + SMALL_ROWS, :] = tail.astype(BF16)


def collect(paired, lengths, *refs):
    pieces, result = refs[:-1], refs[-1]
    if paired:
        whole_parts = [piece[0] for piece in pieces]
        shared_parts = [piece[1] for piece in pieces]
    else:
        whole_parts = [piece[...] for piece in pieces[:4]]
        shared_parts = [piece[...] for piece in pieces[4:]]
    member = lax.axis_index("tensor")
    whole, shared = plan(lengths)
    for distance in range(4):
        slot = choose(member ^ distance, whole) % 8
        result[slot] = whole_parts[distance].astype(result.dtype)
    for side in range(2):
        second = (member >= 2) == (side == 0)
        slot = jnp.where(second, shared[1], shared[0]) % 8
        total = shared_parts[2 * side].astype(F32) + shared_parts[2 * side + 1].astype(F32)
        result[slot] = total.astype(result.dtype)


def finish_late(own, p1, p2, p3, *refs):
    grad_qkv, grad_out = refs[:2]
    vectors, blocks = refs[2:-1], refs[-1]
    width = grad_out.shape[0]
    member = lax.axis_index("tensor")
    for distance, piece in enumerate((own, p1, p2, p3)):
        blocks[member ^ distance] = piece[0:width, :].astype(F32)
    for q in range(3):
        grad_qkv[:, q * width : (q + 1) * width] = blocks[q]
    grad_out[...] = blocks[3]
    tail = own[width : width + 16, :].astype(F32)
    for i, vector in enumerate(vectors):
        vector[...] = tail[i : i + 1, :]


def finish_filters(steps, *refs):
    parts, (grad_conv, grad_proj, work) = refs[:-3], refs[-3:]
    where = lax.axis_index("dp")
    depth = grad_conv.shape[0]
    start = 0
    for step, value, other in zip(steps, parts[::2], parts[1::2]):
        half = value.shape[0]
        bit = (where // step) % 2
        work[at(start + bit * half, half), :] = value[...]
        work[at(start + (1 - bit) * half, half), :] = other[...]
        start += 2 * half
    grad_conv[...] = work[0:depth, :].astype(F32)
    grad_proj[...] = work[depth:, :].astype(F32)


def shards(
    frames,
    lengths,
    w_qkv,
    w_out,
    b_out,
    gain_one,
    shift_one,
    w_conv,
    b_conv,
    w_proj,
    b_proj,
    gain_two,
    shift_two,
    cotangent,
):
    count, quarter, width = frames.shape
    length = 4 * quarter
    taps = w_conv.shape[0]
    depth = taps * width
    filters = 4 * w_conv.shape[2]
    padded = length + BLOCK
    space = 2 * length
    limit = 7 * BLOCK
    smem = pl.BlockSpec(memory_space=pltpu.SMEM)
    vmem = pl.BlockSpec(memory_space=pltpu.VMEM)
    anywhere = pl.BlockSpec(memory_space=pl.ANY)
    shape = jax.ShapeDtypeStruct
    dp_size = lax.axis_size("dp")
    dp_place = lax.axis_index("dp")
    b_out, gain_one, shift_one, b_proj, gain_two, shift_two = [
        v[None] for v in (b_out, gain_one, shift_one, b_proj, gain_two, shift_two)
    ]

    def hop(value, distance):
        return lax.ppermute(value, "tensor", [(i, i ^ distance) for i in range(4)])

    def dp_hop(value, distance):
        return lax.ppermute(value, "dp", [(i, i ^ distance) for i in range(dp_size)])

    def after(value, *others):
        return lax.optimization_barrier((value,) + others)[0]

    def spread_out(parts):
        return [parts[0]] + [hop(parts[d], d) for d in (1, 2, 3)]

    pack_rows = (depth + width + 64) // 64 * 64
    piece = pack_rows // 4
    pack, *frame_picks, own_piece = pl.pallas_call(
        begin_group,
        out_shape=[shape((pack_rows, width), BF16)]
        + [shape((n, quarter, width), BF16) for n in (2, 2, 3)]
        + [shape((piece, width), BF16)],
        in_specs=[smem] + [vmem] * 4,
        out_specs=[vmem] * 5,
        compiler_params=params(),
        name="begin_group",
    )(lengths, frames, w_conv.reshape(depth, width), w_proj, b_conv[None])
    far0 = hop(own_piece, 2)
    near_pack = hop(pack, 1)
    cot_picks = pl.pallas_call(
        pick,
        out_shape=[shape((2, quarter, width), BF16)] * 4,
        in_specs=[smem, vmem],
        out_specs=[vmem] * 4,
        compiler_params=params(),
        name="pick_cotangent",
    )(lengths, after(cotangent, *frame_picks))
    far0, near_pack, *cot_picks = lax.optimization_barrier((far0, near_pack, *cot_picks))
    far_frames = hop(frame_picks[2], 2)
    near_frames = hop(frame_picks[1], 1)
    far1, far2, near_frames = lax.optimization_barrier((dp_hop(far0, 1), dp_hop(far0, 2), near_frames))
    last = [dp_hop(far2[: piece // 2], 1), dp_hop(far1[piece // 2 :], 2)]
    frame_parts = [frame_picks[0], near_frames, far_frames, hop(far_frames[:2], 1)]
    cot_parts = spread_out([after(part, *frame_parts) for part in cot_picks])

    rows = length + length // 2
    normed, stats, mixed = pl.pallas_call(
        attention_forward,
        out_shape=(
            shape((space, width), F32),
            shape((space, 128), F32),
            shape((space, width), BF16),
        ),
        in_specs=[smem] + [vmem] * 7,
        out_specs=[anywhere] * 3,
        scratch_shapes=[
            pltpu.VMEM((2, padded, width), BF16),
            pltpu.VMEM((2, padded, 2 * width), BF16),
            pltpu.VMEM((2, 2, length, width), BF16),
            pltpu.VMEM((2, length, width), F32),
            pltpu.VMEM((2, length, 128), F32),
            pltpu.VMEM((2, length, width), BF16),
            pltpu.SemaphoreType.DMA((2, 3, length // BLOCK)),
        ],
        compiler_params=params(),
        cost_estimate=cost(1e6, 1e5),
        name="attention_forward",
    )(after(lengths, near_pack), *near(*frame_parts), w_qkv, w_out, b_out)

    last = [after(part, normed, *cot_parts) for part in last]
    far_pack = jnp.concatenate([far0, far1, far2] + last)
    far_near_pack = hop(far_pack, 1)
    packs = (pack, near_pack, far_pack, far_near_pack)

    chunk_rows = (depth + width) // 2
    block_count = limit // BLOCK
    result = pl.pallas_call(
        feed_forward,
        out_shape=[shape((2, quarter, width), BF16)] * 4
        + [shape((2, chunk_rows, width), BF16)] * 4
        + [
            shape((limit, filters), BF16),
            shape((limit, width), F32),
            shape((depth, filters), BF16),
            shape((8, width), F32),
            shape((8, filters), F32),
        ],
        in_specs=[smem, anywhere] + [vmem] * 4 + [anywhere] * 4 + [vmem] * 5,
        out_specs=[vmem] * 4 + [anywhere] * 7 + [vmem] * 2,
        scratch_shapes=[
            pltpu.VMEM((pack_rows, filters), BF16),
            pltpu.VMEM((limit, width), F32),
            pltpu.VMEM((limit + 2 * HALO, width), F32),
            pltpu.VMEM((limit, depth), BF16),
            pltpu.VMEM((2, BLOCK, filters), F32),
            pltpu.VMEM((BLOCK, filters), F32),
            pltpu.VMEM((limit, filters), BF16),
            pltpu.VMEM((limit, width), BF16),
            pltpu.VMEM((limit, filters), BF16),
            pltpu.VMEM((limit, width), F32),
            pltpu.VMEM((4, depth + width, width), BF16),
            pltpu.VMEM((2, padded, width), BF16),
            pltpu.VMEM((space, width), BF16),
            pltpu.VMEM((space, width), BF16),
            pltpu.VMEM((padded, width), BF16),
            pltpu.SemaphoreType.DMA((FILTER_COPIES,)),
            pltpu.SemaphoreType.DMA((block_count,)),
            pltpu.SemaphoreType.DMA((2, block_count)),
            pltpu.SemaphoreType.DMA((taps + 1, 4)),
            pltpu.SemaphoreType.DMA((1,)),
        ],
        compiler_params=pltpu.CompilerParams(vmem_limit_bytes=50 * 2**20),
        cost_estimate=cost(1e6, 1e5),
        name="feed_forward",
    )(lengths, normed, *near(*cot_parts, *packs), gain_one, shift_one, b_proj, gain_two, shift_two)
    outputs, kept, sent = result[:4], result[4:6], result[6:8]
    d_hidden, dz_two, conv, small_two, conv_bias = result[8:]

    def add(a, b):
        return (a.astype(F32) + b.astype(F32)).astype(BF16)

    def total(*parts):
        return sum(part.astype(F32) for part in parts).astype(BF16)

    def halves(value, step):
        half = value.shape[-2] // 2
        bit = (dp_place // step) % 2
        axis = value.ndim - 2
        parts = value.reshape(value.shape[:-2] + (2, half, width))
        keep = lax.dynamic_index_in_dim(parts, bit, axis, keepdims=False)
        send = lax.dynamic_index_in_dim(parts, 1 - bit, axis, keepdims=False)
        return keep, dp_hop(send, step)

    def joined(value, other, step):
        bit = (dp_place // step) % 2
        return jnp.where(bit == 0, jnp.concatenate([value, other]), jnp.concatenate([other, value]))

    def begin(value, step):
        return (value[0], hop(value[1], 2)) if step == 0 else halves(value, step)

    def collected(parts, dtype, name):
        return pl.pallas_call(
            functools.partial(collect, len(parts) == 4),
            out_shape=shape((count, quarter, width), dtype),
            in_specs=[smem] + [vmem] * len(parts),
            out_specs=vmem,
            compiler_params=params(),
            name=name,
        )(lengths, *near(*parts))

    more = [2**i for i in range(2, 20) if 2**i < dp_size]
    orders = [[1, 0, 2], [0, 2, 1]]
    moving = [(kept[c], hop(sent[c], 1)) for c in range(2)]
    out_parts = spread_out(outputs)

    d_first = pl.pallas_call(
        conv_backward,
        out_shape=shape((limit, width), F32),
        in_specs=[smem] + [anywhere] * 3,
        out_specs=anywhere,
        scratch_shapes=[
            pltpu.VMEM((depth, filters), BF16),
            pltpu.VMEM((limit, filters), BF16),
            pltpu.VMEM((limit, width), F32),
            pltpu.VMEM((limit, width), F32),
            pltpu.VMEM((limit + HALO, width), F32),
            pltpu.SemaphoreType.DMA((taps,)),
            pltpu.SemaphoreType.DMA((2, block_count)),
            pltpu.SemaphoreType.DMA((1, block_count)),
        ],
        compiler_params=params(),
        cost_estimate=cost(1e6, 1e5),
        name="conv_backward",
    )(lengths, d_hidden, conv, dz_two)

    def attention_back(part, arrays, inputs, ties):
        late_rows = width + SMALL_ROWS
        if part:
            out_shapes = [shape((late_rows, width), BF16)] * 4
            out_specs = [vmem] * 4
            more_scratch = [pltpu.VMEM((4, width, width), BF16)]
        else:
            out_shapes = [
                shape((width, 3 * width), F32),
                shape((space, width), F32),
                shape((space, width), BF16),
                shape((space, 128), F32),
                shape((width, width), F32),
                shape((8, width), F32),
            ]
            out_specs = [vmem] + [anywhere] * 3 + [vmem] * 2
            more_scratch = [
                pltpu.VMEM((limit, width), F32),
                pltpu.VMEM((limit, width), F32),
                pltpu.VMEM((limit, 128), F32),
                pltpu.VMEM((limit, width), BF16),
                pltpu.SemaphoreType.DMA((3, block_count)),
            ]
        held = length if part else limit
        return pl.pallas_call(
            functools.partial(attention_backward, part),
            out_shape=[shape((quarter, width), BF16)] * 4 + out_shapes,
            in_specs=[smem] + [anywhere] * 4 + [vmem] + [anywhere] * len(arrays) + [vmem] * len(inputs),
            out_specs=[vmem] * 4 + out_specs,
            scratch_shapes=[
                pltpu.VMEM((padded, width), BF16),
                pltpu.VMEM((padded, 3 * width), BF16),
                pltpu.VMEM((padded, 3 * width), BF16),
                pltpu.VMEM((length, width), F32),
                pltpu.VMEM((length, width), F32),
                pltpu.VMEM((padded, width), F32),
                pltpu.VMEM((held, width), F32),
                pltpu.VMEM((held, width), BF16),
                pltpu.VMEM((held, 128), F32),
                pltpu.SemaphoreType.DMA((4,)),
                pltpu.SemaphoreType.DMA((4, block_count)),
            ]
            + more_scratch,
            compiler_params=params(),
            cost_estimate=cost(1e6, 1e5),
            name=f"attention_backward_{'ac'[part]}",
        )(after(lengths, *ties), *frame_parts, w_qkv, *arrays, *inputs)

    moving = [(keep, after(other, d_first, *out_parts)) for keep, other in moving]
    state = [add(*pair) for pair in moving]
    moving = [begin(value, order[0]) for value, order in zip(state, orders)]
    *grads_a, grad_qkv, dz_one, d_mixed, soft, grad_out, small = attention_back(
        0, [d_first, normed, stats, mixed], [w_out, gain_one, small_two], state
    )
    moving = [(keep, after(other, grad_qkv)) for keep, other in moving]
    state = [add(*pair) for pair in moving]
    moving = [begin(value, order[1]) for value, order in zip(state, orders)]
    a_far = [hop(grads_a[d], d) for d in (2, 3)]
    *grads_c, late0, late1, late2, late3 = attention_back(
        1, [dz_one, d_mixed, soft], [grad_qkv, grad_out, small, conv_bias], state
    )
    moving = [(keep, after(other, late0, *a_far)) for keep, other in moving]
    state = [add(*pair) for pair in moving]

    late_parts = [hop(after(part, *state), d) for d, part in ((1, late1), (2, late2), (3, late3))]
    moving = [begin(value, order[2]) for value, order in zip(state, orders)]
    late = total(late0, *late_parts)
    state = jnp.concatenate([add(keep, after(other, late)) for keep, other in moving])
    near_grads = hop(after(jnp.stack([grads_a[1], grads_c[1]]), late), 1)
    others = [dp_hop(state, step) for step in more[:1]] + [near_grads]
    late_parts = [dp_hop(late, step) for step in (1, 2, 3)]
    output = collected([after(part, late) for part in out_parts], BF16, "collect_output")
    *others, p1, p2, p3, output = lax.optimization_barrier((*others, *late_parts, output))
    near_grads = others.pop()
    late = total(late, p1, p2, p3)
    for other in others:
        state = add(state, other)
    for step in more[1:]:
        state = add(state, dp_hop(state, step))
    state = jnp.split(state, 2)
    c_far = [hop(after(grads_c[d], late), d) for d in (2, 3)]
    backs = [[step for step in reversed(order) if step] for order in orders]
    others = [dp_hop(value, back[0]) for value, back in zip(state, backs)]
    for step in more:
        late = add(late, dp_hop(late, step))
    *others, late, f1, f2 = lax.optimization_barrier((*others, late, *c_far))
    c_far = [f1, f2]
    state = [joined(value, other, back[0]) for value, other, back in zip(state, others, backs)]
    body = late[:width]
    blocks = [hop(body, d) for d in (1, 2, 3)]
    d_frames = collected(
        [grads_a[0], near_grads[0]] + a_far + [grads_c[0], near_grads[1]] + c_far, F32, "collect_grad"
    )
    last = [back[-1] for back in backs]
    others = [dp_hop(value, step) for value, step in zip(state, last)]
    grad_conv, grad_proj = pl.pallas_call(
        functools.partial(finish_filters, last),
        out_shape=(shape((depth, width), F32), shape((width, width), F32)),
        in_specs=[vmem] * 4,
        out_specs=[vmem] * 2,
        scratch_shapes=[pltpu.VMEM((depth + width, width), BF16)],
        compiler_params=params(),
        name="finish_filters",
    )(*near(*[part for pair in zip(state, others) for part in pair]))
    grad_qkv, grad_out, *vectors = pl.pallas_call(
        finish_late,
        out_shape=[shape((width, 3 * width), F32), shape((width, width), F32)] + [shape((1, width), F32)] * 7,
        in_specs=[vmem] * 4,
        out_specs=[vmem] * 9,
        scratch_shapes=[pltpu.VMEM((4, width, width), F32)],
        compiler_params=params(),
        name="finish_late",
    )(*near(late, *blocks))
    vectors = [v.reshape(width) for v in vectors]
    return (
        output,
        d_frames,
        grad_qkv,
        grad_out,
        vectors[0],
        vectors[1],
        vectors[2],
        grad_conv.reshape(w_conv.shape),
        vectors[6],
        grad_proj,
        vectors[3],
        vectors[4],
        vectors[5],
    )


def solution(mesh):
    return jax.shard_map(
        shards,
        mesh=mesh,
        in_specs=(
            P("dp", "tensor", None),
            P("dp"),
            P(),
            P(),
            P(),
            P(),
            P(),
            P(None, None, "tensor"),
            P("tensor"),
            P("tensor", None),
            P(),
            P(),
            P(),
            P("dp", "tensor", None),
        ),
        out_specs=(
            P("dp", "tensor", None),
            P("dp", "tensor", None),
            P(),
            P(),
            P(),
            P(),
            P(),
            P(None, None, "tensor"),
            P("tensor"),
            P("tensor", None),
            P(),
            P(),
            P(),
        ),
        check_vma=False,
    )
```

```python
import functools
import itertools

import jax
import jax.experimental.pallas as pl
import jax.experimental.pallas.tpu as pltpu
import jax.numpy as jnp
import numpy as np
from jax import lax
from jax.sharding import PartitionSpec as P


EPSILON = 1e-05
F32 = jnp.float32
BF16 = jnp.bfloat16
HALO = 16
BLOCK = 256
MASKED = -1e30
GELU_A = float(np.sqrt(2.0 / np.pi))
GELU_B = 0.044715
LOG2E = float(np.log2(np.e))
VMEM_LIMIT = 54 * 2**20
SMALL_ROWS = 16


def near(*arrays):
    return [pltpu.with_memory_space_constraint(array, pltpu.VMEM) for array in arrays]


def params(**more):
    return pltpu.CompilerParams(vmem_limit_bytes=VMEM_LIMIT, **more)


def cost(flops, size):
    return pl.CostEstimate(flops=int(flops), bytes_accessed=int(size), transcendentals=0)


def dot(a, b):
    return jnp.dot(a, b, preferred_element_type=F32)


def dot_nt(a, b):
    return lax.dot_general(a, b, (((1,), (1,)), ((), ())), preferred_element_type=F32)


def dot_tn(a, b):
    return lax.dot_general(a, b, (((0,), (0,)), ((), ())), preferred_element_type=F32)


def at(start, size, step=HALO):
    return pl.ds(pl.multiple_of(start, step), size)


def up(value, step=HALO):
    return ((value + (step - 1)) // step) * step


def choose(index, options):
    result = options[-1]
    for i, option in enumerate(options[:-1]):
        result = jnp.where(index == i, option, result)
    return result


def plan(lengths):
    keys = [lengths[i] * 8 + i for i in range(6)]
    best, triples = None, None
    for pair in itertools.combinations(range(1, 6), 2):
        mine = (0,) + pair
        rest = tuple(i for i in range(6) if i not in mine)
        gap = jnp.abs(sum(lengths[i] for i in mine) - sum(lengths[i] for i in rest))
        option = [keys[i] for i in mine + rest]
        if best is None:
            best, triples = gap, option
        else:
            better = gap < best
            best = jnp.where(better, gap, best)
            triples = [jnp.where(better, new, old) for new, old in zip(option, triples)]
    whole, shared = [], []
    for a, b, c in (triples[:3], triples[3:]):
        a, b = jnp.maximum(a, b), jnp.minimum(a, b)
        a, c = jnp.maximum(a, c), jnp.minimum(a, c)
        b, c = jnp.maximum(b, c), jnp.minimum(b, c)
        whole += [a, b]
        shared.append(c)
    return whole, shared


class Rows:
    def __init__(self, lengths, length):
        self.member = lax.axis_index("tensor")
        whole, shared = plan(lengths)
        self.whole, self.shared = whole, shared
        role = self.member % 2
        second = self.member >= 2
        key_a = choose(self.member, whole)
        self.len_a = key_a // 8
        self.len_c = jnp.where(second, shared[1], shared[0]) // 8
        first_len = jnp.where(second, whole[2], whole[0]) // 8
        other_len = jnp.where(second, whole[3], whole[1]) // 8
        split = (other_len + self.len_c - first_len) // 2
        split = jnp.maximum((split + HALO // 2) // HALO * HALO, HALO)
        starts = role == 0
        self.own_from = jnp.where(starts, 0, split)
        self.own_to = jnp.where(starts, split, length)
        self.window = jnp.where(starts, 0, split - HALO)
        self.end = jnp.where(starts, jnp.minimum(split + HALO, self.len_c), self.len_c)
        self.rows_a = up(self.len_a) + HALO
        self.rows_c = jnp.maximum(up(self.end) - self.window, 0)
        self.tiles_a = (self.len_a + BLOCK - 1) // BLOCK
        self.tiles_c = (self.rows_c + BLOCK - 1) // BLOCK
        self.blocks = (self.rows_a + self.rows_c + BLOCK - 1) // BLOCK
        self.halo = self.rows_a + jnp.where(starts, split, 0)

    def masks(self, start, size):
        row = start + lax.broadcasted_iota(jnp.int32, (size, 1), 0)
        in_a = row < self.rows_a
        frame = jnp.where(in_a, row, row - self.rows_a + self.window)
        live = frame < jnp.where(in_a, self.len_a, self.end)
        inside = (frame >= self.own_from) & (frame < self.own_to)
        return live, live & (in_a | inside)

    def frames_at(self, part, index):
        return at(BLOCK * index + (self.window if part else 0), BLOCK)

    def base(self, part, index):
        return BLOCK * index + (self.rows_a if part else 0)


def piece_index(piece, part):
    return part if piece.shape[0] == 2 else 2 - part


def place(member, pieces, target):
    quarter = pieces[0].shape[1]
    for distance, piece in enumerate(pieces):
        rows = at((member ^ distance) * quarter, quarter, quarter)
        for part in range(2):
            target[part, rows, :] = piece[piece_index(piece, part)]


def pick(lengths, source, *targets):
    member = lax.axis_index("tensor")
    whole, shared = plan(lengths)
    for distance, target in enumerate(targets):
        there = member ^ distance
        if target.shape[0] == 3:
            target[0] = source[choose(there ^ 1, whole) % 8]
        target[piece_index(target, 0)] = source[choose(there, whole) % 8]
        target[piece_index(target, 1)] = source[jnp.where(there >= 2, shared[1], shared[0]) % 8]


def begin_group(lengths, source, w_conv, w_proj, b_conv, pack, p0, p1, p2, part):
    depth, width = w_conv.shape
    pack[0:depth, :] = w_conv[...]
    pack[depth : depth + width, :] = w_proj[...]
    high = b_conv[...].astype(BF16)
    rest = (b_conv[...] - high.astype(F32)).astype(BF16)
    last = depth + width
    pack[last : last + HALO, :] = jnp.broadcast_to(high, (HALO, width))
    pack[last + HALO :, :] = jnp.broadcast_to(rest, (pack.shape[0] - last - HALO, width))
    piece = part.shape[0]
    part[...] = pack[at((lax.axis_index("dp") % 4) * piece, piece), :]
    pick(lengths, source, p0, p1, p2)


def softmax_parts(rows, part, length):
    return (rows.len_c if part else rows.len_a), lax.broadcasted_iota(jnp.int32, (1, length), 1)


def mask_keys(scores, column, limit):
    half = scores.shape[1] // 2
    tail = jnp.where(column[:, half:] < limit, scores[:, half:], MASKED)
    return jnp.concatenate([scores[:, :half], tail], axis=1)


def attention_forward(
    lengths, r0, r1, r2, r3, w_qkv, w_out, b_out, normed, stats, mixed, placed, qkv, valued, n_out, s_out, m_out, sems
):
    quarter = r0.shape[1]
    length = 4 * quarter
    width = r0.shape[2]
    head = width // 2
    scale = head ** (-0.5) * LOG2E
    rows = Rows(lengths, length)
    spare = placed.shape[1] - length
    placed[:, length:, :] = jnp.zeros((2, spare, width), BF16)
    place(rows.member, (r0, r1, r2, r3), placed)
    for part in range(2):
        for h in range(2):
            valued[part, h, :, head:] = jnp.ones((length, head), BF16)

    def project(index, carry):
        here = at(index * BLOCK, BLOCK, BLOCK)
        for part in range(2):
            value = dot(placed[part, here, :], w_qkv[...]).astype(BF16)
            qkv[part, here, :] = value[:, : 2 * width]
            for h in range(2):
                valued[part, h, here, :head] = value[:, 2 * width + h * head : 2 * width + (h + 1) * head]
        return carry

    lax.fori_loop(0, length // BLOCK, project, 0)
    qkv[:, length:, :] = jnp.zeros((2, spare, 2 * width), BF16)
    lane = lax.broadcasted_iota(jnp.int32, (1, 128), 1)

    def copies(part, index):
        there = at(rows.base(part, index), BLOCK)
        here = at(index * BLOCK, BLOCK, BLOCK)
        pairs = ((n_out, normed), (s_out, stats), (m_out, mixed))
        return [
            pltpu.make_async_copy(source.at[part, here], target.at[there], sems.at[part, i, index])
            for i, (source, target) in enumerate(pairs)
        ]

    def tile(part, index, carry):
        frames_at = rows.frames_at(part, index)
        here = at(index * BLOCK, BLOCK, BLOCK)
        limit, column = softmax_parts(rows, part, length)
        mixtures, logs = [], []
        for h in range(2):
            low, high = h * head, (h + 1) * head
            scores = dot_nt(qkv[part, frames_at, low:high], qkv[part, :length, width + low : width + high])
            scores = mask_keys(scores, column, limit)
            highest = jnp.max(scores, axis=-1, keepdims=True) * scale
            exponent = jnp.exp2(scores * scale - highest).astype(BF16)
            summed = dot(exponent, valued[part, h])
            total = summed[:, head : head + 1]
            mixtures.append((summed[:, :head] / total).astype(BF16))
            logs.append(highest + jnp.log2(total))
        mixture = jnp.concatenate(mixtures, axis=1)
        m_out[part, here, :] = mixture
        residual = placed[part, frames_at, :].astype(F32) + dot(mixture, w_out[...]) + b_out[...]
        centred = residual - jnp.mean(residual, axis=-1, keepdims=True)
        inverse = lax.rsqrt(jnp.mean(centred * centred, axis=-1, keepdims=True) + EPSILON)
        n_out[part, here, :] = centred * inverse
        s_out[part, here, :] = jnp.where(lane == 0, logs[0], jnp.where(lane == 1, logs[1], inverse))
        for copy in copies(part, index):
            copy.start()
        return carry

    def finish(part, index, carry):
        for copy in copies(part, index):
            copy.wait()
        return carry

    for part, count in enumerate((rows.tiles_a, rows.tiles_c)):
        lax.fori_loop(0, count, functools.partial(tile, part), 0)
        lax.fori_loop(0, count, functools.partial(finish, part), 0)


def gelu_pair(x):
    square = x * x
    t = jnp.tanh(GELU_A * x * (1.0 + GELU_B * square))
    half = 0.5 * (1.0 + t)
    slope = half + (0.5 * GELU_A) * x * (1.0 - t * t) * (1.0 + 3.0 * GELU_B * square)
    return x * half, slope


def load_filters(near, far, target, sems):
    width = near[0].shape[1]
    piece = near[0].shape[0] // 4
    shift = lax.axis_index("dp") % 4
    copies = []
    for j, source in enumerate(near):
        copies.append((source, target.at[:, pl.ds(j * width, width)]))
    for j, source in enumerate(far):
        for i in range(4):
            there = at((shift ^ i) * piece, piece)
            part = pl.ds((2 + j) * width, width)
            copies.append((source.at[pl.ds(i * piece, piece)], target.at[there, part]))
    copies = [
        pltpu.make_async_copy(source, there, sems.at[i]) for i, (source, there) in enumerate(copies)
    ]
    for copy in copies:
        copy.start()
    return copies


FILTER_COPIES = 10


def feed_forward(
    lengths,
    normed,
    c0,
    c1,
    c2,
    c3,
    pack0,
    pack1,
    far0,
    far1,
    gain_one,
    shift_one,
    b_proj,
    gain_two,
    shift_two,
    o0,
    o1,
    o_far,
    kept,
    sent,
    d_hidden_out,
    dz_out,
    conv_out,
    small,
    conv_bias,
    weights,
    units,
    first,
    columns,
    hidden,
    slope,
    active,
    d_branch,
    d_hidden,
    dz_two,
    grads,
    cot_frames,
    cot_rows,
    out_rows,
    out_c,
    load_sems,
    unit_sems,
    out_sems,
    grad_sems,
    conv_sem,
):
    quarter, width = c0.shape[1:]
    length = 4 * quarter
    filters = weights.shape[1]
    taps = columns.shape[1] // width
    depth = taps * width
    reach = taps // 2
    loads = load_filters((pack0, pack1), (far0, far1), weights, load_sems)
    rows = Rows(lengths, length)
    blocks = rows.blocks

    def unit_copy(index):
        here = at(index * BLOCK, BLOCK, BLOCK)
        return pltpu.make_async_copy(normed.at[here], units.at[here], unit_sems.at[index])

    def start_unit(index, carry):
        unit_copy(index).start()
        return carry

    lax.fori_loop(0, blocks, start_unit, 0)
    place(rows.member, (c0, c1, c2, c3), cot_frames)
    cot_frames[:, length:, :] = jnp.zeros((2, cot_frames.shape[1] - length, width), BF16)
    cot_rows[0:length, :] = cot_frames[0, 0:length, :]

    def gather_cot(index, carry):
        cot_rows[at(rows.base(1, index), BLOCK), :] = cot_frames[1, rows.frames_at(1, index), :]
        return carry

    lax.fori_loop(0, rows.tiles_c, gather_cot, 0)
    out_rows[...] = jnp.zeros(out_rows.shape, BF16)
    small[...] = jnp.zeros(small.shape, F32)
    conv_bias[...] = jnp.zeros(conv_bias.shape, F32)

    first[0:HALO, :] = jnp.zeros((HALO, width), F32)

    def make_first(index, carry):
        base = index * BLOCK
        unit_copy(index).wait()
        live, _ = rows.masks(base, BLOCK)
        value = units[at(base, BLOCK), :] * gain_one[...] + shift_one[...]
        first[at(base + HALO, BLOCK), :] = jnp.where(live, value, 0.0)
        return carry

    lax.fori_loop(0, blocks, make_first, 0)
    first[at(blocks * BLOCK + HALO, HALO), :] = jnp.zeros((HALO, width), F32)

    def make_columns(index, carry):
        base = index * BLOCK
        around = first[at(base + HALO - 8, BLOCK + 16, 8), :]
        for k in range(taps):
            columns[at(base, BLOCK, BLOCK), k * width : (k + 1) * width] = around[
                8 - reach + k : 8 - reach + k + BLOCK
            ].astype(BF16)
        return carry

    lax.fori_loop(0, blocks, make_columns, 0)
    for copy in loads:
        copy.wait()
    conv_copy = pltpu.make_async_copy(weights.at[pl.ds(0, depth)], conv_out, conv_sem.at[0])
    conv_copy.start()

    def out_copies(index):
        here = at(index * BLOCK, BLOCK, BLOCK)
        return [
            pltpu.make_async_copy(d_hidden.at[here], d_hidden_out.at[here], out_sems.at[0, index]),
            pltpu.make_async_copy(dz_two.at[here], dz_out.at[here], out_sems.at[1, index]),
        ]

    def conv(index, target):
        target[...] = dot(columns[at(index * BLOCK, BLOCK, BLOCK), :], weights[0:depth, :])

    def rest(index, source):
        base = index * BLOCK
        here = at(base, BLOCK, BLOCK)
        live, own = rows.masks(base, BLOCK)
        branch = jnp.zeros((BLOCK, width), F32)
        for j in range(filters // width):
            part = slice(j * width, (j + 1) * width)
            bias = weights[depth + width : depth + width + 1, part].astype(F32) + weights[
                depth + width + 16 : depth + width + 17, part
            ].astype(F32)
            value, derivative = gelu_pair(source[:, part] + bias)
            value = value.astype(BF16)
            active[here, part] = value
            slope[:, part] = derivative
            branch = branch + dot(value, weights[depth : depth + width, part])
        residual = first[at(base + HALO, BLOCK), :] + branch + b_proj[...]
        centred = residual - jnp.mean(residual, axis=-1, keepdims=True)
        inverse = lax.rsqrt(jnp.mean(centred * centred, axis=-1, keepdims=True) + EPSILON)
        normed_two = centred * inverse
        out_rows[here, :] = jnp.where(own, normed_two * gain_two[...] + shift_two[...], 0.0).astype(BF16)
        upstream = jnp.where(live, cot_rows[here, :].astype(F32), 0.0)
        counted = jnp.where(own, upstream, 0.0)
        scaled = upstream * gain_two[...]
        dz = inverse * (
            scaled
            - jnp.mean(scaled, axis=-1, keepdims=True)
            - normed_two * jnp.mean(scaled * normed_two, axis=-1, keepdims=True)
        )
        dz_two[here, :] = dz
        small[3:4, :] += jnp.sum(jnp.where(own, dz, 0.0), axis=0, keepdims=True)
        small[4:5, :] += jnp.sum(counted * normed_two, axis=0, keepdims=True)
        small[5:6, :] += jnp.sum(counted, axis=0, keepdims=True)
        low = dz.astype(BF16)
        d_branch[here, :] = jnp.where(own, low, jnp.zeros_like(low))
        for j in range(filters // width):
            part = slice(j * width, (j + 1) * width)
            grad = dot_nt(low, weights[depth : depth + width, part]) * slope[:, part]
            conv_bias[0:1, part] += jnp.sum(jnp.where(own, grad, 0.0), axis=0, keepdims=True)
            d_hidden[here, part] = grad.astype(BF16)
        for copy in out_copies(index):
            copy.start()

    even, odd = hidden.at[0], hidden.at[1]
    conv(0, even)

    def step(pair, carry):
        index = 2 * pair
        conv(index + 1, odd)
        rest(index, even)
        conv(index + 2, even)
        rest(index + 1, odd)
        return carry

    lax.fori_loop(0, (blocks - 1) // 2, step, 0)

    @pl.when(blocks % 2 == 1)
    def _():
        rest(blocks - 1, even)

    @pl.when(blocks % 2 == 0)
    def _():
        conv(blocks - 1, odd)
        rest(blocks - 2, even)
        rest(blocks - 1, odd)

    columns[at(rows.halo, HALO), :] = jnp.zeros((HALO, columns.shape[1]), BF16)

    per_chunk = (taps + 1) // 2

    x_bit, z_bit = lax.axis_index("dp") % 2, (lax.axis_index("dp") // 2) % 2
    half_rows = kept.shape[2]
    piece = half_rows // 5

    def grad_copies(k, chunk):
        copies = []
        for u in range(width // piece):
            row = (k - chunk * per_chunk) * width + u * piece
            half = row // half_rows
            there = at(row - half * half_rows, piece, piece)
            here = at(k * width + u * piece, piece, piece)
            for j in range(filters // width):
                place = (half ^ x_bit, j // 2) if chunk == 0 else (j // 2, 2 + (half ^ z_bit))
                target = (kept, sent)[j % 2].at[place[0], place[1], there]
                copies.append(pltpu.make_async_copy(grads.at[j, here], target, grad_sems.at[k, j, u]))
        return copies

    for count in range(4, active.shape[0] // BLOCK + 1):

        @pl.when(blocks == count)
        def _():
            n = count * BLOCK

            def tap(k, carry):
                here = at(k * width, width, width)
                value = dot_tn(columns[0:n, here], d_hidden[0:n, :]).astype(BF16)
                for j in range(filters // width):
                    grads[j, here, :] = value[:, j * width : (j + 1) * width]
                for chunk in range(2):

                    @pl.when(k // per_chunk == chunk)
                    def _():
                        for copy in grad_copies(k, chunk):
                            copy.start()

                return carry

            lax.fori_loop(0, taps, tap, 0)
            value = dot_tn(active[0:n, :], d_branch[0:n, :]).astype(BF16)
            for j in range(filters // width):
                grads[j, depth:, :] = value[j * width : (j + 1) * width, :]
            for copy in grad_copies(taps, 1):
                copy.start()

    out_c[...] = jnp.zeros(out_c.shape, BF16)

    def scatter_out(index, carry):
        out_c[rows.frames_at(1, index), :] = out_rows[at(rows.base(1, index), BLOCK), :]
        return carry

    lax.fori_loop(0, rows.tiles_c, scatter_out, 0)
    for distance, (target, slot) in enumerate(((o0, 0), (o1, 0), (o_far, 0), (o_far, 2))):
        start = (rows.member ^ distance) * quarter
        there = at(start, quarter, quarter)
        row = start + lax.broadcasted_iota(jnp.int32, (quarter, 1), 0)
        value = out_rows[there, :]
        target[slot] = jnp.where(row < rows.len_a, value, jnp.zeros_like(value))
        target[slot + 1] = out_c[there, :]

    conv_copy.wait()

    def finish(index, carry):
        for copy in out_copies(index):
            copy.wait()
        return carry

    lax.fori_loop(0, blocks, finish, 0)

    def finish_grads(chunk, k, carry):
        for copy in grad_copies(k, chunk):
            copy.wait()
        return carry

    lax.fori_loop(0, per_chunk, functools.partial(finish_grads, 0), 0)
    lax.fori_loop(per_chunk, 2 * per_chunk, functools.partial(finish_grads, 1), 0)


def block_copies(pairs, sems, index):
    here = at(index * BLOCK, BLOCK, BLOCK)
    return [
        pltpu.make_async_copy(source.at[here], target.at[here], sems.at[i, index])
        for i, (source, target) in enumerate(pairs)
    ]


def conv_backward(
    lengths, d_hidden_in, conv, dz_in, d_first_out, weights, d_hidden, dz_two, d_first, sums, conv_sems, in_sems, out_sems
):
    width = dz_two.shape[1]
    taps = conv.shape[0] // width
    reach = taps // 2
    blocks = Rows(lengths, 4 * width).blocks
    conv_copies = [
        pltpu.make_async_copy(
            conv.at[pl.ds(k * width, width)], weights.at[pl.ds(k * width, width)], conv_sems.at[k]
        )
        for k in range(taps)
    ]
    into = ((d_hidden_in, d_hidden), (dz_in, dz_two))
    onto = ((d_first, d_first_out),)
    for copy in conv_copies:
        copy.start()

    def start(index, carry):
        for copy in block_copies(into, in_sems, index):
            copy.start()
        return carry

    lax.fori_loop(0, blocks, start, 0)
    sums[0:HALO, :] = jnp.zeros((HALO, width), F32)
    for copy in conv_copies:
        copy.wait()

    def back(index, carry):
        base = index * BLOCK
        for copy in block_copies(into, in_sems, index):
            copy.wait()
        value = d_hidden[at(base, BLOCK, BLOCK), :]
        total = jnp.zeros((BLOCK + HALO, width), F32)
        for k in range(taps):
            part = dot_nt(value, weights[k * width : (k + 1) * width, :])
            part = jnp.concatenate([part, jnp.zeros((HALO, width), F32)], axis=0)
            total = total + pltpu.roll(part, 8 - reach + k, axis=0)
        sums[at(base, HALO), :] += total[0:HALO]
        sums[at(base + HALO, BLOCK), :] = total[HALO:]
        return carry

    lax.fori_loop(0, blocks, back, 0)

    def finish(index, carry):
        base = index * BLOCK
        here = at(base, BLOCK, BLOCK)
        d_first[here, :] = dz_two[here, :] + sums[at(base + 8, BLOCK, 8), :]
        block_copies(onto, out_sems, index)[0].start()
        return carry

    lax.fori_loop(0, blocks, finish, 0)

    def drain(index, carry):
        block_copies(onto, out_sems, index)[0].wait()
        return carry

    lax.fori_loop(0, blocks, drain, 0)


def first_norm_backward(rows, ins, outs, blocks_in, blocks_out, in_sems, out_sems, w_out, gain_one, small, grad_out):
    d_first, normed, stats, mixed = blocks_in
    dz_one, d_mixed, soft = blocks_out
    into, onto = tuple(zip(ins, blocks_in)), tuple(zip(blocks_out, outs))
    width = normed.shape[1]
    head = width // 2
    lane = lax.broadcasted_iota(jnp.int32, (1, 128), 1)

    def block(index, carry):
        base = index * BLOCK
        here = at(base, BLOCK, BLOCK)
        for copy in block_copies(into, in_sems, index):
            copy.wait()
        _, own = rows.masks(base, BLOCK)
        total = jnp.where(own, d_first[here, :], 0.0)
        unit = jnp.where(own, normed[here, :], 0.0)
        kept = stats[here, :]
        inverse = kept[:, 2:3]
        scaled = total * gain_one[...]
        dz = inverse * (
            scaled
            - jnp.mean(scaled, axis=-1, keepdims=True)
            - unit * jnp.mean(scaled * unit, axis=-1, keepdims=True)
        )
        dz = jnp.where(own, dz, 0.0)
        dz_one[here, :] = dz
        small[0:1, :] += jnp.sum(dz, axis=0, keepdims=True)
        small[1:2, :] += jnp.sum(total * unit, axis=0, keepdims=True)
        small[2:3, :] += jnp.sum(total, axis=0, keepdims=True)
        low = dz.astype(BF16)
        upstream = dot_nt(low, w_out[...]).astype(BF16)
        d_mixed[here, :] = upstream
        mixture = mixed[here, :]
        mixture = jnp.where(own, mixture, jnp.zeros_like(mixture))
        grad_out[...] += dot_tn(mixture, low)
        product = upstream.astype(F32) * mixture.astype(F32)
        means = [jnp.sum(product[:, h * head : (h + 1) * head], axis=-1, keepdims=True) for h in range(2)]
        soft[here, :] = jnp.where(
            lane < 2, jnp.where(own, kept, -MASKED), jnp.where(lane == 2, means[0], means[1])
        )
        for copy in block_copies(onto, out_sems, index):
            copy.start()
        return carry

    lax.fori_loop(0, rows.blocks, block, 0)

    def finish(index, carry):
        for copy in block_copies(onto, out_sems, index):
            copy.wait()
        return carry

    return finish


def attention_backward(part, *refs):
    (lengths, r0, r1, r2, r3, w_qkv), refs = refs[:6], refs[6:]
    if part:
        in_refs, refs = refs[:3], refs[3:]
        inputs, refs = refs[:4], refs[4:]
        (g0, g1, g_far), refs = refs[:3], refs[3:]
        late, refs = refs[:4], refs[4:]
    else:
        in_refs, refs = refs[:4], refs[4:]
        (w_out, gain_one, small_two), refs = refs[:3], refs[3:]
        (g0, g1, g_far), refs = refs[:3], refs[3:]
        grad_qkv, refs = refs[0], refs[1:]
        out_refs, refs = refs[:3], refs[3:]
        (grad_out, small), refs = refs[:2], refs[2:]
    placed, qkv, d_proj, keys, values, frame_grads, dz_one, d_mixed, soft, place_sems, in_sems = refs[:11]
    quarter = r0.shape[1]
    length = 4 * quarter
    width = r0.shape[2]
    head = width // 2
    scale = head ** (-0.5)
    rows = Rows(lengths, length)
    tiles = rows.tiles_c if part else rows.tiles_a
    spare = placed.shape[0] - length
    places = [
        pltpu.make_async_copy(
            piece.at[piece_index(piece, part)],
            placed.at[at((rows.member ^ distance) * quarter, quarter, quarter)],
            place_sems.at[distance],
        )
        for distance, piece in enumerate((r0, r1, r2, r3))
    ]

    def copies(index):
        there = at(rows.base(part, index), BLOCK)
        here = at(index * BLOCK, BLOCK, BLOCK)
        return [
            pltpu.make_async_copy(source.at[there], target.at[here], in_sems.at[i, index])
            for i, (source, target) in enumerate(zip(in_refs, (dz_one, d_mixed, soft)))
        ]

    if part:

        def start(index, carry):
            for copy in copies(index):
                copy.start()
            return carry

        lax.fori_loop(0, tiles, start, 0)
    else:
        blocks_in, out_sems = refs[11:15], refs[15]

        def start(index, carry):
            for copy in block_copies(tuple(zip(in_refs, blocks_in)), in_sems, index):
                copy.start()
            return carry

        lax.fori_loop(0, rows.blocks, start, 0)
    for copy in places:
        copy.start()
    placed[length:, :] = jnp.zeros((spare, width), BF16)
    d_proj[...] = jnp.zeros(d_proj.shape, BF16)
    keys[...] = jnp.zeros(keys.shape, F32)
    values[...] = jnp.zeros(values.shape, F32)
    frame_grads[...] = jnp.zeros(frame_grads.shape, F32)
    if not part:
        small[...] = small_two[...]
        grad_out[...] = jnp.zeros(grad_out.shape, F32)
        finish = first_norm_backward(
            rows, in_refs, out_refs, blocks_in, (dz_one, d_mixed, soft), in_sems, out_sems, w_out, gain_one, small, grad_out
        )
    for copy in places:
        copy.wait()

    def project(index, carry):
        here = at(index * BLOCK, BLOCK, BLOCK)
        qkv[here, :] = dot(placed[here, :], w_qkv[...]).astype(BF16)
        return carry

    lax.fori_loop(0, length // BLOCK, project, 0)
    qkv[length:, :] = jnp.zeros((spare, 3 * width), BF16)

    def tile(index, carry):
        frames_at = rows.frames_at(part, index)
        here = at(index * BLOCK, BLOCK, BLOCK)
        if part:
            for copy in copies(index):
                copy.wait()
        limit, column = softmax_parts(rows, part, length)
        inside = BLOCK * index + lax.broadcasted_iota(jnp.int32, (BLOCK, 1), 0)
        inside = inside < (rows.rows_c if part else rows.rows_a)
        frame_grads[frames_at, :] = jnp.where(inside, dz_one[here, :], 0.0)
        for h in range(2):
            low, high = h * head, (h + 1) * head
            query = qkv[frames_at, low:high]
            key = qkv[:length, width + low : width + high]
            value = qkv[:length, 2 * width + low : 2 * width + high]
            upstream = d_mixed[here, low:high]
            upstream = jnp.where(inside, upstream, jnp.zeros_like(upstream))
            shift = jnp.where(inside, soft[here, h : h + 1], -MASKED)
            mean = jnp.where(inside, soft[here, 2 + h : 3 + h], 0.0)
            scores = mask_keys(dot_nt(query, key), column, limit)
            weights = jnp.exp2(scores * (scale * LOG2E) - shift)
            d_weights = dot_nt(upstream, value)
            d_scores = (weights * (d_weights - mean)).astype(BF16)
            d_proj[frames_at, low:high] = (dot(d_scores, key) * scale).astype(BF16)
            keys[:, low:high] += dot_tn(d_scores, query)
            values[:, low:high] += dot_tn(weights.astype(BF16), upstream)
        return carry

    lax.fori_loop(0, tiles, tile, 0)
    d_proj[0:length, width : 2 * width] = (keys[...] * scale).astype(BF16)
    d_proj[0:length, 2 * width : 3 * width] = values[...].astype(BF16)
    for distance, target in enumerate((g0, g1, g_far.at[0], g_far.at[1])):
        here = at((rows.member ^ distance) * quarter, quarter, quarter)
        target[...] = (frame_grads[here, :] + dot_nt(d_proj[here, :], w_qkv[...])).astype(BF16)
    grads = dot_tn(placed[0:length, :], d_proj[0:length, :])
    if part == 0:
        grad_qkv[...] = grads
        lax.fori_loop(0, rows.blocks, finish, 0)
        return
    blocks = refs[11]
    grad_before, grad_out, small, conv_bias = inputs
    grads = (grads + grad_before[...]).astype(BF16)
    for q in range(3):
        blocks[q, :, :] = grads[:, q * width : (q + 1) * width]
    blocks[3, :, :] = grad_out[...].astype(BF16)
    line = lax.broadcasted_iota(jnp.int32, (8, 1), 0)
    for j, target in enumerate(late):
        target[0:width, :] = blocks[rows.member ^ j]
        bias = conv_bias[0:1, j * width : (j + 1) * width]
        tail = jnp.where(line == 6, bias, small[...])
        tail = jnp.concatenate([tail, jnp.zeros((SMALL_ROWS - 8, width), F32)], axis=0)
        target[width : width + SMALL_ROWS, :] = tail.astype(BF16)


def collect(places, lengths, *refs):
    result = refs[-1]
    member = lax.axis_index("tensor")
    whole, shared = plan(lengths)

    def piece(place):
        array, index = place
        return refs[array][...] if index is None else refs[array][index]

    for distance in range(4):
        slot = choose(member ^ distance, whole) % 8
        result[slot] = piece(places[distance][0]).astype(result.dtype)
    for side in range(2):
        second = (member >= 2) == (side == 0)
        slot = jnp.where(second, shared[1], shared[0]) % 8
        total = piece(places[2 * side][1]).astype(F32) + piece(places[2 * side + 1][1]).astype(F32)
        result[slot] = total.astype(result.dtype)


def finish_late(own, p1, p2, p3, *refs):
    grad_qkv, grad_out = refs[:2]
    vectors, blocks = refs[2:-1], refs[-1]
    width = grad_out.shape[0]
    member = lax.axis_index("tensor")
    for distance, piece in enumerate((own, p1, p2, p3)):
        blocks[member ^ distance] = piece[0:width, :].astype(F32)
    for q in range(3):
        grad_qkv[:, q * width : (q + 1) * width] = blocks[q]
    grad_out[...] = blocks[3]
    tail = own[width : width + 16, :].astype(F32)
    for i, vector in enumerate(vectors):
        vector[...] = tail[i : i + 1, :]


def finish_filters(steps, *refs):
    parts, (grad_conv, grad_proj, work) = refs[:-3], refs[-3:]
    where = lax.axis_index("dp")
    depth = grad_conv.shape[0]
    start = 0
    for step, value, other in zip(steps, parts[::2], parts[1::2]):
        half = value.shape[0]
        bit = (where // step) % 2
        work[at(start + bit * half, half), :] = value[...]
        work[at(start + (1 - bit) * half, half), :] = other[...]
        start += 2 * half
    grad_conv[...] = work[0:depth, :].astype(F32)
    grad_proj[...] = work[depth:, :].astype(F32)


def shards(
    frames,
    lengths,
    w_qkv,
    w_out,
    b_out,
    gain_one,
    shift_one,
    w_conv,
    b_conv,
    w_proj,
    b_proj,
    gain_two,
    shift_two,
    cotangent,
):
    count, quarter, width = frames.shape
    length = 4 * quarter
    taps = w_conv.shape[0]
    depth = taps * width
    filters = 4 * w_conv.shape[2]
    padded = length + BLOCK
    space = 2 * length
    limit = 7 * BLOCK
    smem = pl.BlockSpec(memory_space=pltpu.SMEM)
    vmem = pl.BlockSpec(memory_space=pltpu.VMEM)
    anywhere = pl.BlockSpec(memory_space=pl.ANY)
    shape = jax.ShapeDtypeStruct
    dp_size = lax.axis_size("dp")
    dp_place = lax.axis_index("dp")
    b_out, gain_one, shift_one, b_proj, gain_two, shift_two = [
        v[None] for v in (b_out, gain_one, shift_one, b_proj, gain_two, shift_two)
    ]

    def hop(value, distance):
        return lax.ppermute(value, "tensor", [(i, i ^ distance) for i in range(4)])

    def dp_hop(value, distance):
        return lax.ppermute(value, "dp", [(i, i ^ distance) for i in range(dp_size)])

    def after(value, *others):
        return lax.optimization_barrier((value,) + others)[0]

    def spread_out(parts):
        return [parts[0]] + [hop(parts[d], d) for d in (1, 2, 3)]

    pack_rows = (depth + width + 64) // 64 * 64
    piece = pack_rows // 4
    pack, *frame_picks, own_piece = pl.pallas_call(
        begin_group,
        out_shape=[shape((pack_rows, width), BF16)]
        + [shape((n, quarter, width), BF16) for n in (2, 2, 3)]
        + [shape((piece, width), BF16)],
        in_specs=[smem] + [vmem] * 4,
        out_specs=[vmem] * 5,
        compiler_params=params(),
        name="begin_group",
    )(lengths, frames, w_conv.reshape(depth, width), w_proj, b_conv[None])
    far0 = hop(own_piece, 2)
    near_pack = hop(pack, 1)
    cot_picks = pl.pallas_call(
        pick,
        out_shape=[shape((2, quarter, width), BF16)] * 4,
        in_specs=[smem, vmem],
        out_specs=[vmem] * 4,
        compiler_params=params(),
        name="pick_cotangent",
    )(lengths, after(cotangent, *frame_picks))
    far0, near_pack, *cot_picks = lax.optimization_barrier((far0, near_pack, *cot_picks))
    far_frames = hop(frame_picks[2], 2)
    near_frames = hop(frame_picks[1], 1)
    far1, far2, near_frames = lax.optimization_barrier((dp_hop(far0, 1), dp_hop(far0, 2), near_frames))
    last = [dp_hop(far2[: piece // 2], 1), dp_hop(far1[piece // 2 :], 2)]
    frame_parts = [frame_picks[0], near_frames, far_frames, hop(far_frames[:2], 1)]
    cot_parts = spread_out([after(part, *frame_parts) for part in cot_picks])

    rows = length + length // 2
    normed, stats, mixed = pl.pallas_call(
        attention_forward,
        out_shape=(
            shape((space, width), F32),
            shape((space, 128), F32),
            shape((space, width), BF16),
        ),
        in_specs=[smem] + [vmem] * 7,
        out_specs=[anywhere] * 3,
        scratch_shapes=[
            pltpu.VMEM((2, padded, width), BF16),
            pltpu.VMEM((2, padded, 2 * width), BF16),
            pltpu.VMEM((2, 2, length, width), BF16),
            pltpu.VMEM((2, length, width), F32),
            pltpu.VMEM((2, length, 128), F32),
            pltpu.VMEM((2, length, width), BF16),
            pltpu.SemaphoreType.DMA((2, 3, length // BLOCK)),
        ],
        compiler_params=params(),
        cost_estimate=cost(1e6, 1e5),
        name="attention_forward",
    )(after(lengths, near_pack), *near(*frame_parts), w_qkv, w_out, b_out)

    last = [after(part, normed, *cot_parts) for part in last]
    far_pack = jnp.concatenate([far0, far1, far2] + last)
    far_near_pack = hop(far_pack, 1)
    packs = (pack, near_pack, far_pack, far_near_pack)

    chunk_rows = (depth + width) // 2
    block_count = limit // BLOCK
    result = pl.pallas_call(
        feed_forward,
        out_shape=[shape((n, quarter, width), BF16) for n in (2, 2, 4)]
        + [shape((2, 4, chunk_rows // 2, width), BF16)] * 2
        + [
            shape((limit, filters), BF16),
            shape((limit, width), F32),
            shape((depth, filters), BF16),
            shape((8, width), F32),
            shape((8, filters), F32),
        ],
        in_specs=[smem, anywhere] + [vmem] * 4 + [anywhere] * 4 + [vmem] * 5,
        out_specs=[vmem] * 3 + [anywhere] * 5 + [vmem] * 2,
        scratch_shapes=[
            pltpu.VMEM((pack_rows, filters), BF16),
            pltpu.VMEM((limit, width), F32),
            pltpu.VMEM((limit + 2 * HALO, width), F32),
            pltpu.VMEM((limit, depth), BF16),
            pltpu.VMEM((2, BLOCK, filters), F32),
            pltpu.VMEM((BLOCK, filters), F32),
            pltpu.VMEM((limit, filters), BF16),
            pltpu.VMEM((limit, width), BF16),
            pltpu.VMEM((limit, filters), BF16),
            pltpu.VMEM((limit, width), F32),
            pltpu.VMEM((4, depth + width, width), BF16),
            pltpu.VMEM((2, padded, width), BF16),
            pltpu.VMEM((space, width), BF16),
            pltpu.VMEM((space, width), BF16),
            pltpu.VMEM((padded, width), BF16),
            pltpu.SemaphoreType.DMA((FILTER_COPIES,)),
            pltpu.SemaphoreType.DMA((block_count,)),
            pltpu.SemaphoreType.DMA((2, block_count)),
            pltpu.SemaphoreType.DMA((taps + 1, 4, width // (chunk_rows // 10))),
            pltpu.SemaphoreType.DMA((1,)),
        ],
        compiler_params=pltpu.CompilerParams(vmem_limit_bytes=50 * 2**20),
        cost_estimate=cost(1e6, 1e5),
        name="feed_forward",
    )(lengths, normed, *near(*cot_parts, *packs), gain_one, shift_one, b_proj, gain_two, shift_two)
    (out_own, out_near, out_far), kept, sent = result[:3], result[3], result[4]
    d_hidden, dz_two, conv, small_two, conv_bias = result[5:]

    def add(a, b):
        return (a.astype(F32) + b.astype(F32)).astype(BF16)

    def total(*parts):
        return sum(part.astype(F32) for part in parts).astype(BF16)

    def halves(value, step):
        half = value.shape[-2] // 2
        bit = (dp_place // step) % 2
        axis = value.ndim - 2
        parts = value.reshape(value.shape[:-2] + (2, half, width))
        keep = lax.dynamic_index_in_dim(parts, bit, axis, keepdims=False)
        send = lax.dynamic_index_in_dim(parts, 1 - bit, axis, keepdims=False)
        return keep, dp_hop(send, step)

    def joined(value, other, step):
        bit = (dp_place // step) % 2
        return jnp.where(bit == 0, jnp.concatenate([value, other]), jnp.concatenate([other, value]))

    def collected(places, parts, dtype, name):
        return pl.pallas_call(
            functools.partial(collect, places),
            out_shape=shape((count, quarter, width), dtype),
            in_specs=[smem] + [vmem] * len(parts),
            out_specs=vmem,
            compiler_params=params(),
            name=name,
        )(lengths, *near(*parts))

    more = [2**i for i in range(2, 20) if 2**i < dp_size]
    got = hop(sent, 1)
    out_far = hop(out_far, 2)
    out_near = hop(out_near, 1)

    d_first = pl.pallas_call(
        conv_backward,
        out_shape=shape((limit, width), F32),
        in_specs=[smem] + [anywhere] * 3,
        out_specs=anywhere,
        scratch_shapes=[
            pltpu.VMEM((depth, filters), BF16),
            pltpu.VMEM((limit, filters), BF16),
            pltpu.VMEM((limit, width), F32),
            pltpu.VMEM((limit, width), F32),
            pltpu.VMEM((limit + HALO, width), F32),
            pltpu.SemaphoreType.DMA((taps,)),
            pltpu.SemaphoreType.DMA((2, block_count)),
            pltpu.SemaphoreType.DMA((1, block_count)),
        ],
        compiler_params=params(),
        cost_estimate=cost(1e6, 1e5),
        name="conv_backward",
    )(lengths, d_hidden, conv, dz_two)

    def attention_back(part, arrays, inputs, ties):
        late_rows = width + SMALL_ROWS
        if part:
            out_shapes = [shape((late_rows, width), BF16)] * 4
            out_specs = [vmem] * 4
            more_scratch = [pltpu.VMEM((4, width, width), BF16)]
        else:
            out_shapes = [
                shape((width, 3 * width), F32),
                shape((space, width), F32),
                shape((space, width), BF16),
                shape((space, 128), F32),
                shape((width, width), F32),
                shape((8, width), F32),
            ]
            out_specs = [vmem] + [anywhere] * 3 + [vmem] * 2
            more_scratch = [
                pltpu.VMEM((limit, width), F32),
                pltpu.VMEM((limit, width), F32),
                pltpu.VMEM((limit, 128), F32),
                pltpu.VMEM((limit, width), BF16),
                pltpu.SemaphoreType.DMA((3, block_count)),
            ]
        held = length if part else limit
        return pl.pallas_call(
            functools.partial(attention_backward, part),
            out_shape=[shape((quarter, width), BF16)] * 2 + [shape((2, quarter, width), BF16)] + out_shapes,
            in_specs=[smem] + [anywhere] * 4 + [vmem] + [anywhere] * len(arrays) + [vmem] * len(inputs),
            out_specs=[vmem] * 3 + out_specs,
            scratch_shapes=[
                pltpu.VMEM((padded, width), BF16),
                pltpu.VMEM((padded, 3 * width), BF16),
                pltpu.VMEM((padded, 3 * width), BF16),
                pltpu.VMEM((length, width), F32),
                pltpu.VMEM((length, width), F32),
                pltpu.VMEM((padded, width), F32),
                pltpu.VMEM((held, width), F32),
                pltpu.VMEM((held, width), BF16),
                pltpu.VMEM((held, 128), F32),
                pltpu.SemaphoreType.DMA((4,)),
                pltpu.SemaphoreType.DMA((4, block_count)),
            ]
            + more_scratch,
            compiler_params=params(),
            cost_estimate=cost(1e6, 1e5),
            name=f"attention_backward_{'ac'[part]}",
        )(after(lengths, *ties), *frame_parts, w_qkv, *arrays, *inputs)

    got, out_far, out_near = lax.optimization_barrier((got, out_far, out_near, d_first))[:3]
    send_x, send_y = total(kept[1, :2], got[1, :2]), total(kept[1, 2:], got[1, 2:])
    got_x, got_y = dp_hop(send_x, 1), hop(send_y, 2)
    out_beyond = hop(out_far[2:], 1)
    a_own, a_near, a_far, grad_qkv, dz_one, d_mixed, soft, grad_out, small = attention_back(
        0, [d_first, normed, stats, mixed], [w_out, gain_one, small_two], [send_x, send_y]
    )
    got_x, got_y, out_beyond = lax.optimization_barrier((got_x, got_y, out_beyond, grad_qkv))[:3]
    send_x, send_y = total(kept[0, 1], got[0, 1], got_x[1]), total(kept[0, 3], got[0, 3], got_y[1])
    next_x, next_y = hop(send_x, 2), dp_hop(send_y, 2)
    a_far = hop(a_far, 2)
    c_own, c_near, c_far, late0, late1, late2, late3 = attention_back(
        1, [dz_one, d_mixed, soft], [grad_qkv, grad_out, small, conv_bias], [send_x, send_y]
    )
    next_x, next_y = lax.optimization_barrier((next_x, next_y, late0))[:2]
    state = [total(kept[0, 0], got[0, 0], got_x[0], next_x), total(kept[0, 2], got[0, 2], got_y[0], next_y)]

    late_parts = [hop(after(part, *state), d) for d, part in ((1, late1), (2, late2), (3, late3))]
    moving = [halves(state[0], 2), halves(state[1], 1)]
    late = total(late0, *late_parts)
    state = jnp.concatenate([add(keep, after(other, late)) for keep, other in moving])
    c_far = hop(after(c_far, late), 2)
    others = [dp_hop(state, step) for step in more[:1]]
    late_parts = [dp_hop(late, step) for step in (1, 2, 3)]
    output = collected(
        [((0, 0), (0, 1)), ((1, 0), (1, 1)), ((2, 0), (2, 1)), ((3, 0), (3, 1))],
        [after(out_own, late), out_near, out_far, out_beyond],
        BF16,
        "collect_output",
    )
    *others, p1, p2, p3, output, c_far = lax.optimization_barrier((*others, *late_parts, output, c_far))
    late = total(late, p1, p2, p3)
    for other in others:
        state = add(state, other)
    for step in more[1:]:
        state = add(state, dp_hop(state, step))
    state = jnp.split(state, 2)
    backs = [[2, 1], [1, 2]]
    others = [dp_hop(value, back[0]) for value, back in zip(state, backs)]
    near_grads = hop(after(jnp.stack([a_near, c_near, a_far[1], c_far[1]]), late), 1)
    for step in more:
        late = add(late, dp_hop(late, step))
    *others, late, near_grads = lax.optimization_barrier((*others, late, near_grads))
    state = [joined(value, other, back[0]) for value, other, back in zip(state, others, backs)]
    last = [back[-1] for back in backs]
    others = [dp_hop(value, step) for value, step in zip(state, last)]
    blocks = [hop(late[:width], d) for d in (1, 2, 3)]
    d_frames = collected(
        [((0, None), (1, None)), ((2, 0), (2, 1)), ((3, 0), (4, 0)), ((2, 2), (2, 3))],
        [a_own, c_own, near_grads, a_far, c_far],
        F32,
        "collect_grad",
    )
    grad_conv, grad_proj = pl.pallas_call(
        functools.partial(finish_filters, last),
        out_shape=(shape((depth, width), F32), shape((width, width), F32)),
        in_specs=[vmem] * 4,
        out_specs=[vmem] * 2,
        scratch_shapes=[pltpu.VMEM((depth + width, width), BF16)],
        compiler_params=params(),
        name="finish_filters",
    )(*near(*[part for pair in zip(state, others) for part in pair]))
    grad_qkv, grad_out, *vectors = pl.pallas_call(
        finish_late,
        out_shape=[shape((width, 3 * width), F32), shape((width, width), F32)] + [shape((1, width), F32)] * 7,
        in_specs=[vmem] * 4,
        out_specs=[vmem] * 9,
        scratch_shapes=[pltpu.VMEM((4, width, width), F32)],
        compiler_params=params(),
        name="finish_late",
    )(*near(late, *blocks))
    vectors = [v.reshape(width) for v in vectors]
    return (
        output,
        d_frames,
        grad_qkv,
        grad_out,
        vectors[0],
        vectors[1],
        vectors[2],
        grad_conv.reshape(w_conv.shape),
        vectors[6],
        grad_proj,
        vectors[3],
        vectors[4],
        vectors[5],
    )


def solution(mesh):
    return jax.shard_map(
        shards,
        mesh=mesh,
        in_specs=(
            P("dp", "tensor", None),
            P("dp"),
            P(),
            P(),
            P(),
            P(),
            P(),
            P(None, None, "tensor"),
            P("tensor"),
            P("tensor", None),
            P(),
            P(),
            P(),
            P("dp", "tensor", None),
        ),
        out_specs=(
            P("dp", "tensor", None),
            P("dp", "tensor", None),
            P(),
            P(),
            P(),
            P(),
            P(),
            P(None, None, "tensor"),
            P("tensor"),
            P("tensor", None),
            P(),
            P(),
            P(),
        ),
        check_vma=False,
    )
```

```python
import functools
import itertools

import jax
import jax.experimental.pallas as pl
import jax.experimental.pallas.tpu as pltpu
import jax.numpy as jnp
import numpy as np
from jax import lax
from jax.sharding import PartitionSpec as P


EPSILON = 1e-05
F32 = jnp.float32
BF16 = jnp.bfloat16
HALO = 16
BLOCK = 256
MASKED = -1e30
GELU_A = float(np.sqrt(2.0 / np.pi))
GELU_B = 0.044715
LOG2E = float(np.log2(np.e))
VMEM_LIMIT = 54 * 2**20
SMALL_ROWS = 16


def near(*arrays):
    return [pltpu.with_memory_space_constraint(array, pltpu.VMEM) for array in arrays]


def params(**more):
    return pltpu.CompilerParams(vmem_limit_bytes=VMEM_LIMIT, **more)


def cost(flops, size):
    return pl.CostEstimate(flops=int(flops), bytes_accessed=int(size), transcendentals=0)


def dot(a, b):
    return jnp.dot(a, b, preferred_element_type=F32)


def dot_nt(a, b):
    return lax.dot_general(a, b, (((1,), (1,)), ((), ())), preferred_element_type=F32)


def dot_tn(a, b):
    return lax.dot_general(a, b, (((0,), (0,)), ((), ())), preferred_element_type=F32)


def at(start, size, step=HALO):
    return pl.ds(pl.multiple_of(start, step), size)


def up(value, step=HALO):
    return ((value + (step - 1)) // step) * step


def choose(index, options):
    result = options[-1]
    for i, option in enumerate(options[:-1]):
        result = jnp.where(index == i, option, result)
    return result


def plan(lengths):
    keys = [lengths[i] * 8 + i for i in range(6)]
    best, triples = None, None
    for pair in itertools.combinations(range(1, 6), 2):
        mine = (0,) + pair
        rest = tuple(i for i in range(6) if i not in mine)
        gap = jnp.abs(sum(lengths[i] for i in mine) - sum(lengths[i] for i in rest))
        option = [keys[i] for i in mine + rest]
        if best is None:
            best, triples = gap, option
        else:
            better = gap < best
            best = jnp.where(better, gap, best)
            triples = [jnp.where(better, new, old) for new, old in zip(option, triples)]
    whole, shared = [], []
    for a, b, c in (triples[:3], triples[3:]):
        a, b = jnp.maximum(a, b), jnp.minimum(a, b)
        a, c = jnp.maximum(a, c), jnp.minimum(a, c)
        b, c = jnp.maximum(b, c), jnp.minimum(b, c)
        whole += [a, b]
        shared.append(c)
    return whole, shared


class Rows:
    def __init__(self, lengths, length):
        self.member = lax.axis_index("tensor")
        whole, shared = plan(lengths)
        self.whole, self.shared = whole, shared
        role = self.member % 2
        second = self.member >= 2
        key_a = choose(self.member, whole)
        self.len_a = key_a // 8
        self.len_c = jnp.where(second, shared[1], shared[0]) // 8
        first_len = jnp.where(second, whole[2], whole[0]) // 8
        other_len = jnp.where(second, whole[3], whole[1]) // 8
        split = (other_len + self.len_c - first_len) // 2
        split = jnp.maximum((split + HALO // 2) // HALO * HALO, HALO)
        starts = role == 0
        self.own_from = jnp.where(starts, 0, split)
        self.own_to = jnp.where(starts, split, length)
        self.window = jnp.where(starts, 0, split - HALO)
        self.end = jnp.where(starts, jnp.minimum(split + HALO, self.len_c), self.len_c)
        self.rows_a = up(self.len_a) + HALO
        self.rows_c = jnp.maximum(up(self.end) - self.window, 0)
        self.tiles_a = (self.len_a + BLOCK - 1) // BLOCK
        self.tiles_c = (self.rows_c + BLOCK - 1) // BLOCK
        self.blocks = (self.rows_a + self.rows_c + BLOCK - 1) // BLOCK
        self.halo = self.rows_a + jnp.where(starts, split, 0)

    def masks(self, start, size):
        row = start + lax.broadcasted_iota(jnp.int32, (size, 1), 0)
        in_a = row < self.rows_a
        frame = jnp.where(in_a, row, row - self.rows_a + self.window)
        live = frame < jnp.where(in_a, self.len_a, self.end)
        inside = (frame >= self.own_from) & (frame < self.own_to)
        return live, live & (in_a | inside)

    def frames_at(self, part, index):
        return at(BLOCK * index + (self.window if part else 0), BLOCK)

    def base(self, part, index):
        return BLOCK * index + (self.rows_a if part else 0)


def piece_index(piece, part):
    return part if piece.shape[0] == 2 else 2 - part


def place(member, pieces, target):
    quarter = pieces[0].shape[1]
    for distance, piece in enumerate(pieces):
        rows = at((member ^ distance) * quarter, quarter, quarter)
        for part in range(2):
            target[part, rows, :] = piece[piece_index(piece, part)]


def pick(lengths, source, *targets):
    member = lax.axis_index("tensor")
    whole, shared = plan(lengths)
    for distance, target in enumerate(targets):
        there = member ^ distance
        if target.shape[0] == 3:
            target[0] = source[choose(there ^ 1, whole) % 8]
        target[piece_index(target, 0)] = source[choose(there, whole) % 8]
        target[piece_index(target, 1)] = source[jnp.where(there >= 2, shared[1], shared[0]) % 8]


def begin_group(lengths, source, w_conv, w_proj, b_conv, pack, p0, p1, p2, part):
    depth, width = w_conv.shape
    pack[0:depth, :] = w_conv[...]
    pack[depth : depth + width, :] = w_proj[...]
    high = b_conv[...].astype(BF16)
    rest = (b_conv[...] - high.astype(F32)).astype(BF16)
    last = depth + width
    pack[last : last + HALO, :] = jnp.broadcast_to(high, (HALO, width))
    pack[last + HALO :, :] = jnp.broadcast_to(rest, (pack.shape[0] - last - HALO, width))
    piece = part.shape[0]
    part[...] = pack[at((lax.axis_index("dp") % 4) * piece, piece), :]
    pick(lengths, source, p0, p1, p2)


def softmax_parts(rows, part, length):
    return (rows.len_c if part else rows.len_a), lax.broadcasted_iota(jnp.int32, (1, length), 1)


def mask_keys(scores, column, limit):
    half = scores.shape[1] // 2
    tail = jnp.where(column[:, half:] < limit, scores[:, half:], MASKED)
    return jnp.concatenate([scores[:, :half], tail], axis=1)


def attention_forward(
    lengths, r0, r1, r2, r3, w_qkv, w_out, b_out, normed, stats, mixed, placed, qkv, valued, n_out, s_out, m_out, sems
):
    quarter = r0.shape[1]
    length = 4 * quarter
    width = r0.shape[2]
    head = width // 2
    scale = head ** (-0.5) * LOG2E
    rows = Rows(lengths, length)
    spare = placed.shape[1] - length
    placed[:, length:, :] = jnp.zeros((2, spare, width), BF16)
    place(rows.member, (r0, r1, r2, r3), placed)
    for part in range(2):
        for h in range(2):
            valued[part, h, :, head:] = jnp.ones((length, head), BF16)

    def project(index, carry):
        here = at(index * BLOCK, BLOCK, BLOCK)
        for part in range(2):
            value = dot(placed[part, here, :], w_qkv[...]).astype(BF16)
            qkv[part, here, :] = value[:, : 2 * width]
            for h in range(2):
                valued[part, h, here, :head] = value[:, 2 * width + h * head : 2 * width + (h + 1) * head]
        return carry

    lax.fori_loop(0, length // BLOCK, project, 0)
    qkv[:, length:, :] = jnp.zeros((2, spare, 2 * width), BF16)
    lane = lax.broadcasted_iota(jnp.int32, (1, 128), 1)

    def copies(part, index):
        there = at(rows.base(part, index), BLOCK)
        here = at(index * BLOCK, BLOCK, BLOCK)
        pairs = ((n_out, normed), (s_out, stats), (m_out, mixed))
        return [
            pltpu.make_async_copy(source.at[part, here], target.at[there], sems.at[part, i, index])
            for i, (source, target) in enumerate(pairs)
        ]

    def tile(part, index, carry):
        frames_at = rows.frames_at(part, index)
        here = at(index * BLOCK, BLOCK, BLOCK)
        limit, column = softmax_parts(rows, part, length)
        mixtures, logs = [], []
        for h in range(2):
            low, high = h * head, (h + 1) * head
            scores = dot_nt(qkv[part, frames_at, low:high], qkv[part, :length, width + low : width + high])
            scores = mask_keys(scores, column, limit)
            highest = jnp.max(scores, axis=-1, keepdims=True) * scale
            exponent = jnp.exp2(scores * scale - highest).astype(BF16)
            summed = dot(exponent, valued[part, h])
            total = summed[:, head : head + 1]
            mixtures.append((summed[:, :head] / total).astype(BF16))
            logs.append(highest + jnp.log2(total))
        mixture = jnp.concatenate(mixtures, axis=1)
        m_out[part, here, :] = mixture
        residual = placed[part, frames_at, :].astype(F32) + dot(mixture, w_out[...]) + b_out[...]
        centred = residual - jnp.mean(residual, axis=-1, keepdims=True)
        inverse = lax.rsqrt(jnp.mean(centred * centred, axis=-1, keepdims=True) + EPSILON)
        n_out[part, here, :] = centred * inverse
        s_out[part, here, :] = jnp.where(lane == 0, logs[0], jnp.where(lane == 1, logs[1], inverse))
        for copy in copies(part, index):
            copy.start()
        return carry

    def finish(part, index, carry):
        for copy in copies(part, index):
            copy.wait()
        return carry

    for part, count in enumerate((rows.tiles_a, rows.tiles_c)):
        lax.fori_loop(0, count, functools.partial(tile, part), 0)
        lax.fori_loop(0, count, functools.partial(finish, part), 0)


def gelu_pair(x):
    square = x * x
    t = jnp.tanh(GELU_A * x * (1.0 + GELU_B * square))
    half = 0.5 * (1.0 + t)
    slope = half + (0.5 * GELU_A) * x * (1.0 - t * t) * (1.0 + 3.0 * GELU_B * square)
    return x * half, slope


def load_filters(near, far, target, sems):
    width = near[0].shape[1]
    piece = near[0].shape[0] // 4
    shift = lax.axis_index("dp") % 4
    copies = []
    for j, source in enumerate(near):
        copies.append((source, target.at[:, pl.ds(j * width, width)]))
    for j, source in enumerate(far):
        for i in range(4):
            there = at((shift ^ i) * piece, piece)
            part = pl.ds((2 + j) * width, width)
            copies.append((source.at[pl.ds(i * piece, piece)], target.at[there, part]))
    copies = [
        pltpu.make_async_copy(source, there, sems.at[i]) for i, (source, there) in enumerate(copies)
    ]
    for copy in copies:
        copy.start()
    return copies


FILTER_COPIES = 10


def feed_forward(
    lengths,
    normed,
    c0,
    c1,
    c2,
    c3,
    pack0,
    pack1,
    far0,
    far1,
    gain_one,
    shift_one,
    b_proj,
    gain_two,
    shift_two,
    o0,
    o1,
    o_far,
    kept,
    sent,
    d_hidden_out,
    dz_out,
    conv_out,
    small,
    conv_bias,
    weights,
    units,
    first,
    columns,
    hidden,
    slope,
    active,
    d_branch,
    d_hidden,
    dz_two,
    grads,
    cot_frames,
    cot_rows,
    out_rows,
    out_c,
    load_sems,
    unit_sems,
    out_sems,
    grad_sems,
    conv_sem,
):
    quarter, width = c0.shape[1:]
    length = 4 * quarter
    filters = weights.shape[1]
    taps = columns.shape[1] // width
    depth = taps * width
    reach = taps // 2
    loads = load_filters((pack0, pack1), (far0, far1), weights, load_sems)
    rows = Rows(lengths, length)
    blocks = rows.blocks

    def unit_copy(index):
        here = at(index * BLOCK, BLOCK, BLOCK)
        return pltpu.make_async_copy(normed.at[here], units.at[here], unit_sems.at[index])

    def start_unit(index, carry):
        unit_copy(index).start()
        return carry

    lax.fori_loop(0, blocks, start_unit, 0)
    place(rows.member, (c0, c1, c2, c3), cot_frames)
    cot_frames[:, length:, :] = jnp.zeros((2, cot_frames.shape[1] - length, width), BF16)
    cot_rows[0:length, :] = cot_frames[0, 0:length, :]

    def gather_cot(index, carry):
        cot_rows[at(rows.base(1, index), BLOCK), :] = cot_frames[1, rows.frames_at(1, index), :]
        return carry

    lax.fori_loop(0, rows.tiles_c, gather_cot, 0)
    out_rows[...] = jnp.zeros(out_rows.shape, BF16)
    small[...] = jnp.zeros(small.shape, F32)
    conv_bias[...] = jnp.zeros(conv_bias.shape, F32)

    first[0:HALO, :] = jnp.zeros((HALO, width), F32)

    def make_first(index, carry):
        base = index * BLOCK
        unit_copy(index).wait()
        live, _ = rows.masks(base, BLOCK)
        value = units[at(base, BLOCK), :] * gain_one[...] + shift_one[...]
        first[at(base + HALO, BLOCK), :] = jnp.where(live, value, 0.0)
        return carry

    lax.fori_loop(0, blocks, make_first, 0)
    first[at(blocks * BLOCK + HALO, HALO), :] = jnp.zeros((HALO, width), F32)

    def make_columns(index, carry):
        base = index * BLOCK
        around = first[at(base + HALO - 8, BLOCK + 16, 8), :]
        for k in range(taps):
            columns[at(base, BLOCK, BLOCK), k * width : (k + 1) * width] = around[
                8 - reach + k : 8 - reach + k + BLOCK
            ].astype(BF16)
        return carry

    lax.fori_loop(0, blocks, make_columns, 0)
    for copy in loads:
        copy.wait()
    conv_copy = pltpu.make_async_copy(weights.at[pl.ds(0, depth)], conv_out, conv_sem.at[0])
    conv_copy.start()

    def out_copies(index):
        here = at(index * BLOCK, BLOCK, BLOCK)
        return [
            pltpu.make_async_copy(d_hidden.at[here], d_hidden_out.at[here], out_sems.at[0, index]),
            pltpu.make_async_copy(dz_two.at[here], dz_out.at[here], out_sems.at[1, index]),
        ]

    def conv(index, target):
        target[...] = dot(columns[at(index * BLOCK, BLOCK, BLOCK), :], weights[0:depth, :])

    def rest(index, source):
        base = index * BLOCK
        here = at(base, BLOCK, BLOCK)
        live, own = rows.masks(base, BLOCK)
        branch = jnp.zeros((BLOCK, width), F32)
        for j in range(filters // width):
            part = slice(j * width, (j + 1) * width)
            bias = weights[depth + width : depth + width + 1, part].astype(F32) + weights[
                depth + width + 16 : depth + width + 17, part
            ].astype(F32)
            value, derivative = gelu_pair(source[:, part] + bias)
            value = value.astype(BF16)
            active[here, part] = value
            slope[:, part] = derivative
            branch = branch + dot(value, weights[depth : depth + width, part])
        residual = first[at(base + HALO, BLOCK), :] + branch + b_proj[...]
        centred = residual - jnp.mean(residual, axis=-1, keepdims=True)
        inverse = lax.rsqrt(jnp.mean(centred * centred, axis=-1, keepdims=True) + EPSILON)
        normed_two = centred * inverse
        out_rows[here, :] = jnp.where(own, normed_two * gain_two[...] + shift_two[...], 0.0).astype(BF16)
        upstream = jnp.where(live, cot_rows[here, :].astype(F32), 0.0)
        counted = jnp.where(own, upstream, 0.0)
        scaled = upstream * gain_two[...]
        dz = inverse * (
            scaled
            - jnp.mean(scaled, axis=-1, keepdims=True)
            - normed_two * jnp.mean(scaled * normed_two, axis=-1, keepdims=True)
        )
        dz_two[here, :] = dz
        small[3:4, :] += jnp.sum(jnp.where(own, dz, 0.0), axis=0, keepdims=True)
        small[4:5, :] += jnp.sum(counted * normed_two, axis=0, keepdims=True)
        small[5:6, :] += jnp.sum(counted, axis=0, keepdims=True)
        low = dz.astype(BF16)
        d_branch[here, :] = jnp.where(own, low, jnp.zeros_like(low))
        for j in range(filters // width):
            part = slice(j * width, (j + 1) * width)
            grad = dot_nt(low, weights[depth : depth + width, part]) * slope[:, part]
            conv_bias[0:1, part] += jnp.sum(jnp.where(own, grad, 0.0), axis=0, keepdims=True)
            d_hidden[here, part] = grad.astype(BF16)
        for copy in out_copies(index):
            copy.start()

    even, odd = hidden.at[0], hidden.at[1]
    conv(0, even)

    def step(pair, carry):
        index = 2 * pair
        conv(index + 1, odd)
        rest(index, even)
        conv(index + 2, even)
        rest(index + 1, odd)
        return carry

    lax.fori_loop(0, (blocks - 1) // 2, step, 0)

    @pl.when(blocks % 2 == 1)
    def _():
        rest(blocks - 1, even)

    @pl.when(blocks % 2 == 0)
    def _():
        conv(blocks - 1, odd)
        rest(blocks - 2, even)
        rest(blocks - 1, odd)

    columns[at(rows.halo, HALO), :] = jnp.zeros((HALO, columns.shape[1]), BF16)

    per_chunk = (taps + 1) // 2

    x_bit, z_bit = lax.axis_index("dp") % 2, (lax.axis_index("dp") // 2) % 2
    half_rows = kept.shape[2]
    piece = half_rows // 5

    def grad_copies(k, chunk):
        copies = []
        for u in range(width // piece):
            row = (k - chunk * per_chunk) * width + u * piece
            half = row // half_rows
            there = at(row - half * half_rows, piece, piece)
            here = at(k * width + u * piece, piece, piece)
            for j in range(filters // width):
                place = (half ^ x_bit, j // 2) if chunk == 0 else (j // 2, 2 + (half ^ z_bit))
                target = (kept, sent)[j % 2].at[place[0], place[1], there]
                copies.append(pltpu.make_async_copy(grads.at[j, here], target, grad_sems.at[k, j, u]))
        return copies

    for count in range(4, active.shape[0] // BLOCK + 1):

        @pl.when(blocks == count)
        def _():
            n = count * BLOCK

            def tap(k, carry):
                here = at(k * width, width, width)
                value = dot_tn(columns[0:n, here], d_hidden[0:n, :]).astype(BF16)
                for j in range(filters // width):
                    grads[j, here, :] = value[:, j * width : (j + 1) * width]
                for chunk in range(2):

                    @pl.when(k // per_chunk == chunk)
                    def _():
                        for copy in grad_copies(k, chunk):
                            copy.start()

                return carry

            lax.fori_loop(0, taps, tap, 0)
            value = dot_tn(active[0:n, :], d_branch[0:n, :]).astype(BF16)
            for j in range(filters // width):
                grads[j, depth:, :] = value[j * width : (j + 1) * width, :]
            for copy in grad_copies(taps, 1):
                copy.start()

    out_c[...] = jnp.zeros(out_c.shape, BF16)

    def scatter_out(index, carry):
        out_c[rows.frames_at(1, index), :] = out_rows[at(rows.base(1, index), BLOCK), :]
        return carry

    lax.fori_loop(0, rows.tiles_c, scatter_out, 0)
    for distance, (target, slot) in enumerate(((o0, 0), (o1, 0), (o_far, 0), (o_far, 2))):
        start = (rows.member ^ distance) * quarter
        there = at(start, quarter, quarter)
        row = start + lax.broadcasted_iota(jnp.int32, (quarter, 1), 0)
        value = out_rows[there, :]
        target[slot] = jnp.where(row < rows.len_a, value, jnp.zeros_like(value))
        target[slot + 1] = out_c[there, :]

    conv_copy.wait()

    def finish(index, carry):
        for copy in out_copies(index):
            copy.wait()
        return carry

    lax.fori_loop(0, blocks, finish, 0)

    def finish_grads(chunk, k, carry):
        for copy in grad_copies(k, chunk):
            copy.wait()
        return carry

    lax.fori_loop(0, per_chunk, functools.partial(finish_grads, 0), 0)
    lax.fori_loop(per_chunk, 2 * per_chunk, functools.partial(finish_grads, 1), 0)


def block_copies(pairs, sems, index):
    here = at(index * BLOCK, BLOCK, BLOCK)
    return [
        pltpu.make_async_copy(source.at[here], target.at[here], sems.at[i, index])
        for i, (source, target) in enumerate(pairs)
    ]


def conv_backward(
    lengths, d_hidden_in, conv, dz_in, d_first_out, weights, d_hidden, dz_two, d_first, sums, conv_sems, in_sems, out_sems
):
    width = dz_two.shape[1]
    taps = conv.shape[0] // width
    reach = taps // 2
    blocks = Rows(lengths, 4 * width).blocks
    conv_copies = [
        pltpu.make_async_copy(
            conv.at[pl.ds(k * width, width)], weights.at[pl.ds(k * width, width)], conv_sems.at[k]
        )
        for k in range(taps)
    ]
    into = ((d_hidden_in, d_hidden), (dz_in, dz_two))
    onto = ((d_first, d_first_out),)
    for copy in conv_copies:
        copy.start()

    def start(index, carry):
        for copy in block_copies(into, in_sems, index):
            copy.start()
        return carry

    lax.fori_loop(0, blocks, start, 0)
    sums[0:HALO, :] = jnp.zeros((HALO, width), F32)
    for copy in conv_copies:
        copy.wait()

    def back(index, carry):
        base = index * BLOCK
        for copy in block_copies(into, in_sems, index):
            copy.wait()
        value = d_hidden[at(base, BLOCK, BLOCK), :]
        total = jnp.zeros((BLOCK + HALO, width), F32)
        for k in range(taps):
            part = dot_nt(value, weights[k * width : (k + 1) * width, :])
            part = jnp.concatenate([part, jnp.zeros((HALO, width), F32)], axis=0)
            total = total + pltpu.roll(part, 8 - reach + k, axis=0)
        sums[at(base, HALO), :] += total[0:HALO]
        sums[at(base + HALO, BLOCK), :] = total[HALO:]
        return carry

    lax.fori_loop(0, blocks, back, 0)

    def finish(index, carry):
        base = index * BLOCK
        here = at(base, BLOCK, BLOCK)
        d_first[here, :] = dz_two[here, :] + sums[at(base + 8, BLOCK, 8), :]
        block_copies(onto, out_sems, index)[0].start()
        return carry

    lax.fori_loop(0, blocks, finish, 0)

    def drain(index, carry):
        block_copies(onto, out_sems, index)[0].wait()
        return carry

    lax.fori_loop(0, blocks, drain, 0)


def first_norm_backward(rows, ins, outs, blocks_in, blocks_out, in_sems, out_sems, w_out, gain_one, small, grad_out):
    d_first, normed, stats, mixed = blocks_in
    dz_one, d_mixed, soft = blocks_out
    into, onto = tuple(zip(ins, blocks_in)), tuple(zip(blocks_out, outs))
    width = normed.shape[1]
    head = width // 2
    lane = lax.broadcasted_iota(jnp.int32, (1, 128), 1)

    def block(index, carry):
        base = index * BLOCK
        here = at(base, BLOCK, BLOCK)
        for copy in block_copies(into, in_sems, index):
            copy.wait()
        _, own = rows.masks(base, BLOCK)
        total = jnp.where(own, d_first[here, :], 0.0)
        unit = jnp.where(own, normed[here, :], 0.0)
        kept = stats[here, :]
        inverse = kept[:, 2:3]
        scaled = total * gain_one[...]
        dz = inverse * (
            scaled
            - jnp.mean(scaled, axis=-1, keepdims=True)
            - unit * jnp.mean(scaled * unit, axis=-1, keepdims=True)
        )
        dz = jnp.where(own, dz, 0.0)
        dz_one[here, :] = dz
        small[0:1, :] += jnp.sum(dz, axis=0, keepdims=True)
        small[1:2, :] += jnp.sum(total * unit, axis=0, keepdims=True)
        small[2:3, :] += jnp.sum(total, axis=0, keepdims=True)
        low = dz.astype(BF16)
        upstream = dot_nt(low, w_out[...]).astype(BF16)
        d_mixed[here, :] = upstream
        mixture = mixed[here, :]
        mixture = jnp.where(own, mixture, jnp.zeros_like(mixture))
        grad_out[...] += dot_tn(mixture, low)
        product = upstream.astype(F32) * mixture.astype(F32)
        means = [jnp.sum(product[:, h * head : (h + 1) * head], axis=-1, keepdims=True) for h in range(2)]
        soft[here, :] = jnp.where(
            lane < 2, jnp.where(own, kept, -MASKED), jnp.where(lane == 2, means[0], means[1])
        )
        for copy in block_copies(onto, out_sems, index):
            copy.start()
        return carry

    lax.fori_loop(0, rows.blocks, block, 0)

    def finish(index, carry):
        for copy in block_copies(onto, out_sems, index):
            copy.wait()
        return carry

    return finish


def attention_backward(part, *refs):
    (lengths, r0, r1, r2, r3, w_qkv), refs = refs[:6], refs[6:]
    if part:
        in_refs, refs = refs[:3], refs[3:]
        inputs, refs = refs[:4], refs[4:]
        (g0, g1, g_far), refs = refs[:3], refs[3:]
        late, refs = refs[:4], refs[4:]
    else:
        in_refs, refs = refs[:4], refs[4:]
        (w_out, gain_one, small_two), refs = refs[:3], refs[3:]
        (g0, g1, g_far), refs = refs[:3], refs[3:]
        grad_qkv, refs = refs[0], refs[1:]
        out_refs, refs = refs[:3], refs[3:]
        (grad_out, small), refs = refs[:2], refs[2:]
    placed, qkv, d_proj, keys, values, frame_grads, dz_one, d_mixed, soft, place_sems, in_sems = refs[:11]
    quarter = r0.shape[1]
    length = 4 * quarter
    width = r0.shape[2]
    head = width // 2
    scale = head ** (-0.5)
    rows = Rows(lengths, length)
    tiles = rows.tiles_c if part else rows.tiles_a
    spare = placed.shape[0] - length
    places = [
        pltpu.make_async_copy(
            piece.at[piece_index(piece, part)],
            placed.at[at((rows.member ^ distance) * quarter, quarter, quarter)],
            place_sems.at[distance],
        )
        for distance, piece in enumerate((r0, r1, r2, r3))
    ]

    def copies(index):
        there = at(rows.base(part, index), BLOCK)
        here = at(index * BLOCK, BLOCK, BLOCK)
        return [
            pltpu.make_async_copy(source.at[there], target.at[here], in_sems.at[i, index])
            for i, (source, target) in enumerate(zip(in_refs, (dz_one, d_mixed, soft)))
        ]

    if part:

        def start(index, carry):
            for copy in copies(index):
                copy.start()
            return carry

        lax.fori_loop(0, tiles, start, 0)
    else:
        blocks_in, out_sems = refs[11:15], refs[15]

        def start(index, carry):
            for copy in block_copies(tuple(zip(in_refs, blocks_in)), in_sems, index):
                copy.start()
            return carry

        lax.fori_loop(0, rows.blocks, start, 0)
    for copy in places:
        copy.start()
    placed[length:, :] = jnp.zeros((spare, width), BF16)
    d_proj[...] = jnp.zeros(d_proj.shape, BF16)
    keys[...] = jnp.zeros(keys.shape, F32)
    values[...] = jnp.zeros(values.shape, F32)
    frame_grads[...] = jnp.zeros(frame_grads.shape, F32)
    if not part:
        small[...] = small_two[...]
        grad_out[...] = jnp.zeros(grad_out.shape, F32)
        finish = first_norm_backward(
            rows, in_refs, out_refs, blocks_in, (dz_one, d_mixed, soft), in_sems, out_sems, w_out, gain_one, small, grad_out
        )
    for copy in places:
        copy.wait()

    def project(index, carry):
        here = at(index * BLOCK, BLOCK, BLOCK)
        qkv[here, :] = dot(placed[here, :], w_qkv[...]).astype(BF16)
        return carry

    lax.fori_loop(0, length // BLOCK, project, 0)
    qkv[length:, :] = jnp.zeros((spare, 3 * width), BF16)

    def tile(index, carry):
        frames_at = rows.frames_at(part, index)
        here = at(index * BLOCK, BLOCK, BLOCK)
        if part:
            for copy in copies(index):
                copy.wait()
        limit, column = softmax_parts(rows, part, length)
        inside = BLOCK * index + lax.broadcasted_iota(jnp.int32, (BLOCK, 1), 0)
        inside = inside < (rows.rows_c if part else rows.rows_a)
        frame_grads[frames_at, :] = jnp.where(inside, dz_one[here, :], 0.0)
        for h in range(2):
            low, high = h * head, (h + 1) * head
            query = qkv[frames_at, low:high]
            key = qkv[:length, width + low : width + high]
            value = qkv[:length, 2 * width + low : 2 * width + high]
            upstream = d_mixed[here, low:high]
            upstream = jnp.where(inside, upstream, jnp.zeros_like(upstream))
            shift = jnp.where(inside, soft[here, h : h + 1], -MASKED)
            mean = jnp.where(inside, soft[here, 2 + h : 3 + h], 0.0)
            scores = mask_keys(dot_nt(query, key), column, limit)
            weights = jnp.exp2(scores * (scale * LOG2E) - shift)
            d_weights = dot_nt(upstream, value)
            d_scores = (weights * (d_weights - mean)).astype(BF16)
            d_proj[frames_at, low:high] = (dot(d_scores, key) * scale).astype(BF16)
            keys[:, low:high] += dot_tn(d_scores, query)
            values[:, low:high] += dot_tn(weights.astype(BF16), upstream)
        return carry

    lax.fori_loop(0, tiles, tile, 0)
    d_proj[0:length, width : 2 * width] = (keys[...] * scale).astype(BF16)
    d_proj[0:length, 2 * width : 3 * width] = values[...].astype(BF16)
    for distance, target in enumerate((g0, g1, g_far.at[0], g_far.at[1])):
        here = at((rows.member ^ distance) * quarter, quarter, quarter)
        target[...] = (frame_grads[here, :] + dot_nt(d_proj[here, :], w_qkv[...])).astype(BF16)
    grads = dot_tn(placed[0:length, :], d_proj[0:length, :])
    if part == 0:
        grad_qkv[...] = grads
        lax.fori_loop(0, rows.blocks, finish, 0)
        return
    blocks = refs[11]
    grad_before, grad_out, small, conv_bias = inputs
    grads = (grads + grad_before[...]).astype(BF16)
    for q in range(3):
        blocks[q, :, :] = grads[:, q * width : (q + 1) * width]
    blocks[3, :, :] = grad_out[...].astype(BF16)
    line = lax.broadcasted_iota(jnp.int32, (8, 1), 0)
    for j, target in enumerate(late):
        target[0:width, :] = blocks[rows.member ^ j]
        bias = conv_bias[0:1, j * width : (j + 1) * width]
        tail = jnp.where(line == 6, bias, small[...])
        tail = jnp.concatenate([tail, jnp.zeros((SMALL_ROWS - 8, width), F32)], axis=0)
        target[width : width + SMALL_ROWS, :] = tail.astype(BF16)


def collect(places, lengths, *refs):
    result = refs[-1]
    member = lax.axis_index("tensor")
    whole, shared = plan(lengths)

    def piece(place):
        array, index = place
        return refs[array][...] if index is None else refs[array][index]

    for distance in range(4):
        slot = choose(member ^ distance, whole) % 8
        result[slot] = piece(places[distance][0]).astype(result.dtype)
    for side in range(2):
        second = (member >= 2) == (side == 0)
        slot = jnp.where(second, shared[1], shared[0]) % 8
        total = piece(places[2 * side][1]).astype(F32) + piece(places[2 * side + 1][1]).astype(F32)
        result[slot] = total.astype(result.dtype)


def finish_late(own, p1, p2, p3, *refs):
    grad_qkv, grad_out = refs[:2]
    vectors, blocks = refs[2:-1], refs[-1]
    width = grad_out.shape[0]
    member = lax.axis_index("tensor")
    for distance, piece in enumerate((own, p1, p2, p3)):
        blocks[member ^ distance] = piece[0:width, :].astype(F32)
    for q in range(3):
        grad_qkv[:, q * width : (q + 1) * width] = blocks[q]
    grad_out[...] = blocks[3]
    tail = own[width : width + 16, :].astype(F32)
    for i, vector in enumerate(vectors):
        vector[...] = tail[i : i + 1, :]


def finish_filters(steps, *refs):
    parts, (grad_conv, grad_proj, work) = refs[:-3], refs[-3:]
    where = lax.axis_index("dp")
    depth = grad_conv.shape[0]
    start = 0
    for step, value, other in zip(steps, parts[::2], parts[1::2]):
        half = value.shape[0]
        bit = (where // step) % 2
        work[at(start + bit * half, half), :] = value[...]
        work[at(start + (1 - bit) * half, half), :] = other[...]
        start += 2 * half
    grad_conv[...] = work[0:depth, :].astype(F32)
    grad_proj[...] = work[depth:, :].astype(F32)


def shards(
    frames,
    lengths,
    w_qkv,
    w_out,
    b_out,
    gain_one,
    shift_one,
    w_conv,
    b_conv,
    w_proj,
    b_proj,
    gain_two,
    shift_two,
    cotangent,
):
    count, quarter, width = frames.shape
    length = 4 * quarter
    taps = w_conv.shape[0]
    depth = taps * width
    filters = 4 * w_conv.shape[2]
    padded = length + BLOCK
    space = 2 * length
    limit = 7 * BLOCK
    smem = pl.BlockSpec(memory_space=pltpu.SMEM)
    vmem = pl.BlockSpec(memory_space=pltpu.VMEM)
    anywhere = pl.BlockSpec(memory_space=pl.ANY)
    shape = jax.ShapeDtypeStruct
    dp_size = lax.axis_size("dp")
    dp_place = lax.axis_index("dp")
    b_out, gain_one, shift_one, b_proj, gain_two, shift_two = [
        v[None] for v in (b_out, gain_one, shift_one, b_proj, gain_two, shift_two)
    ]

    def hop(value, distance):
        return lax.ppermute(value, "tensor", [(i, i ^ distance) for i in range(4)])

    def dp_hop(value, distance):
        return lax.ppermute(value, "dp", [(i, i ^ distance) for i in range(dp_size)])

    def after(value, *others):
        return lax.optimization_barrier((value,) + others)[0]

    pack_rows = (depth + width + 64) // 64 * 64
    piece = pack_rows // 4
    pack, *frame_picks, own_piece = pl.pallas_call(
        begin_group,
        out_shape=[shape((pack_rows, width), BF16)]
        + [shape((n, quarter, width), BF16) for n in (2, 2, 3)]
        + [shape((piece, width), BF16)],
        in_specs=[smem] + [vmem] * 4,
        out_specs=[vmem] * 5,
        compiler_params=params(),
        name="begin_group",
    )(lengths, frames, w_conv.reshape(depth, width), w_proj, b_conv[None])
    far0 = hop(own_piece, 2)
    near_pack = hop(pack, 1)
    cot_picks = pl.pallas_call(
        pick,
        out_shape=[shape((n, quarter, width), BF16) for n in (2, 2, 3)],
        in_specs=[smem, vmem],
        out_specs=[vmem] * 3,
        compiler_params=params(),
        name="pick_cotangent",
    )(lengths, after(cotangent, *frame_picks))
    far0, near_pack, *cot_picks = lax.optimization_barrier((far0, near_pack, *cot_picks))
    far_frames = hop(frame_picks[2], 2)
    near_frames = hop(frame_picks[1], 1)
    far1, far2, near_frames = lax.optimization_barrier((dp_hop(far0, 1), dp_hop(far0, 2), near_frames))
    last = [dp_hop(far2[: piece // 2], 1), dp_hop(far1[piece // 2 :], 2)]
    frame_parts = [frame_picks[0], near_frames, far_frames, hop(far_frames[:2], 1)]
    cot_near = hop(after(cot_picks[1], far_frames), 1)
    cot_far = hop(after(cot_picks[2], far_frames), 2)

    rows = length + length // 2
    normed, stats, mixed = pl.pallas_call(
        attention_forward,
        out_shape=(
            shape((space, width), F32),
            shape((space, 128), F32),
            shape((space, width), BF16),
        ),
        in_specs=[smem] + [vmem] * 7,
        out_specs=[anywhere] * 3,
        scratch_shapes=[
            pltpu.VMEM((2, padded, width), BF16),
            pltpu.VMEM((2, padded, 2 * width), BF16),
            pltpu.VMEM((2, 2, length, width), BF16),
            pltpu.VMEM((2, length, width), F32),
            pltpu.VMEM((2, length, 128), F32),
            pltpu.VMEM((2, length, width), BF16),
            pltpu.SemaphoreType.DMA((2, 3, length // BLOCK)),
        ],
        compiler_params=params(),
        cost_estimate=cost(1e6, 1e5),
        name="attention_forward",
    )(after(lengths, near_pack), *near(*frame_parts), w_qkv, w_out, b_out)

    *last, cot_near, cot_far, normed = lax.optimization_barrier((*last, cot_near, cot_far, normed))
    cot_parts = [cot_picks[0], cot_near, cot_far, hop(cot_far[:2], 1)]
    far_pack = jnp.concatenate([far0, far1, far2] + last)
    far_near_pack = hop(far_pack, 1)
    packs = (pack, near_pack, far_pack, far_near_pack)

    chunk_rows = (depth + width) // 2
    block_count = limit // BLOCK
    result = pl.pallas_call(
        feed_forward,
        out_shape=[shape((n, quarter, width), BF16) for n in (2, 2, 4)]
        + [shape((2, 4, chunk_rows // 2, width), BF16)] * 2
        + [
            shape((limit, filters), BF16),
            shape((limit, width), F32),
            shape((depth, filters), BF16),
            shape((8, width), F32),
            shape((8, filters), F32),
        ],
        in_specs=[smem, anywhere] + [vmem] * 4 + [anywhere] * 4 + [vmem] * 5,
        out_specs=[vmem] * 3 + [anywhere] * 5 + [vmem] * 2,
        scratch_shapes=[
            pltpu.VMEM((pack_rows, filters), BF16),
            pltpu.VMEM((limit, width), F32),
            pltpu.VMEM((limit + 2 * HALO, width), F32),
            pltpu.VMEM((limit, depth), BF16),
            pltpu.VMEM((2, BLOCK, filters), F32),
            pltpu.VMEM((BLOCK, filters), F32),
            pltpu.VMEM((limit, filters), BF16),
            pltpu.VMEM((limit, width), BF16),
            pltpu.VMEM((limit, filters), BF16),
            pltpu.VMEM((limit, width), F32),
            pltpu.VMEM((4, depth + width, width), BF16),
            pltpu.VMEM((2, padded, width), BF16),
            pltpu.VMEM((space, width), BF16),
            pltpu.VMEM((space, width), BF16),
            pltpu.VMEM((padded, width), BF16),
            pltpu.SemaphoreType.DMA((FILTER_COPIES,)),
            pltpu.SemaphoreType.DMA((block_count,)),
            pltpu.SemaphoreType.DMA((2, block_count)),
            pltpu.SemaphoreType.DMA((taps + 1, 4, width // (chunk_rows // 10))),
            pltpu.SemaphoreType.DMA((1,)),
        ],
        compiler_params=pltpu.CompilerParams(vmem_limit_bytes=50 * 2**20),
        cost_estimate=cost(1e6, 1e5),
        name="feed_forward",
    )(lengths, normed, *near(*cot_parts, *packs), gain_one, shift_one, b_proj, gain_two, shift_two)
    (out_own, out_near, out_far), kept, sent = result[:3], result[3], result[4]
    d_hidden, dz_two, conv, small_two, conv_bias = result[5:]

    def add(a, b):
        return (a.astype(F32) + b.astype(F32)).astype(BF16)

    def total(*parts):
        return sum(part.astype(F32) for part in parts).astype(BF16)

    def halves(value, step):
        half = value.shape[-2] // 2
        bit = (dp_place // step) % 2
        axis = value.ndim - 2
        parts = value.reshape(value.shape[:-2] + (2, half, width))
        keep = lax.dynamic_index_in_dim(parts, bit, axis, keepdims=False)
        send = lax.dynamic_index_in_dim(parts, 1 - bit, axis, keepdims=False)
        return keep, dp_hop(send, step)

    def joined(value, other, step):
        bit = (dp_place // step) % 2
        return jnp.where(bit == 0, jnp.concatenate([value, other]), jnp.concatenate([other, value]))

    def collected(places, parts, dtype, name):
        return pl.pallas_call(
            functools.partial(collect, places),
            out_shape=shape((count, quarter, width), dtype),
            in_specs=[smem] + [vmem] * len(parts),
            out_specs=vmem,
            compiler_params=params(),
            name=name,
        )(lengths, *near(*parts))

    more = [2**i for i in range(2, 20) if 2**i < dp_size]
    got = hop(sent, 1)
    out_far = hop(out_far, 2)
    out_near = hop(out_near, 1)

    d_first = pl.pallas_call(
        conv_backward,
        out_shape=shape((limit, width), F32),
        in_specs=[smem] + [anywhere] * 3,
        out_specs=anywhere,
        scratch_shapes=[
            pltpu.VMEM((depth, filters), BF16),
            pltpu.VMEM((limit, filters), BF16),
            pltpu.VMEM((limit, width), F32),
            pltpu.VMEM((limit, width), F32),
            pltpu.VMEM((limit + HALO, width), F32),
            pltpu.SemaphoreType.DMA((taps,)),
            pltpu.SemaphoreType.DMA((2, block_count)),
            pltpu.SemaphoreType.DMA((1, block_count)),
        ],
        compiler_params=params(),
        cost_estimate=cost(1e6, 1e5),
        name="conv_backward",
    )(lengths, d_hidden, conv, dz_two)

    def attention_back(part, arrays, inputs, ties):
        late_rows = width + SMALL_ROWS
        if part:
            out_shapes = [shape((late_rows, width), BF16)] * 4
            out_specs = [vmem] * 4
            more_scratch = [pltpu.VMEM((4, width, width), BF16)]
        else:
            out_shapes = [
                shape((width, 3 * width), F32),
                shape((space, width), F32),
                shape((space, width), BF16),
                shape((space, 128), F32),
                shape((width, width), F32),
                shape((8, width), F32),
            ]
            out_specs = [vmem] + [anywhere] * 3 + [vmem] * 2
            more_scratch = [
                pltpu.VMEM((limit, width), F32),
                pltpu.VMEM((limit, width), F32),
                pltpu.VMEM((limit, 128), F32),
                pltpu.VMEM((limit, width), BF16),
                pltpu.SemaphoreType.DMA((3, block_count)),
            ]
        held = length if part else limit
        return pl.pallas_call(
            functools.partial(attention_backward, part),
            out_shape=[shape((quarter, width), BF16)] * 2 + [shape((2, quarter, width), BF16)] + out_shapes,
            in_specs=[smem] + [anywhere] * 4 + [vmem] + [anywhere] * len(arrays) + [vmem] * len(inputs),
            out_specs=[vmem] * 3 + out_specs,
            scratch_shapes=[
                pltpu.VMEM((padded, width), BF16),
                pltpu.VMEM((padded, 3 * width), BF16),
                pltpu.VMEM((padded, 3 * width), BF16),
                pltpu.VMEM((length, width), F32),
                pltpu.VMEM((length, width), F32),
                pltpu.VMEM((padded, width), F32),
                pltpu.VMEM((held, width), F32),
                pltpu.VMEM((held, width), BF16),
                pltpu.VMEM((held, 128), F32),
                pltpu.SemaphoreType.DMA((4,)),
                pltpu.SemaphoreType.DMA((4, block_count)),
            ]
            + more_scratch,
            compiler_params=params(),
            cost_estimate=cost(1e6, 1e5),
            name=f"attention_backward_{'ac'[part]}",
        )(after(lengths, *ties), *frame_parts, w_qkv, *arrays, *inputs)

    got, out_far, out_near = lax.optimization_barrier((got, out_far, out_near, d_first))[:3]
    send_x, send_y = total(kept[1, :2], got[1, :2]), total(kept[1, 2:], got[1, 2:])
    got_x, got_y = dp_hop(send_x, 1), hop(send_y, 2)
    out_beyond = hop(out_far[2:], 1)
    a_own, a_near, a_far, grad_qkv, dz_one, d_mixed, soft, grad_out, small = attention_back(
        0, [d_first, normed, stats, mixed], [w_out, gain_one, small_two], [send_x, send_y]
    )
    got_x, got_y, out_beyond = lax.optimization_barrier((got_x, got_y, out_beyond, grad_qkv))[:3]
    send_x, send_y = total(kept[0, 1], got[0, 1], got_x[1]), total(kept[0, 3], got[0, 3], got_y[1])
    next_x, next_y = hop(send_x, 2), dp_hop(send_y, 2)
    a_far = hop(a_far, 2)
    c_own, c_near, c_far, late0, late1, late2, late3 = attention_back(
        1, [dz_one, d_mixed, soft], [grad_qkv, grad_out, small, conv_bias], [send_x, send_y]
    )
    next_x, next_y = lax.optimization_barrier((next_x, next_y, late0))[:2]
    state = [total(kept[0, 0], got[0, 0], got_x[0], next_x), total(kept[0, 2], got[0, 2], got_y[0], next_y)]

    late_parts = [hop(after(part, *state), d) for d, part in ((1, late1), (2, late2), (3, late3))]
    moving = [halves(state[0], 2), halves(state[1], 1)]
    late = total(late0, *late_parts)
    state = jnp.concatenate([add(keep, after(other, late)) for keep, other in moving])
    c_far = hop(after(c_far, late), 2)
    others = [dp_hop(state, step) for step in more[:1]]
    late_parts = [dp_hop(late, step) for step in (1, 2, 3)]
    output = collected(
        [((0, 0), (0, 1)), ((1, 0), (1, 1)), ((2, 0), (2, 1)), ((3, 0), (3, 1))],
        [after(out_own, late), out_near, out_far, out_beyond],
        BF16,
        "collect_output",
    )
    *others, p1, p2, p3, output, c_far = lax.optimization_barrier((*others, *late_parts, output, c_far))
    late = total(late, p1, p2, p3)
    for other in others:
        state = add(state, other)
    for step in more[1:]:
        state = add(state, dp_hop(state, step))
    state = jnp.split(state, 2)
    backs = [[2, 1], [1, 2]]
    others = [dp_hop(value, back[0]) for value, back in zip(state, backs)]
    near_grads = hop(after(jnp.stack([a_near, c_near, a_far[1], c_far[1]]), late), 1)
    for step in more:
        late = add(late, dp_hop(late, step))
    *others, late, near_grads = lax.optimization_barrier((*others, late, near_grads))
    state = [joined(value, other, back[0]) for value, other, back in zip(state, others, backs)]
    last = [back[-1] for back in backs]
    others = [dp_hop(value, step) for value, step in zip(state, last)]
    blocks = [hop(late[:width], d) for d in (1, 2, 3)]
    d_frames = collected(
        [((0, None), (1, None)), ((2, 0), (2, 1)), ((3, 0), (4, 0)), ((2, 2), (2, 3))],
        [a_own, c_own, near_grads, a_far, c_far],
        F32,
        "collect_grad",
    )
    grad_conv, grad_proj = pl.pallas_call(
        functools.partial(finish_filters, last),
        out_shape=(shape((depth, width), F32), shape((width, width), F32)),
        in_specs=[vmem] * 4,
        out_specs=[vmem] * 2,
        scratch_shapes=[pltpu.VMEM((depth + width, width), BF16)],
        compiler_params=params(),
        name="finish_filters",
    )(*near(*[part for pair in zip(state, others) for part in pair]))
    grad_qkv, grad_out, *vectors = pl.pallas_call(
        finish_late,
        out_shape=[shape((width, 3 * width), F32), shape((width, width), F32)] + [shape((1, width), F32)] * 7,
        in_specs=[vmem] * 4,
        out_specs=[vmem] * 9,
        scratch_shapes=[pltpu.VMEM((4, width, width), F32)],
        compiler_params=params(),
        name="finish_late",
    )(*near(late, *blocks))
    vectors = [v.reshape(width) for v in vectors]
    return (
        output,
        d_frames,
        grad_qkv,
        grad_out,
        vectors[0],
        vectors[1],
        vectors[2],
        grad_conv.reshape(w_conv.shape),
        vectors[6],
        grad_proj,
        vectors[3],
        vectors[4],
        vectors[5],
    )


def solution(mesh):
    return jax.shard_map(
        shards,
        mesh=mesh,
        in_specs=(
            P("dp", "tensor", None),
            P("dp"),
            P(),
            P(),
            P(),
            P(),
            P(),
            P(None, None, "tensor"),
            P("tensor"),
            P("tensor", None),
            P(),
            P(),
            P(),
            P("dp", "tensor", None),
        ),
        out_specs=(
            P("dp", "tensor", None),
            P("dp", "tensor", None),
            P(),
            P(),
            P(),
            P(),
            P(),
            P(None, None, "tensor"),
            P("tensor"),
            P("tensor", None),
            P(),
            P(),
            P(),
        ),
        check_vma=False,
    )
```

```python
import functools
import itertools

import jax
import jax.experimental.pallas as pl
import jax.experimental.pallas.tpu as pltpu
import jax.numpy as jnp
import numpy as np
from jax import lax
from jax.sharding import PartitionSpec as P


EPSILON = 1e-05
F32 = jnp.float32
BF16 = jnp.bfloat16
HALO = 16
BLOCK = 256
MASKED = -1e30
GELU_A = float(np.sqrt(2.0 / np.pi))
GELU_B = 0.044715
LOG2E = float(np.log2(np.e))
VMEM_LIMIT = 54 * 2**20
SMALL_ROWS = 16


def near(*arrays):
    return [pltpu.with_memory_space_constraint(array, pltpu.VMEM) for array in arrays]


def params(**more):
    return pltpu.CompilerParams(vmem_limit_bytes=VMEM_LIMIT, **more)


def cost(flops, size):
    return pl.CostEstimate(flops=int(flops), bytes_accessed=int(size), transcendentals=0)


def dot(a, b):
    return jnp.dot(a, b, preferred_element_type=F32)


def dot_nt(a, b):
    return lax.dot_general(a, b, (((1,), (1,)), ((), ())), preferred_element_type=F32)


def dot_tn(a, b):
    return lax.dot_general(a, b, (((0,), (0,)), ((), ())), preferred_element_type=F32)


def at(start, size, step=HALO):
    return pl.ds(pl.multiple_of(start, step), size)


def up(value, step=HALO):
    return ((value + (step - 1)) // step) * step


def choose(index, options):
    result = options[-1]
    for i, option in enumerate(options[:-1]):
        result = jnp.where(index == i, option, result)
    return result


def plan(lengths):
    keys = [lengths[i] * 8 + i for i in range(6)]
    best, triples = None, None
    for pair in itertools.combinations(range(1, 6), 2):
        mine = (0,) + pair
        rest = tuple(i for i in range(6) if i not in mine)
        gap = jnp.abs(sum(lengths[i] for i in mine) - sum(lengths[i] for i in rest))
        option = [keys[i] for i in mine + rest]
        if best is None:
            best, triples = gap, option
        else:
            better = gap < best
            best = jnp.where(better, gap, best)
            triples = [jnp.where(better, new, old) for new, old in zip(option, triples)]
    whole, shared = [], []
    for a, b, c in (triples[:3], triples[3:]):
        a, b = jnp.maximum(a, b), jnp.minimum(a, b)
        a, c = jnp.maximum(a, c), jnp.minimum(a, c)
        b, c = jnp.maximum(b, c), jnp.minimum(b, c)
        whole += [a, b]
        shared.append(c)
    return whole, shared


class Rows:
    def __init__(self, lengths, length):
        self.member = lax.axis_index("tensor")
        whole, shared = plan(lengths)
        self.whole, self.shared = whole, shared
        role = self.member % 2
        second = self.member >= 2
        key_a = choose(self.member, whole)
        self.len_a = key_a // 8
        self.len_c = jnp.where(second, shared[1], shared[0]) // 8
        first_len = jnp.where(second, whole[2], whole[0]) // 8
        other_len = jnp.where(second, whole[3], whole[1]) // 8
        split = (other_len + self.len_c - first_len) // 2
        split = jnp.maximum((split + HALO // 2) // HALO * HALO, HALO)
        starts = role == 0
        self.own_from = jnp.where(starts, 0, split)
        self.own_to = jnp.where(starts, split, length)
        self.window = jnp.where(starts, 0, split - HALO)
        self.end = jnp.where(starts, jnp.minimum(split + HALO, self.len_c), self.len_c)
        self.rows_a = up(self.len_a + 4)
        self.rows_c = jnp.maximum(up(self.end) - self.window, 0)
        self.tiles_a = (self.len_a + BLOCK - 1) // BLOCK
        self.tiles_c = (self.rows_c + BLOCK - 1) // BLOCK
        self.blocks = (self.rows_a + self.rows_c + BLOCK - 1) // BLOCK
        self.halo = self.rows_a + jnp.where(starts, split, 0)

    def masks(self, start, size):
        row = start + lax.broadcasted_iota(jnp.int32, (size, 1), 0)
        in_a = row < self.rows_a
        frame = jnp.where(in_a, row, row - self.rows_a + self.window)
        live = frame < jnp.where(in_a, self.len_a, self.end)
        inside = (frame >= self.own_from) & (frame < self.own_to)
        return live, live & (in_a | inside)

    def frames_at(self, part, index):
        return at(BLOCK * index + (self.window if part else 0), BLOCK)

    def base(self, part, index):
        return BLOCK * index + (self.rows_a if part else 0)


def piece_index(piece, part):
    return part if piece.shape[0] == 2 else 2 - part


def place(member, pieces, target):
    quarter = pieces[0].shape[1]
    for distance, piece in enumerate(pieces):
        rows = at((member ^ distance) * quarter, quarter, quarter)
        for part in range(2):
            target[part, rows, :] = piece[piece_index(piece, part)]


def pick(lengths, source, *targets):
    member = lax.axis_index("tensor")
    whole, shared = plan(lengths)
    for distance, target in enumerate(targets):
        there = member ^ distance
        if target.shape[0] == 3:
            target[0] = source[choose(there ^ 1, whole) % 8]
        target[piece_index(target, 0)] = source[choose(there, whole) % 8]
        target[piece_index(target, 1)] = source[jnp.where(there >= 2, shared[1], shared[0]) % 8]


def begin_group(lengths, source, w_conv, w_proj, b_conv, pack, p0, p1, p2, part):
    depth, width = w_conv.shape
    pack[0:depth, :] = w_conv[...]
    pack[depth : depth + width, :] = w_proj[...]
    high = b_conv[...].astype(BF16)
    rest = (b_conv[...] - high.astype(F32)).astype(BF16)
    last = depth + width
    pack[last : last + HALO, :] = jnp.broadcast_to(high, (HALO, width))
    pack[last + HALO :, :] = jnp.broadcast_to(rest, (pack.shape[0] - last - HALO, width))
    piece = part.shape[0]
    part[...] = pack[at((lax.axis_index("dp") % 4) * piece, piece), :]
    pick(lengths, source, p0, p1, p2)


def softmax_parts(rows, part, length):
    return (rows.len_c if part else rows.len_a), lax.broadcasted_iota(jnp.int32, (1, length), 1)


def mask_keys(scores, column, limit):
    half = scores.shape[1] // 2
    tail = jnp.where(column[:, half:] < limit, scores[:, half:], MASKED)
    return jnp.concatenate([scores[:, :half], tail], axis=1)


def attention_forward(
    lengths, r0, r1, r2, r3, w_qkv, w_out, b_out, normed, stats, mixed, placed, qkv, valued, n_out, s_out, m_out, sems
):
    quarter = r0.shape[1]
    length = 4 * quarter
    width = r0.shape[2]
    head = width // 2
    scale = head ** (-0.5) * LOG2E
    rows = Rows(lengths, length)
    spare = placed.shape[1] - length
    placed[:, length:, :] = jnp.zeros((2, spare, width), BF16)
    place(rows.member, (r0, r1, r2, r3), placed)
    for part in range(2):
        for h in range(2):
            valued[part, h, :, head:] = jnp.ones((length, head), BF16)

    def project(index, carry):
        here = at(index * BLOCK, BLOCK, BLOCK)
        for part in range(2):
            value = dot(placed[part, here, :], w_qkv[...]).astype(BF16)
            qkv[part, here, :] = value[:, : 2 * width]
            for h in range(2):
                valued[part, h, here, :head] = value[:, 2 * width + h * head : 2 * width + (h + 1) * head]
        return carry

    lax.fori_loop(0, length // BLOCK, project, 0)
    qkv[:, length:, :] = jnp.zeros((2, spare, 2 * width), BF16)
    lane = lax.broadcasted_iota(jnp.int32, (1, 128), 1)

    def copies(part, index):
        there = at(rows.base(part, index), BLOCK)
        here = at(index * BLOCK, BLOCK, BLOCK)
        pairs = ((n_out, normed), (s_out, stats), (m_out, mixed))
        return [
            pltpu.make_async_copy(source.at[part, here], target.at[there], sems.at[part, i, index])
            for i, (source, target) in enumerate(pairs)
        ]

    def tile(part, index, carry):
        frames_at = rows.frames_at(part, index)
        here = at(index * BLOCK, BLOCK, BLOCK)
        limit, column = softmax_parts(rows, part, length)
        mixtures, logs = [], []
        for h in range(2):
            low, high = h * head, (h + 1) * head
            scores = dot_nt(qkv[part, frames_at, low:high], qkv[part, :length, width + low : width + high])
            scores = mask_keys(scores, column, limit)
            highest = jnp.max(scores, axis=-1, keepdims=True) * scale
            exponent = jnp.exp2(scores * scale - highest).astype(BF16)
            summed = dot(exponent, valued[part, h])
            total = summed[:, head : head + 1]
            mixtures.append((summed[:, :head] / total).astype(BF16))
            logs.append(highest + jnp.log2(total))
        mixture = jnp.concatenate(mixtures, axis=1)
        m_out[part, here, :] = mixture
        residual = placed[part, frames_at, :].astype(F32) + dot(mixture, w_out[...]) + b_out[...]
        centred = residual - jnp.mean(residual, axis=-1, keepdims=True)
        inverse = lax.rsqrt(jnp.mean(centred * centred, axis=-1, keepdims=True) + EPSILON)
        n_out[part, here, :] = centred * inverse
        s_out[part, here, :] = jnp.where(lane == 0, logs[0], jnp.where(lane == 1, logs[1], inverse))
        for copy in copies(part, index):
            copy.start()
        return carry

    def finish(part, index, carry):
        for copy in copies(part, index):
            copy.wait()
        return carry

    for part, count in enumerate((rows.tiles_a, rows.tiles_c)):
        lax.fori_loop(0, count, functools.partial(tile, part), 0)
        lax.fori_loop(0, count, functools.partial(finish, part), 0)


def gelu_pair(x):
    square = x * x
    t = jnp.tanh(GELU_A * x * (1.0 + GELU_B * square))
    half = 0.5 * (1.0 + t)
    slope = half + (0.5 * GELU_A) * x * (1.0 - t * t) * (1.0 + 3.0 * GELU_B * square)
    return x * half, slope


def load_filters(near, far, target, sems):
    width = near[0].shape[1]
    piece = near[0].shape[0] // 4
    shift = lax.axis_index("dp") % 4
    copies = []
    for j, source in enumerate(near):
        copies.append((source, target.at[:, pl.ds(j * width, width)]))
    for j, source in enumerate(far):
        for i in range(4):
            there = at((shift ^ i) * piece, piece)
            part = pl.ds((2 + j) * width, width)
            copies.append((source.at[pl.ds(i * piece, piece)], target.at[there, part]))
    copies = [
        pltpu.make_async_copy(source, there, sems.at[i]) for i, (source, there) in enumerate(copies)
    ]
    for copy in copies:
        copy.start()
    return copies


FILTER_COPIES = 10


def feed_forward(
    lengths,
    normed,
    c0,
    c1,
    c2,
    c3,
    pack0,
    pack1,
    far0,
    far1,
    gain_one,
    shift_one,
    b_proj,
    gain_two,
    shift_two,
    o0,
    o1,
    o_far,
    kept,
    sent,
    d_hidden_out,
    dz_out,
    small,
    conv_bias,
    weights,
    units,
    first,
    columns,
    hidden,
    slope,
    active,
    d_branch,
    d_hidden,
    dz_two,
    grads,
    cot_frames,
    cot_rows,
    out_rows,
    out_c,
    load_sems,
    unit_sems,
    out_sems,
    grad_sems,
):
    quarter, width = c0.shape[1:]
    length = 4 * quarter
    filters = weights.shape[1]
    taps = columns.shape[1] // width
    depth = taps * width
    reach = taps // 2
    loads = load_filters((pack0, pack1), (far0, far1), weights, load_sems)
    rows = Rows(lengths, length)
    blocks = rows.blocks

    def unit_copy(index):
        here = at(index * BLOCK, BLOCK, BLOCK)
        return pltpu.make_async_copy(normed.at[here], units.at[here], unit_sems.at[index])

    def start_unit(index, carry):
        unit_copy(index).start()
        return carry

    lax.fori_loop(0, blocks, start_unit, 0)
    place(rows.member, (c0, c1, c2, c3), cot_frames)
    cot_frames[:, length:, :] = jnp.zeros((2, cot_frames.shape[1] - length, width), BF16)
    cot_rows[0:length, :] = cot_frames[0, 0:length, :]

    def gather_cot(index, carry):
        cot_rows[at(rows.base(1, index), BLOCK), :] = cot_frames[1, rows.frames_at(1, index), :]
        return carry

    lax.fori_loop(0, rows.tiles_c, gather_cot, 0)
    out_rows[...] = jnp.zeros(out_rows.shape, BF16)
    small[...] = jnp.zeros(small.shape, F32)
    conv_bias[...] = jnp.zeros(conv_bias.shape, F32)

    first[0:HALO, :] = jnp.zeros((HALO, width), F32)

    def make_first(index, carry):
        base = index * BLOCK
        unit_copy(index).wait()
        live, _ = rows.masks(base, BLOCK)
        value = units[at(base, BLOCK), :] * gain_one[...] + shift_one[...]
        first[at(base + HALO, BLOCK), :] = jnp.where(live, value, 0.0)
        return carry

    lax.fori_loop(0, blocks, make_first, 0)
    first[at(blocks * BLOCK + HALO, HALO), :] = jnp.zeros((HALO, width), F32)

    def make_columns(index, carry):
        base = index * BLOCK
        around = first[at(base + HALO - 8, BLOCK + 16, 8), :]
        for k in range(taps):
            columns[at(base, BLOCK, BLOCK), k * width : (k + 1) * width] = around[
                8 - reach + k : 8 - reach + k + BLOCK
            ].astype(BF16)
        return carry

    lax.fori_loop(0, blocks, make_columns, 0)
    for copy in loads:
        copy.wait()

    def out_copies(index):
        here = at(index * BLOCK, BLOCK, BLOCK)
        return [
            pltpu.make_async_copy(d_hidden.at[here], d_hidden_out.at[here], out_sems.at[0, index]),
            pltpu.make_async_copy(dz_two.at[here], dz_out.at[here], out_sems.at[1, index]),
        ]

    def conv(index, target):
        target[...] = dot(columns[at(index * BLOCK, BLOCK, BLOCK), :], weights[0:depth, :])

    def rest(index, source):
        base = index * BLOCK
        here = at(base, BLOCK, BLOCK)
        live, own = rows.masks(base, BLOCK)
        branch = jnp.zeros((BLOCK, width), F32)
        for j in range(filters // width):
            part = slice(j * width, (j + 1) * width)
            bias = weights[depth + width : depth + width + 1, part].astype(F32) + weights[
                depth + width + 16 : depth + width + 17, part
            ].astype(F32)
            value, derivative = gelu_pair(source[:, part] + bias)
            value = value.astype(BF16)
            active[here, part] = value
            slope[:, part] = derivative
            branch = branch + dot(value, weights[depth : depth + width, part])
        residual = first[at(base + HALO, BLOCK), :] + branch + b_proj[...]
        centred = residual - jnp.mean(residual, axis=-1, keepdims=True)
        inverse = lax.rsqrt(jnp.mean(centred * centred, axis=-1, keepdims=True) + EPSILON)
        normed_two = centred * inverse
        out_rows[here, :] = jnp.where(own, normed_two * gain_two[...] + shift_two[...], 0.0).astype(BF16)
        upstream = jnp.where(live, cot_rows[here, :].astype(F32), 0.0)
        counted = jnp.where(own, upstream, 0.0)
        scaled = upstream * gain_two[...]
        dz = inverse * (
            scaled
            - jnp.mean(scaled, axis=-1, keepdims=True)
            - normed_two * jnp.mean(scaled * normed_two, axis=-1, keepdims=True)
        )
        dz_two[here, :] = dz
        small[3:4, :] += jnp.sum(jnp.where(own, dz, 0.0), axis=0, keepdims=True)
        small[4:5, :] += jnp.sum(counted * normed_two, axis=0, keepdims=True)
        small[5:6, :] += jnp.sum(counted, axis=0, keepdims=True)
        low = dz.astype(BF16)
        d_branch[here, :] = jnp.where(own, low, jnp.zeros_like(low))
        for j in range(filters // width):
            part = slice(j * width, (j + 1) * width)
            grad = dot_nt(low, weights[depth : depth + width, part]) * slope[:, part]
            conv_bias[0:1, part] += jnp.sum(jnp.where(own, grad, 0.0), axis=0, keepdims=True)
            d_hidden[here, part] = grad.astype(BF16)
        for copy in out_copies(index):
            copy.start()

    even, odd = hidden.at[0], hidden.at[1]
    conv(0, even)

    def step(pair, carry):
        index = 2 * pair
        conv(index + 1, odd)
        rest(index, even)
        conv(index + 2, even)
        rest(index + 1, odd)
        return carry

    lax.fori_loop(0, (blocks - 1) // 2, step, 0)

    @pl.when(blocks % 2 == 1)
    def _():
        rest(blocks - 1, even)

    @pl.when(blocks % 2 == 0)
    def _():
        conv(blocks - 1, odd)
        rest(blocks - 2, even)
        rest(blocks - 1, odd)

    columns[at(rows.halo, HALO), :] = jnp.zeros((HALO, columns.shape[1]), BF16)

    per_chunk = (taps + 1) // 2

    x_bit, z_bit = lax.axis_index("dp") % 2, (lax.axis_index("dp") // 2) % 2
    half_rows = kept.shape[2]
    piece = half_rows // 5

    def grad_copies(k, chunk):
        copies = []
        for u in range(width // piece):
            row = (k - chunk * per_chunk) * width + u * piece
            half = row // half_rows
            there = at(row - half * half_rows, piece, piece)
            here = at(k * width + u * piece, piece, piece)
            for j in range(filters // width):
                place = (half ^ x_bit, j // 2) if chunk == 0 else (j // 2, 2 + (half ^ z_bit))
                target = (kept, sent)[j % 2].at[place[0], place[1], there]
                copies.append(pltpu.make_async_copy(grads.at[j, here], target, grad_sems.at[k, j, u]))
        return copies

    for count in range(4, active.shape[0] // BLOCK + 1):

        @pl.when(blocks == count)
        def _():
            n = count * BLOCK

            def tap(k, carry):
                here = at(k * width, width, width)
                value = dot_tn(columns[0:n, here], d_hidden[0:n, :]).astype(BF16)
                for j in range(filters // width):
                    grads[j, here, :] = value[:, j * width : (j + 1) * width]
                for chunk in range(2):

                    @pl.when(k // per_chunk == chunk)
                    def _():
                        for copy in grad_copies(k, chunk):
                            copy.start()

                return carry

            lax.fori_loop(0, taps, tap, 0)
            value = dot_tn(active[0:n, :], d_branch[0:n, :]).astype(BF16)
            for j in range(filters // width):
                grads[j, depth:, :] = value[j * width : (j + 1) * width, :]
            for copy in grad_copies(taps, 1):
                copy.start()

    out_c[...] = jnp.zeros(out_c.shape, BF16)

    def scatter_out(index, carry):
        out_c[rows.frames_at(1, index), :] = out_rows[at(rows.base(1, index), BLOCK), :]
        return carry

    lax.fori_loop(0, rows.tiles_c, scatter_out, 0)
    for distance, (target, slot) in enumerate(((o0, 0), (o1, 0), (o_far, 0), (o_far, 2))):
        start = (rows.member ^ distance) * quarter
        there = at(start, quarter, quarter)
        row = start + lax.broadcasted_iota(jnp.int32, (quarter, 1), 0)
        value = out_rows[there, :]
        target[slot] = jnp.where(row < rows.len_a, value, jnp.zeros_like(value))
        target[slot + 1] = out_c[there, :]


    def finish(index, carry):
        for copy in out_copies(index):
            copy.wait()
        return carry

    lax.fori_loop(0, blocks, finish, 0)

    def finish_grads(chunk, k, carry):
        for copy in grad_copies(k, chunk):
            copy.wait()
        return carry

    lax.fori_loop(0, per_chunk, functools.partial(finish_grads, 0), 0)
    lax.fori_loop(per_chunk, 2 * per_chunk, functools.partial(finish_grads, 1), 0)


def block_copies(pairs, sems, index):
    here = at(index * BLOCK, BLOCK, BLOCK)
    return [
        pltpu.make_async_copy(source.at[here], target.at[here], sems.at[i, index])
        for i, (source, target) in enumerate(pairs)
    ]


def conv_backward(
    lengths,
    d_hidden_in,
    pack0,
    pack1,
    far0,
    far1,
    dz_in,
    d_first_out,
    weights,
    d_hidden,
    dz_two,
    d_first,
    sums,
    conv_sems,
    in_sems,
    out_sems,
):
    width = dz_two.shape[1]
    taps = weights.shape[0] // width - 1
    reach = taps // 2
    conv_copies = load_filters((pack0, pack1), (far0, far1), weights, conv_sems)
    blocks = Rows(lengths, 4 * width).blocks
    into = ((d_hidden_in, d_hidden), (dz_in, dz_two))
    onto = ((d_first, d_first_out),)

    def start(index, carry):
        for copy in block_copies(into, in_sems, index):
            copy.start()
        return carry

    lax.fori_loop(0, blocks, start, 0)
    sums[0:HALO, :] = jnp.zeros((HALO, width), F32)
    for copy in conv_copies:
        copy.wait()

    def back(index, carry):
        base = index * BLOCK
        for copy in block_copies(into, in_sems, index):
            copy.wait()
        value = d_hidden[at(base, BLOCK, BLOCK), :]
        total = jnp.zeros((BLOCK + HALO, width), F32)
        for k in range(taps):
            part = dot_nt(value, weights[k * width : (k + 1) * width, :])
            part = jnp.concatenate([part, jnp.zeros((HALO, width), F32)], axis=0)
            total = total + pltpu.roll(part, 8 - reach + k, axis=0)
        sums[at(base, HALO), :] += total[0:HALO]
        sums[at(base + HALO, BLOCK), :] = total[HALO:]
        return carry

    lax.fori_loop(0, blocks, back, 0)

    def finish(index, carry):
        base = index * BLOCK
        here = at(base, BLOCK, BLOCK)
        d_first[here, :] = dz_two[here, :] + sums[at(base + 8, BLOCK, 8), :]
        block_copies(onto, out_sems, index)[0].start()
        return carry

    lax.fori_loop(0, blocks, finish, 0)

    def drain(index, carry):
        block_copies(onto, out_sems, index)[0].wait()
        return carry

    lax.fori_loop(0, blocks, drain, 0)


def first_norm_backward(rows, ins, outs, blocks_in, blocks_out, in_sems, out_sems, w_out, gain_one, small, grad_out):
    d_first, normed, stats, mixed = blocks_in
    dz_one, d_mixed, soft = blocks_out
    into, onto = tuple(zip(ins, blocks_in)), tuple(zip(blocks_out, outs))
    width = normed.shape[1]
    head = width // 2
    lane = lax.broadcasted_iota(jnp.int32, (1, 128), 1)

    def block(index, carry):
        base = index * BLOCK
        here = at(base, BLOCK, BLOCK)
        for copy in block_copies(into, in_sems, index):
            copy.wait()
        _, own = rows.masks(base, BLOCK)
        total = jnp.where(own, d_first[here, :], 0.0)
        unit = jnp.where(own, normed[here, :], 0.0)
        kept = stats[here, :]
        inverse = kept[:, 2:3]
        scaled = total * gain_one[...]
        dz = inverse * (
            scaled
            - jnp.mean(scaled, axis=-1, keepdims=True)
            - unit * jnp.mean(scaled * unit, axis=-1, keepdims=True)
        )
        dz = jnp.where(own, dz, 0.0)
        dz_one[here, :] = dz
        small[0:1, :] += jnp.sum(dz, axis=0, keepdims=True)
        small[1:2, :] += jnp.sum(total * unit, axis=0, keepdims=True)
        small[2:3, :] += jnp.sum(total, axis=0, keepdims=True)
        low = dz.astype(BF16)
        upstream = dot_nt(low, w_out[...]).astype(BF16)
        d_mixed[here, :] = upstream
        mixture = mixed[here, :]
        mixture = jnp.where(own, mixture, jnp.zeros_like(mixture))
        grad_out[...] += dot_tn(mixture, low)
        product = upstream.astype(F32) * mixture.astype(F32)
        means = [jnp.sum(product[:, h * head : (h + 1) * head], axis=-1, keepdims=True) for h in range(2)]
        soft[here, :] = jnp.where(
            lane < 2, jnp.where(own, kept, -MASKED), jnp.where(lane == 2, means[0], means[1])
        )
        for copy in block_copies(onto, out_sems, index):
            copy.start()
        return carry

    lax.fori_loop(0, rows.blocks, block, 0)

    def finish(index, carry):
        for copy in block_copies(onto, out_sems, index):
            copy.wait()
        return carry

    return finish


def attention_backward(part, *refs):
    (lengths, r0, r1, r2, r3, w_qkv), refs = refs[:6], refs[6:]
    if part:
        in_refs, refs = refs[:3], refs[3:]
        inputs, refs = refs[:4], refs[4:]
        (g0, g1, g_far), refs = refs[:3], refs[3:]
        late, refs = refs[:4], refs[4:]
    else:
        in_refs, refs = refs[:4], refs[4:]
        (w_out, gain_one, small_two), refs = refs[:3], refs[3:]
        (g0, g1, g_far), refs = refs[:3], refs[3:]
        grad_qkv, refs = refs[0], refs[1:]
        out_refs, refs = refs[:3], refs[3:]
        (grad_out, small), refs = refs[:2], refs[2:]
    placed, qkv, d_proj, keys, values, frame_grads, dz_one, d_mixed, soft, place_sems, in_sems = refs[:11]
    quarter = r0.shape[1]
    length = 4 * quarter
    width = r0.shape[2]
    head = width // 2
    scale = head ** (-0.5)
    rows = Rows(lengths, length)
    tiles = rows.tiles_c if part else rows.tiles_a
    spare = placed.shape[0] - length
    places = [
        pltpu.make_async_copy(
            piece.at[piece_index(piece, part)],
            placed.at[at((rows.member ^ distance) * quarter, quarter, quarter)],
            place_sems.at[distance],
        )
        for distance, piece in enumerate((r0, r1, r2, r3))
    ]

    def copies(index):
        there = at(rows.base(part, index), BLOCK)
        here = at(index * BLOCK, BLOCK, BLOCK)
        return [
            pltpu.make_async_copy(source.at[there], target.at[here], in_sems.at[i, index])
            for i, (source, target) in enumerate(zip(in_refs, (dz_one, d_mixed, soft)))
        ]

    if part:

        def start(index, carry):
            for copy in copies(index):
                copy.start()
            return carry

        lax.fori_loop(0, tiles, start, 0)
    else:
        blocks_in, out_sems = refs[11:15], refs[15]

        def start(index, carry):
            for copy in block_copies(tuple(zip(in_refs, blocks_in)), in_sems, index):
                copy.start()
            return carry

        lax.fori_loop(0, rows.blocks, start, 0)
    for copy in places:
        copy.start()
    placed[length:, :] = jnp.zeros((spare, width), BF16)
    d_proj[...] = jnp.zeros(d_proj.shape, BF16)
    keys[...] = jnp.zeros(keys.shape, F32)
    values[...] = jnp.zeros(values.shape, F32)
    frame_grads[...] = jnp.zeros(frame_grads.shape, F32)
    if not part:
        small[...] = small_two[...]
        grad_out[...] = jnp.zeros(grad_out.shape, F32)
        finish = first_norm_backward(
            rows, in_refs, out_refs, blocks_in, (dz_one, d_mixed, soft), in_sems, out_sems, w_out, gain_one, small, grad_out
        )
    for copy in places:
        copy.wait()

    def project(index, carry):
        here = at(index * BLOCK, BLOCK, BLOCK)
        qkv[here, :] = dot(placed[here, :], w_qkv[...]).astype(BF16)
        return carry

    lax.fori_loop(0, length // BLOCK, project, 0)
    qkv[length:, :] = jnp.zeros((spare, 3 * width), BF16)

    def tile(index, carry):
        frames_at = rows.frames_at(part, index)
        here = at(index * BLOCK, BLOCK, BLOCK)
        if part:
            for copy in copies(index):
                copy.wait()
        limit, column = softmax_parts(rows, part, length)
        inside = BLOCK * index + lax.broadcasted_iota(jnp.int32, (BLOCK, 1), 0)
        inside = inside < (rows.rows_c if part else rows.rows_a)
        frame_grads[frames_at, :] = jnp.where(inside, dz_one[here, :], 0.0)
        for h in range(2):
            low, high = h * head, (h + 1) * head
            query = qkv[frames_at, low:high]
            key = qkv[:length, width + low : width + high]
            value = qkv[:length, 2 * width + low : 2 * width + high]
            upstream = d_mixed[here, low:high]
            upstream = jnp.where(inside, upstream, jnp.zeros_like(upstream))
            shift = jnp.where(inside, soft[here, h : h + 1], -MASKED)
            mean = jnp.where(inside, soft[here, 2 + h : 3 + h], 0.0)
            scores = mask_keys(dot_nt(query, key), column, limit)
            weights = jnp.exp2(scores * (scale * LOG2E) - shift)
            d_weights = dot_nt(upstream, value)
            d_scores = (weights * (d_weights - mean)).astype(BF16)
            d_proj[frames_at, low:high] = (dot(d_scores, key) * scale).astype(BF16)
            keys[:, low:high] += dot_tn(d_scores, query)
            values[:, low:high] += dot_tn(weights.astype(BF16), upstream)
        return carry

    lax.fori_loop(0, tiles, tile, 0)
    d_proj[0:length, width : 2 * width] = (keys[...] * scale).astype(BF16)
    d_proj[0:length, 2 * width : 3 * width] = values[...].astype(BF16)
    for distance, target in enumerate((g0, g1, g_far.at[0], g_far.at[1])):
        here = at((rows.member ^ distance) * quarter, quarter, quarter)
        target[...] = (frame_grads[here, :] + dot_nt(d_proj[here, :], w_qkv[...])).astype(BF16)
    grads = dot_tn(placed[0:length, :], d_proj[0:length, :])
    if part == 0:
        grad_qkv[...] = grads
        lax.fori_loop(0, rows.blocks, finish, 0)
        return
    blocks = refs[11]
    grad_before, grad_out, small, conv_bias = inputs
    grads = (grads + grad_before[...]).astype(BF16)
    for q in range(3):
        blocks[q, :, :] = grads[:, q * width : (q + 1) * width]
    blocks[3, :, :] = grad_out[...].astype(BF16)
    line = lax.broadcasted_iota(jnp.int32, (8, 1), 0)
    for j, target in enumerate(late):
        target[0:width, :] = blocks[rows.member ^ j]
        bias = conv_bias[0:1, j * width : (j + 1) * width]
        tail = jnp.where(line == 6, bias, small[...])
        tail = jnp.concatenate([tail, jnp.zeros((SMALL_ROWS - 8, width), F32)], axis=0)
        target[width : width + SMALL_ROWS, :] = tail.astype(BF16)


def collect(places, lengths, *refs):
    result = refs[-1]
    member = lax.axis_index("tensor")
    whole, shared = plan(lengths)

    def piece(place):
        array, index = place
        return refs[array][...] if index is None else refs[array][index]

    for distance in range(4):
        slot = choose(member ^ distance, whole) % 8
        result[slot] = piece(places[distance][0]).astype(result.dtype)
    for side in range(2):
        second = (member >= 2) == (side == 0)
        slot = jnp.where(second, shared[1], shared[0]) % 8
        total = piece(places[2 * side][1]).astype(F32) + piece(places[2 * side + 1][1]).astype(F32)
        result[slot] = total.astype(result.dtype)


def finish_late(own, p1, p2, p3, *refs):
    grad_qkv, grad_out = refs[:2]
    vectors, blocks = refs[2:-1], refs[-1]
    width = grad_out.shape[0]
    member = lax.axis_index("tensor")
    for distance, piece in enumerate((own, p1, p2, p3)):
        blocks[member ^ distance] = piece[0:width, :].astype(F32)
    for q in range(3):
        grad_qkv[:, q * width : (q + 1) * width] = blocks[q]
    grad_out[...] = blocks[3]
    tail = own[width : width + 16, :].astype(F32)
    for i, vector in enumerate(vectors):
        vector[...] = tail[i : i + 1, :]


def finish_filters(steps, *refs):
    parts, (grad_conv, grad_proj, work) = refs[:-3], refs[-3:]
    where = lax.axis_index("dp")
    depth = grad_conv.shape[0]
    start = 0
    for step, value, other in zip(steps, parts[::2], parts[1::2]):
        half = value.shape[0]
        bit = (where // step) % 2
        work[at(start + bit * half, half), :] = value[...]
        work[at(start + (1 - bit) * half, half), :] = other[...]
        start += 2 * half
    grad_conv[...] = work[0:depth, :].astype(F32)
    grad_proj[...] = work[depth:, :].astype(F32)


def shards(
    frames,
    lengths,
    w_qkv,
    w_out,
    b_out,
    gain_one,
    shift_one,
    w_conv,
    b_conv,
    w_proj,
    b_proj,
    gain_two,
    shift_two,
    cotangent,
):
    count, quarter, width = frames.shape
    length = 4 * quarter
    taps = w_conv.shape[0]
    depth = taps * width
    filters = 4 * w_conv.shape[2]
    padded = length + BLOCK
    space = 2 * length
    limit = 7 * BLOCK
    smem = pl.BlockSpec(memory_space=pltpu.SMEM)
    vmem = pl.BlockSpec(memory_space=pltpu.VMEM)
    anywhere = pl.BlockSpec(memory_space=pl.ANY)
    shape = jax.ShapeDtypeStruct
    dp_size = lax.axis_size("dp")
    dp_place = lax.axis_index("dp")
    b_out, gain_one, shift_one, b_proj, gain_two, shift_two = [
        v[None] for v in (b_out, gain_one, shift_one, b_proj, gain_two, shift_two)
    ]

    def hop(value, distance):
        return lax.ppermute(value, "tensor", [(i, i ^ distance) for i in range(4)])

    def dp_hop(value, distance):
        return lax.ppermute(value, "dp", [(i, i ^ distance) for i in range(dp_size)])

    def after(value, *others):
        return lax.optimization_barrier((value,) + others)[0]

    pack_rows = (depth + width + 64) // 64 * 64
    piece = pack_rows // 4
    pack, *frame_picks, own_piece = pl.pallas_call(
        begin_group,
        out_shape=[shape((pack_rows, width), BF16)]
        + [shape((n, quarter, width), BF16) for n in (2, 2, 3)]
        + [shape((piece, width), BF16)],
        in_specs=[smem] + [vmem] * 4,
        out_specs=[vmem] * 5,
        compiler_params=params(),
        name="begin_group",
    )(lengths, frames, w_conv.reshape(depth, width), w_proj, b_conv[None])
    far0 = hop(own_piece, 2)
    near_pack = hop(pack, 1)
    cot_picks = pl.pallas_call(
        pick,
        out_shape=[shape((n, quarter, width), BF16) for n in (2, 2, 3)],
        in_specs=[smem, vmem],
        out_specs=[vmem] * 3,
        compiler_params=params(),
        name="pick_cotangent",
    )(lengths, after(cotangent, *frame_picks))
    far0, near_pack, *cot_picks = lax.optimization_barrier((far0, near_pack, *cot_picks))
    far_frames = hop(frame_picks[2], 2)
    near_frames = hop(frame_picks[1], 1)
    far1, far2, near_frames = lax.optimization_barrier((dp_hop(far0, 1), dp_hop(far0, 2), near_frames))
    last = [dp_hop(far2[: piece // 2], 1), dp_hop(far1[piece // 2 :], 2)]
    frame_parts = [frame_picks[0], near_frames, far_frames, hop(far_frames[:2], 1)]
    cot_near = hop(after(cot_picks[1], far_frames), 1)
    cot_far = hop(after(cot_picks[2], far_frames), 2)

    rows = length + length // 2
    normed, stats, mixed = pl.pallas_call(
        attention_forward,
        out_shape=(
            shape((space, width), F32),
            shape((space, 128), F32),
            shape((space, width), BF16),
        ),
        in_specs=[smem] + [vmem] * 7,
        out_specs=[anywhere] * 3,
        scratch_shapes=[
            pltpu.VMEM((2, padded, width), BF16),
            pltpu.VMEM((2, padded, 2 * width), BF16),
            pltpu.VMEM((2, 2, length, width), BF16),
            pltpu.VMEM((2, length, width), F32),
            pltpu.VMEM((2, length, 128), F32),
            pltpu.VMEM((2, length, width), BF16),
            pltpu.SemaphoreType.DMA((2, 3, length // BLOCK)),
        ],
        compiler_params=params(),
        cost_estimate=cost(1e6, 1e5),
        name="attention_forward",
    )(after(lengths, near_pack), *near(*frame_parts), w_qkv, w_out, b_out)

    *last, cot_near, cot_far, normed = lax.optimization_barrier((*last, cot_near, cot_far, normed))
    cot_parts = [cot_picks[0], cot_near, cot_far, hop(cot_far[:2], 1)]
    far_pack = jnp.concatenate([far0, far1, far2] + last)
    far_near_pack = hop(far_pack, 1)
    packs = (pack, near_pack, far_pack, far_near_pack)

    chunk_rows = (depth + width) // 2
    block_count = limit // BLOCK
    result = pl.pallas_call(
        feed_forward,
        out_shape=[shape((n, quarter, width), BF16) for n in (2, 2, 4)]
        + [shape((2, 4, chunk_rows // 2, width), BF16)] * 2
        + [
            shape((limit, filters), BF16),
            shape((limit, width), F32),
            shape((8, width), F32),
            shape((8, filters), F32),
        ],
        in_specs=[smem, anywhere] + [vmem] * 4 + [anywhere] * 4 + [vmem] * 5,
        out_specs=[vmem] * 3 + [anywhere] * 4 + [vmem] * 2,
        scratch_shapes=[
            pltpu.VMEM((pack_rows, filters), BF16),
            pltpu.VMEM((limit, width), F32),
            pltpu.VMEM((limit + 2 * HALO, width), F32),
            pltpu.VMEM((limit, depth), BF16),
            pltpu.VMEM((2, BLOCK, filters), F32),
            pltpu.VMEM((BLOCK, filters), F32),
            pltpu.VMEM((limit, filters), BF16),
            pltpu.VMEM((limit, width), BF16),
            pltpu.VMEM((limit, filters), BF16),
            pltpu.VMEM((limit, width), F32),
            pltpu.VMEM((4, depth + width, width), BF16),
            pltpu.VMEM((2, padded, width), BF16),
            pltpu.VMEM((space, width), BF16),
            pltpu.VMEM((space, width), BF16),
            pltpu.VMEM((padded, width), BF16),
            pltpu.SemaphoreType.DMA((FILTER_COPIES,)),
            pltpu.SemaphoreType.DMA((block_count,)),
            pltpu.SemaphoreType.DMA((2, block_count)),
            pltpu.SemaphoreType.DMA((taps + 1, 4, width // (chunk_rows // 10))),
        ],
        compiler_params=pltpu.CompilerParams(vmem_limit_bytes=50 * 2**20),
        cost_estimate=cost(1e6, 1e5),
        name="feed_forward",
    )(lengths, normed, *near(*cot_parts, *packs), gain_one, shift_one, b_proj, gain_two, shift_two)
    (out_own, out_near, out_far), kept, sent = result[:3], result[3], result[4]
    d_hidden, dz_two, small_two, conv_bias = result[5:]

    def add(a, b):
        return (a.astype(F32) + b.astype(F32)).astype(BF16)

    def total(*parts):
        return sum(part.astype(F32) for part in parts).astype(BF16)

    def halves(value, step):
        half = value.shape[-2] // 2
        bit = (dp_place // step) % 2
        axis = value.ndim - 2
        parts = value.reshape(value.shape[:-2] + (2, half, width))
        keep = lax.dynamic_index_in_dim(parts, bit, axis, keepdims=False)
        send = lax.dynamic_index_in_dim(parts, 1 - bit, axis, keepdims=False)
        return keep, dp_hop(send, step)

    def joined(value, other, step):
        bit = (dp_place // step) % 2
        return jnp.where(bit == 0, jnp.concatenate([value, other]), jnp.concatenate([other, value]))

    def collected(places, parts, dtype, name):
        return pl.pallas_call(
            functools.partial(collect, places),
            out_shape=shape((count, quarter, width), dtype),
            in_specs=[smem] + [vmem] * len(parts),
            out_specs=vmem,
            compiler_params=params(),
            name=name,
        )(lengths, *near(*parts))

    more = [2**i for i in range(2, 20) if 2**i < dp_size]
    got = hop(sent, 1)
    out_far = hop(out_far, 2)
    out_near = hop(out_near, 1)

    d_first = pl.pallas_call(
        conv_backward,
        out_shape=shape((limit, width), F32),
        in_specs=[smem] + [anywhere] * 6,
        out_specs=anywhere,
        scratch_shapes=[
            pltpu.VMEM((pack_rows, filters), BF16),
            pltpu.VMEM((limit, filters), BF16),
            pltpu.VMEM((limit, width), F32),
            pltpu.VMEM((limit, width), F32),
            pltpu.VMEM((limit + HALO, width), F32),
            pltpu.SemaphoreType.DMA((FILTER_COPIES,)),
            pltpu.SemaphoreType.DMA((2, block_count)),
            pltpu.SemaphoreType.DMA((1, block_count)),
        ],
        compiler_params=params(),
        cost_estimate=cost(1e6, 1e5),
        name="conv_backward",
    )(lengths, d_hidden, *packs, dz_two)

    def attention_back(part, arrays, inputs, ties):
        late_rows = width + SMALL_ROWS
        if part:
            out_shapes = [shape((late_rows, width), BF16)] * 4
            out_specs = [vmem] * 4
            more_scratch = [pltpu.VMEM((4, width, width), BF16)]
        else:
            out_shapes = [
                shape((width, 3 * width), F32),
                shape((space, width), F32),
                shape((space, width), BF16),
                shape((space, 128), F32),
                shape((width, width), F32),
                shape((8, width), F32),
            ]
            out_specs = [vmem] + [anywhere] * 3 + [vmem] * 2
            more_scratch = [
                pltpu.VMEM((limit, width), F32),
                pltpu.VMEM((limit, width), F32),
                pltpu.VMEM((limit, 128), F32),
                pltpu.VMEM((limit, width), BF16),
                pltpu.SemaphoreType.DMA((3, block_count)),
            ]
        held = length if part else limit
        return pl.pallas_call(
            functools.partial(attention_backward, part),
            out_shape=[shape((quarter, width), BF16)] * 2 + [shape((2, quarter, width), BF16)] + out_shapes,
            in_specs=[smem] + [anywhere] * 4 + [vmem] + [anywhere] * len(arrays) + [vmem] * len(inputs),
            out_specs=[vmem] * 3 + out_specs,
            scratch_shapes=[
                pltpu.VMEM((padded, width), BF16),
                pltpu.VMEM((padded, 3 * width), BF16),
                pltpu.VMEM((padded, 3 * width), BF16),
                pltpu.VMEM((length, width), F32),
                pltpu.VMEM((length, width), F32),
                pltpu.VMEM((padded, width), F32),
                pltpu.VMEM((held, width), F32),
                pltpu.VMEM((held, width), BF16),
                pltpu.VMEM((held, 128), F32),
                pltpu.SemaphoreType.DMA((4,)),
                pltpu.SemaphoreType.DMA((4, block_count)),
            ]
            + more_scratch,
            compiler_params=params(),
            cost_estimate=cost(1e6, 1e5),
            name=f"attention_backward_{'ac'[part]}",
        )(after(lengths, *ties), *frame_parts, w_qkv, *arrays, *inputs)

    got, out_far, out_near = lax.optimization_barrier((got, out_far, out_near, d_first))[:3]
    send_x, send_y = total(kept[1, :2], got[1, :2]), total(kept[1, 2:], got[1, 2:])
    got_x, got_y = dp_hop(send_x, 1), hop(send_y, 2)
    out_beyond = hop(out_far[2:], 1)
    a_own, a_near, a_far, grad_qkv, dz_one, d_mixed, soft, grad_out, small = attention_back(
        0, [d_first, normed, stats, mixed], [w_out, gain_one, small_two], [send_x, send_y]
    )
    got_x, got_y, out_beyond = lax.optimization_barrier((got_x, got_y, out_beyond, grad_qkv))[:3]
    send_x, send_y = total(kept[0, 1], got[0, 1], got_x[1]), total(kept[0, 3], got[0, 3], got_y[1])
    next_x, next_y = hop(send_x, 2), dp_hop(send_y, 2)
    a_far = hop(a_far, 2)
    c_own, c_near, c_far, late0, late1, late2, late3 = attention_back(
        1, [dz_one, d_mixed, soft], [grad_qkv, grad_out, small, conv_bias], [send_x, send_y]
    )
    next_x, next_y = lax.optimization_barrier((next_x, next_y, late0))[:2]
    state = [total(kept[0, 0], got[0, 0], got_x[0], next_x), total(kept[0, 2], got[0, 2], got_y[0], next_y)]

    late_parts = [hop(after(part, *state), d) for d, part in ((1, late1), (2, late2), (3, late3))]
    moving = [halves(state[0], 2), halves(state[1], 1)]
    late = total(late0, *late_parts)
    state = jnp.concatenate([add(keep, after(other, late)) for keep, other in moving])
    c_far = hop(after(c_far, late), 2)
    others = [dp_hop(state, step) for step in more[:1]]
    late_parts = [dp_hop(late, step) for step in (1, 2, 3)]
    output = collected(
        [((0, 0), (0, 1)), ((1, 0), (1, 1)), ((2, 0), (2, 1)), ((3, 0), (3, 1))],
        [after(out_own, late), out_near, out_far, out_beyond],
        BF16,
        "collect_output",
    )
    *others, p1, p2, p3, output, c_far = lax.optimization_barrier((*others, *late_parts, output, c_far))
    late = total(late, p1, p2, p3)
    for other in others:
        state = add(state, other)
    for step in more[1:]:
        state = add(state, dp_hop(state, step))
    state = jnp.split(state, 2)
    backs = [[2, 1], [1, 2]]
    others = [dp_hop(value, back[0]) for value, back in zip(state, backs)]
    near_grads = hop(after(jnp.stack([a_near, c_near, a_far[1], c_far[1]]), late), 1)
    for step in more:
        late = add(late, dp_hop(late, step))
    *others, late, near_grads = lax.optimization_barrier((*others, late, near_grads))
    state = [joined(value, other, back[0]) for value, other, back in zip(state, others, backs)]
    last = [back[-1] for back in backs]
    others = [dp_hop(value, step) for value, step in zip(state, last)]
    blocks = [hop(late[:width], d) for d in (1, 2, 3)]
    d_frames = collected(
        [((0, None), (1, None)), ((2, 0), (2, 1)), ((3, 0), (4, 0)), ((2, 2), (2, 3))],
        [a_own, c_own, near_grads, a_far, c_far],
        F32,
        "collect_grad",
    )
    grad_conv, grad_proj = pl.pallas_call(
        functools.partial(finish_filters, last),
        out_shape=(shape((depth, width), F32), shape((width, width), F32)),
        in_specs=[vmem] * 4,
        out_specs=[vmem] * 2,
        scratch_shapes=[pltpu.VMEM((depth + width, width), BF16)],
        compiler_params=params(),
        name="finish_filters",
    )(*near(*[part for pair in zip(state, others) for part in pair]))
    grad_qkv, grad_out, *vectors = pl.pallas_call(
        finish_late,
        out_shape=[shape((width, 3 * width), F32), shape((width, width), F32)] + [shape((1, width), F32)] * 7,
        in_specs=[vmem] * 4,
        out_specs=[vmem] * 9,
        scratch_shapes=[pltpu.VMEM((4, width, width), F32)],
        compiler_params=params(),
        name="finish_late",
    )(*near(late, *blocks))
    vectors = [v.reshape(width) for v in vectors]
    return (
        output,
        d_frames,
        grad_qkv,
        grad_out,
        vectors[0],
        vectors[1],
        vectors[2],
        grad_conv.reshape(w_conv.shape),
        vectors[6],
        grad_proj,
        vectors[3],
        vectors[4],
        vectors[5],
    )


def solution(mesh):
    return jax.shard_map(
        shards,
        mesh=mesh,
        in_specs=(
            P("dp", "tensor", None),
            P("dp"),
            P(),
            P(),
            P(),
            P(),
            P(),
            P(None, None, "tensor"),
            P("tensor"),
            P("tensor", None),
            P(),
            P(),
            P(),
            P("dp", "tensor", None),
        ),
        out_specs=(
            P("dp", "tensor", None),
            P("dp", "tensor", None),
            P(),
            P(),
            P(),
            P(),
            P(),
            P(None, None, "tensor"),
            P("tensor"),
            P("tensor", None),
            P(),
            P(),
            P(),
        ),
        check_vma=False,
    )
```

```python
import functools
import itertools

import jax
import jax.experimental.pallas as pl
import jax.experimental.pallas.tpu as pltpu
import jax.numpy as jnp
import numpy as np
from jax import lax
from jax.sharding import PartitionSpec as P


EPSILON = 1e-05
F32 = jnp.float32
BF16 = jnp.bfloat16
HALO = 16
BLOCK = 256
MASKED = -1e30
GELU_A = float(np.sqrt(2.0 / np.pi))
GELU_B = 0.044715
LOG2E = float(np.log2(np.e))
VMEM_LIMIT = 54 * 2**20
SMALL_ROWS = 16


def near(*arrays):
    return [pltpu.with_memory_space_constraint(array, pltpu.VMEM) for array in arrays]


def params(**more):
    return pltpu.CompilerParams(vmem_limit_bytes=VMEM_LIMIT, **more)


def cost(flops, size):
    return pl.CostEstimate(flops=int(flops), bytes_accessed=int(size), transcendentals=0)


def dot(a, b):
    return jnp.dot(a, b, preferred_element_type=F32)


def dot_nt(a, b):
    return lax.dot_general(a, b, (((1,), (1,)), ((), ())), preferred_element_type=F32)


def dot_tn(a, b):
    return lax.dot_general(a, b, (((0,), (0,)), ((), ())), preferred_element_type=F32)


def at(start, size, step=HALO):
    return pl.ds(pl.multiple_of(start, step), size)


def up(value, step=HALO):
    return ((value + (step - 1)) // step) * step


def choose(index, options):
    result = options[-1]
    for i, option in enumerate(options[:-1]):
        result = jnp.where(index == i, option, result)
    return result


def plan(lengths):
    keys = [lengths[i] * 8 + i for i in range(6)]
    best, triples = None, None
    for pair in itertools.combinations(range(1, 6), 2):
        mine = (0,) + pair
        rest = tuple(i for i in range(6) if i not in mine)
        gap = jnp.abs(sum(lengths[i] for i in mine) - sum(lengths[i] for i in rest))
        option = [keys[i] for i in mine + rest]
        if best is None:
            best, triples = gap, option
        else:
            better = gap < best
            best = jnp.where(better, gap, best)
            triples = [jnp.where(better, new, old) for new, old in zip(option, triples)]
    whole, shared = [], []
    for a, b, c in (triples[:3], triples[3:]):
        a, b = jnp.maximum(a, b), jnp.minimum(a, b)
        a, c = jnp.maximum(a, c), jnp.minimum(a, c)
        b, c = jnp.maximum(b, c), jnp.minimum(b, c)
        whole += [a, b]
        shared.append(c)
    return whole, shared


class Rows:
    def __init__(self, lengths, length):
        self.member = lax.axis_index("tensor")
        whole, shared = plan(lengths)
        self.whole, self.shared = whole, shared
        role = self.member % 2
        second = self.member >= 2
        key_a = choose(self.member, whole)
        self.len_a = key_a // 8
        self.len_c = jnp.where(second, shared[1], shared[0]) // 8
        first_len = jnp.where(second, whole[2], whole[0]) // 8
        other_len = jnp.where(second, whole[3], whole[1]) // 8
        split = (other_len + self.len_c - first_len) // 2
        split = jnp.maximum((split + HALO // 2) // HALO * HALO, HALO)
        starts = role == 0
        self.own_from = jnp.where(starts, 0, split)
        self.own_to = jnp.where(starts, split, length)
        self.window = jnp.where(starts, 0, split - HALO)
        self.end = jnp.where(starts, jnp.minimum(split + HALO, self.len_c), self.len_c)
        self.rows_a = up(self.len_a + 4)
        self.rows_c = jnp.maximum(up(self.end) - self.window, 0)
        self.tiles_a = (self.len_a + BLOCK - 1) // BLOCK
        self.tiles_c = (self.rows_c + BLOCK - 1) // BLOCK
        self.blocks = (self.rows_a + self.rows_c + BLOCK - 1) // BLOCK
        self.halo = self.rows_a + jnp.where(starts, split, 0)

    def masks(self, start, size):
        row = start + lax.broadcasted_iota(jnp.int32, (size, 1), 0)
        in_a = row < self.rows_a
        frame = jnp.where(in_a, row, row - self.rows_a + self.window)
        live = frame < jnp.where(in_a, self.len_a, self.end)
        inside = (frame >= self.own_from) & (frame < self.own_to)
        return live, live & (in_a | inside)

    def frames_at(self, part, index):
        return at(BLOCK * index + (self.window if part else 0), BLOCK)

    def base(self, part, index):
        return BLOCK * index + (self.rows_a if part else 0)


def piece_index(piece, part):
    return part if piece.shape[0] == 2 else 2 - part


def place(member, pieces, target):
    quarter = pieces[0].shape[1]
    for distance, piece in enumerate(pieces):
        rows = at((member ^ distance) * quarter, quarter, quarter)
        for part in range(2):
            target[part, rows, :] = piece[piece_index(piece, part)]


def pick(lengths, source, *targets):
    member = lax.axis_index("tensor")
    whole, shared = plan(lengths)
    for distance, target in enumerate(targets):
        there = member ^ distance
        if target.shape[0] == 3:
            target[0] = source[choose(there ^ 1, whole) % 8]
        target[piece_index(target, 0)] = source[choose(there, whole) % 8]
        target[piece_index(target, 1)] = source[jnp.where(there >= 2, shared[1], shared[0]) % 8]


def begin_group(lengths, source, w_conv, w_proj, b_conv, pack, p0, p1, p2, part):
    depth, width = w_conv.shape
    pack[0:depth, :] = w_conv[...]
    pack[depth : depth + width, :] = w_proj[...]
    high = b_conv[...].astype(BF16)
    rest = (b_conv[...] - high.astype(F32)).astype(BF16)
    last = depth + width
    pack[last : last + HALO, :] = jnp.broadcast_to(high, (HALO, width))
    pack[last + HALO :, :] = jnp.broadcast_to(rest, (pack.shape[0] - last - HALO, width))
    piece = part.shape[0]
    part[...] = pack[at((lax.axis_index("dp") % 4) * piece, piece), :]
    pick(lengths, source, p0, p1, p2)


def softmax_parts(rows, part, length):
    return (rows.len_c if part else rows.len_a), lax.broadcasted_iota(jnp.int32, (1, length), 1)


def mask_keys(scores, column, limit):
    half = scores.shape[1] // 2
    tail = jnp.where(column[:, half:] < limit, scores[:, half:], MASKED)
    return jnp.concatenate([scores[:, :half], tail], axis=1)


def attention_forward(
    lengths, r0, r1, r2, r3, w_qkv, w_out, b_out, normed, stats, mixed, placed, qkv, valued, n_out, s_out, m_out, sems
):
    quarter = r0.shape[1]
    length = 4 * quarter
    width = r0.shape[2]
    head = width // 2
    scale = head ** (-0.5) * LOG2E
    rows = Rows(lengths, length)
    spare = placed.shape[1] - length
    placed[:, length:, :] = jnp.zeros((2, spare, width), BF16)
    place(rows.member, (r0, r1, r2, r3), placed)
    for part in range(2):
        for h in range(2):
            valued[part, h, :, head:] = jnp.ones((length, head), BF16)

    def project(index, carry):
        here = at(index * BLOCK, BLOCK, BLOCK)
        for part in range(2):
            value = dot(placed[part, here, :], w_qkv[...]).astype(BF16)
            qkv[part, here, :] = value[:, : 2 * width]
            for h in range(2):
                valued[part, h, here, :head] = value[:, 2 * width + h * head : 2 * width + (h + 1) * head]
        return carry

    lax.fori_loop(0, length // BLOCK, project, 0)
    qkv[:, length:, :] = jnp.zeros((2, spare, 2 * width), BF16)
    lane = lax.broadcasted_iota(jnp.int32, (1, 128), 1)

    def copies(part, index):
        there = at(rows.base(part, index), BLOCK)
        here = at(index * BLOCK, BLOCK, BLOCK)
        pairs = ((n_out, normed), (s_out, stats), (m_out, mixed))
        return [
            pltpu.make_async_copy(source.at[part, here], target.at[there], sems.at[part, i, index])
            for i, (source, target) in enumerate(pairs)
        ]

    def tile(part, index, carry):
        frames_at = rows.frames_at(part, index)
        here = at(index * BLOCK, BLOCK, BLOCK)
        limit, column = softmax_parts(rows, part, length)
        mixtures, logs = [], []
        for h in range(2):
            low, high = h * head, (h + 1) * head
            scores = dot_nt(qkv[part, frames_at, low:high], qkv[part, :length, width + low : width + high])
            scores = mask_keys(scores, column, limit)
            highest = jnp.max(scores, axis=-1, keepdims=True) * scale
            exponent = jnp.exp2(scores * scale - highest).astype(BF16)
            summed = dot(exponent, valued[part, h])
            total = summed[:, head : head + 1]
            mixtures.append((summed[:, :head] / total).astype(BF16))
            logs.append(highest + jnp.log2(total))
        mixture = jnp.concatenate(mixtures, axis=1)
        m_out[part, here, :] = mixture
        residual = placed[part, frames_at, :].astype(F32) + dot(mixture, w_out[...]) + b_out[...]
        centred = residual - jnp.mean(residual, axis=-1, keepdims=True)
        inverse = lax.rsqrt(jnp.mean(centred * centred, axis=-1, keepdims=True) + EPSILON)
        n_out[part, here, :] = centred * inverse
        s_out[part, here, :] = jnp.where(lane == 0, logs[0], jnp.where(lane == 1, logs[1], inverse))
        for copy in copies(part, index):
            copy.start()
        return carry

    def finish(part, index, carry):
        for copy in copies(part, index):
            copy.wait()
        return carry

    for part, count in enumerate((rows.tiles_a, rows.tiles_c)):
        lax.fori_loop(0, count, functools.partial(tile, part), 0)
        lax.fori_loop(0, count, functools.partial(finish, part), 0)


def gelu_pair(x):
    square = x * x
    t = jnp.tanh(GELU_A * x * (1.0 + GELU_B * square))
    half = 0.5 * (1.0 + t)
    slope = half + (0.5 * GELU_A) * x * (1.0 - t * t) * (1.0 + 3.0 * GELU_B * square)
    return x * half, slope


def load_filters(near, far, target, sems):
    width = near[0].shape[1]
    piece = near[0].shape[0] // 4
    shift = lax.axis_index("dp") % 4
    copies = []
    for j, source in enumerate(near):
        copies.append((source, target.at[:, pl.ds(j * width, width)]))
    for j, source in enumerate(far):
        for i in range(4):
            there = at((shift ^ i) * piece, piece)
            part = pl.ds((2 + j) * width, width)
            copies.append((source.at[pl.ds(i * piece, piece)], target.at[there, part]))
    copies = [
        pltpu.make_async_copy(source, there, sems.at[i]) for i, (source, there) in enumerate(copies)
    ]
    for copy in copies:
        copy.start()
    return copies


FILTER_COPIES = 10


def feed_forward(
    lengths,
    normed,
    c0,
    c1,
    c2,
    c3,
    pack0,
    pack1,
    far0,
    far1,
    gain_one,
    shift_one,
    b_proj,
    gain_two,
    shift_two,
    o0,
    o1,
    o_far,
    kept,
    sent,
    d_hidden_out,
    dz_out,
    conv_out,
    small,
    conv_bias,
    weights,
    units,
    first,
    columns,
    hidden,
    slope,
    active,
    d_branch,
    d_hidden,
    dz_two,
    grads,
    cot_frames,
    cot_rows,
    out_rows,
    out_c,
    load_sems,
    unit_sems,
    out_sems,
    grad_sems,
    conv_sem,
):
    quarter, width = c0.shape[1:]
    length = 4 * quarter
    filters = weights.shape[1]
    taps = columns.shape[1] // width
    depth = taps * width
    reach = taps // 2
    loads = load_filters((pack0, pack1), (far0, far1), weights, load_sems)
    rows = Rows(lengths, length)
    blocks = rows.blocks

    def unit_copy(index):
        here = at(index * BLOCK, BLOCK, BLOCK)
        return pltpu.make_async_copy(normed.at[here], units.at[here], unit_sems.at[index])

    def start_unit(index, carry):
        unit_copy(index).start()
        return carry

    lax.fori_loop(0, blocks, start_unit, 0)
    place(rows.member, (c0, c1, c2, c3), cot_frames)
    cot_frames[:, length:, :] = jnp.zeros((2, cot_frames.shape[1] - length, width), BF16)
    cot_rows[0:length, :] = cot_frames[0, 0:length, :]

    def gather_cot(index, carry):
        cot_rows[at(rows.base(1, index), BLOCK), :] = cot_frames[1, rows.frames_at(1, index), :]
        return carry

    lax.fori_loop(0, rows.tiles_c, gather_cot, 0)
    out_rows[...] = jnp.zeros(out_rows.shape, BF16)
    small[...] = jnp.zeros(small.shape, F32)
    conv_bias[...] = jnp.zeros(conv_bias.shape, F32)

    first[0:HALO, :] = jnp.zeros((HALO, width), F32)

    def make_first(index, carry):
        base = index * BLOCK
        unit_copy(index).wait()
        live, _ = rows.masks(base, BLOCK)
        value = units[at(base, BLOCK), :] * gain_one[...] + shift_one[...]
        first[at(base + HALO, BLOCK), :] = jnp.where(live, value, 0.0)
        return carry

    lax.fori_loop(0, blocks, make_first, 0)
    first[at(blocks * BLOCK + HALO, HALO), :] = jnp.zeros((HALO, width), F32)

    def make_columns(index, carry):
        base = index * BLOCK
        around = first[at(base + HALO - 8, BLOCK + 16, 8), :]
        for k in range(taps):
            columns[at(base, BLOCK, BLOCK), k * width : (k + 1) * width] = around[
                8 - reach + k : 8 - reach + k + BLOCK
            ].astype(BF16)
        return carry

    lax.fori_loop(0, blocks, make_columns, 0)
    for copy in loads:
        copy.wait()
    conv_copy = pltpu.make_async_copy(weights.at[pl.ds(0, depth)], conv_out, conv_sem.at[0])
    conv_copy.start()

    def out_copies(index):
        here = at(index * BLOCK, BLOCK, BLOCK)
        return [
            pltpu.make_async_copy(d_hidden.at[here], d_hidden_out.at[here], out_sems.at[0, index]),
            pltpu.make_async_copy(dz_two.at[here], dz_out.at[here], out_sems.at[1, index]),
        ]

    def conv(index, target):
        target[...] = dot(columns[at(index * BLOCK, BLOCK, BLOCK), :], weights[0:depth, :])

    def rest(index, source):
        base = index * BLOCK
        here = at(base, BLOCK, BLOCK)
        live, own = rows.masks(base, BLOCK)
        branch = jnp.zeros((BLOCK, width), F32)
        for j in range(filters // width):
            part = slice(j * width, (j + 1) * width)
            bias = weights[depth + width : depth + width + 1, part].astype(F32) + weights[
                depth + width + 16 : depth + width + 17, part
            ].astype(F32)
            value, derivative = gelu_pair(source[:, part] + bias)
            value = value.astype(BF16)
            active[here, part] = value
            slope[:, part] = derivative
            branch = branch + dot(value, weights[depth : depth + width, part])
        residual = first[at(base + HALO, BLOCK), :] + branch + b_proj[...]
        centred = residual - jnp.mean(residual, axis=-1, keepdims=True)
        inverse = lax.rsqrt(jnp.mean(centred * centred, axis=-1, keepdims=True) + EPSILON)
        normed_two = centred * inverse
        out_rows[here, :] = jnp.where(own, normed_two * gain_two[...] + shift_two[...], 0.0).astype(BF16)
        upstream = jnp.where(live, cot_rows[here, :].astype(F32), 0.0)
        counted = jnp.where(own, upstream, 0.0)
        scaled = upstream * gain_two[...]
        dz = inverse * (
            scaled
            - jnp.mean(scaled, axis=-1, keepdims=True)
            - normed_two * jnp.mean(scaled * normed_two, axis=-1, keepdims=True)
        )
        dz_two[here, :] = dz
        small[3:4, :] += jnp.sum(jnp.where(own, dz, 0.0), axis=0, keepdims=True)
        small[4:5, :] += jnp.sum(counted * normed_two, axis=0, keepdims=True)
        small[5:6, :] += jnp.sum(counted, axis=0, keepdims=True)
        low = dz.astype(BF16)
        d_branch[here, :] = jnp.where(own, low, jnp.zeros_like(low))
        for j in range(filters // width):
            part = slice(j * width, (j + 1) * width)
            grad = dot_nt(low, weights[depth : depth + width, part]) * slope[:, part]
            conv_bias[0:1, part] += jnp.sum(jnp.where(own, grad, 0.0), axis=0, keepdims=True)
            d_hidden[here, part] = grad.astype(BF16)
        for copy in out_copies(index):
            copy.start()

    even, odd = hidden.at[0], hidden.at[1]
    conv(0, even)

    def step(pair, carry):
        index = 2 * pair
        conv(index + 1, odd)
        rest(index, even)
        conv(index + 2, even)
        rest(index + 1, odd)
        return carry

    lax.fori_loop(0, (blocks - 1) // 2, step, 0)

    @pl.when(blocks % 2 == 1)
    def _():
        rest(blocks - 1, even)

    @pl.when(blocks % 2 == 0)
    def _():
        conv(blocks - 1, odd)
        rest(blocks - 2, even)
        rest(blocks - 1, odd)

    columns[at(rows.halo, HALO), :] = jnp.zeros((HALO, columns.shape[1]), BF16)

    per_chunk = (taps + 1) // 2

    x_bit, z_bit = lax.axis_index("dp") % 2, (lax.axis_index("dp") // 2) % 2
    half_rows = kept.shape[2]
    piece = half_rows // 5

    def grad_copies(k, chunk):
        copies = []
        for u in range(width // piece):
            row = (k - chunk * per_chunk) * width + u * piece
            half = row // half_rows
            there = at(row - half * half_rows, piece, piece)
            here = at(k * width + u * piece, piece, piece)
            for j in range(filters // width):
                place = (half ^ x_bit, j // 2) if chunk == 0 else (j // 2, 2 + (half ^ z_bit))
                target = (kept, sent)[j % 2].at[place[0], place[1], there]
                copies.append(pltpu.make_async_copy(grads.at[j, here], target, grad_sems.at[k, j, u]))
        return copies

    for count in range(4, active.shape[0] // BLOCK + 1):

        @pl.when(blocks == count)
        def _():
            n = count * BLOCK

            def tap(k, carry):
                here = at(k * width, width, width)
                value = dot_tn(columns[0:n, here], d_hidden[0:n, :]).astype(BF16)
                for j in range(filters // width):
                    grads[j, here, :] = value[:, j * width : (j + 1) * width]
                for chunk in range(2):

                    @pl.when(k // per_chunk == chunk)
                    def _():
                        for copy in grad_copies(k, chunk):
                            copy.start()

                return carry

            lax.fori_loop(0, taps, tap, 0)
            value = dot_tn(active[0:n, :], d_branch[0:n, :]).astype(BF16)
            for j in range(filters // width):
                grads[j, depth:, :] = value[j * width : (j + 1) * width, :]
            for copy in grad_copies(taps, 1):
                copy.start()

    out_c[...] = jnp.zeros(out_c.shape, BF16)

    def scatter_out(index, carry):
        out_c[rows.frames_at(1, index), :] = out_rows[at(rows.base(1, index), BLOCK), :]
        return carry

    lax.fori_loop(0, rows.tiles_c, scatter_out, 0)
    for distance, (target, slot) in enumerate(((o0, 0), (o1, 0), (o_far, 0), (o_far, 2))):
        start = (rows.member ^ distance) * quarter
        there = at(start, quarter, quarter)
        row = start + lax.broadcasted_iota(jnp.int32, (quarter, 1), 0)
        value = out_rows[there, :]
        target[slot] = jnp.where(row < rows.len_a, value, jnp.zeros_like(value))
        target[slot + 1] = out_c[there, :]

    conv_copy.wait()

    def finish(index, carry):
        for copy in out_copies(index):
            copy.wait()
        return carry

    lax.fori_loop(0, blocks, finish, 0)

    def finish_grads(chunk, k, carry):
        for copy in grad_copies(k, chunk):
            copy.wait()
        return carry

    lax.fori_loop(0, per_chunk, functools.partial(finish_grads, 0), 0)
    lax.fori_loop(per_chunk, 2 * per_chunk, functools.partial(finish_grads, 1), 0)


def block_copies(pairs, sems, index):
    here = at(index * BLOCK, BLOCK, BLOCK)
    return [
        pltpu.make_async_copy(source.at[here], target.at[here], sems.at[i, index])
        for i, (source, target) in enumerate(pairs)
    ]


def conv_backward(
    lengths, d_hidden_in, conv, dz_in, d_first_out, weights, d_hidden, dz_two, d_first, sums, conv_sems, in_sems, out_sems
):
    width = dz_two.shape[1]
    taps = conv.shape[0] // width
    reach = taps // 2
    blocks = Rows(lengths, 4 * width).blocks
    conv_copies = [
        pltpu.make_async_copy(
            conv.at[pl.ds(k * width, width)], weights.at[pl.ds(k * width, width)], conv_sems.at[k]
        )
        for k in range(taps)
    ]
    into = ((d_hidden_in, d_hidden), (dz_in, dz_two))
    onto = ((d_first, d_first_out),)
    for copy in conv_copies:
        copy.start()

    def start(index, carry):
        for copy in block_copies(into, in_sems, index):
            copy.start()
        return carry

    lax.fori_loop(0, blocks, start, 0)
    sums[0:HALO, :] = jnp.zeros((HALO, width), F32)
    for copy in conv_copies:
        copy.wait()

    def back(index, carry):
        base = index * BLOCK
        for copy in block_copies(into, in_sems, index):
            copy.wait()
        value = d_hidden[at(base, BLOCK, BLOCK), :]
        total = jnp.zeros((BLOCK + HALO, width), F32)
        for k in range(taps):
            part = dot_nt(value, weights[k * width : (k + 1) * width, :])
            part = jnp.concatenate([part, jnp.zeros((HALO, width), F32)], axis=0)
            total = total + pltpu.roll(part, 8 - reach + k, axis=0)
        sums[at(base, HALO), :] += total[0:HALO]
        sums[at(base + HALO, BLOCK), :] = total[HALO:]
        return carry

    lax.fori_loop(0, blocks, back, 0)

    def finish(index, carry):
        base = index * BLOCK
        here = at(base, BLOCK, BLOCK)
        d_first[here, :] = dz_two[here, :] + sums[at(base + 8, BLOCK, 8), :]
        block_copies(onto, out_sems, index)[0].start()
        return carry

    lax.fori_loop(0, blocks, finish, 0)

    def drain(index, carry):
        block_copies(onto, out_sems, index)[0].wait()
        return carry

    lax.fori_loop(0, blocks, drain, 0)


def first_norm_backward(rows, ins, outs, blocks_in, blocks_out, in_sems, out_sems, w_out, gain_one, small, grad_out):
    d_first, normed, stats, mixed = blocks_in
    dz_one, d_mixed, soft = blocks_out
    into, onto = tuple(zip(ins, blocks_in)), tuple(zip(blocks_out, outs))
    width = normed.shape[1]
    head = width // 2
    lane = lax.broadcasted_iota(jnp.int32, (1, 128), 1)

    def block(index, carry):
        base = index * BLOCK
        here = at(base, BLOCK, BLOCK)
        for copy in block_copies(into, in_sems, index):
            copy.wait()
        _, own = rows.masks(base, BLOCK)
        total = jnp.where(own, d_first[here, :], 0.0)
        unit = jnp.where(own, normed[here, :], 0.0)
        kept = stats[here, :]
        inverse = kept[:, 2:3]
        scaled = total * gain_one[...]
        dz = inverse * (
            scaled
            - jnp.mean(scaled, axis=-1, keepdims=True)
            - unit * jnp.mean(scaled * unit, axis=-1, keepdims=True)
        )
        dz = jnp.where(own, dz, 0.0)
        dz_one[here, :] = dz
        small[0:1, :] += jnp.sum(dz, axis=0, keepdims=True)
        small[1:2, :] += jnp.sum(total * unit, axis=0, keepdims=True)
        small[2:3, :] += jnp.sum(total, axis=0, keepdims=True)
        low = dz.astype(BF16)
        upstream = dot_nt(low, w_out[...]).astype(BF16)
        d_mixed[here, :] = upstream
        mixture = mixed[here, :]
        mixture = jnp.where(own, mixture, jnp.zeros_like(mixture))
        grad_out[...] += dot_tn(mixture, low)
        product = upstream.astype(F32) * mixture.astype(F32)
        means = [jnp.sum(product[:, h * head : (h + 1) * head], axis=-1, keepdims=True) for h in range(2)]
        soft[here, :] = jnp.where(
            lane < 2, jnp.where(own, kept, -MASKED), jnp.where(lane == 2, means[0], means[1])
        )
        for copy in block_copies(onto, out_sems, index):
            copy.start()
        return carry

    lax.fori_loop(0, rows.blocks, block, 0)

    def finish(index, carry):
        for copy in block_copies(onto, out_sems, index):
            copy.wait()
        return carry

    return finish


def attention_backward(part, *refs):
    (lengths, r0, r1, r2, r3, w_qkv), refs = refs[:6], refs[6:]
    if part:
        in_refs, refs = refs[:3], refs[3:]
        inputs, refs = refs[:4], refs[4:]
        (g0, g1, g_far), refs = refs[:3], refs[3:]
        late, refs = refs[:4], refs[4:]
    else:
        in_refs, refs = refs[:4], refs[4:]
        (w_out, gain_one, small_two), refs = refs[:3], refs[3:]
        (g0, g1, g_far), refs = refs[:3], refs[3:]
        grad_qkv, refs = refs[0], refs[1:]
        out_refs, refs = refs[:3], refs[3:]
        (grad_out, small), refs = refs[:2], refs[2:]
    placed, qkv, d_proj, keys, values, frame_grads, dz_one, d_mixed, soft, place_sems, in_sems = refs[:11]
    quarter = r0.shape[1]
    length = 4 * quarter
    width = r0.shape[2]
    head = width // 2
    scale = head ** (-0.5)
    rows = Rows(lengths, length)
    tiles = rows.tiles_c if part else rows.tiles_a
    spare = placed.shape[0] - length
    places = [
        pltpu.make_async_copy(
            piece.at[piece_index(piece, part)],
            placed.at[at((rows.member ^ distance) * quarter, quarter, quarter)],
            place_sems.at[distance],
        )
        for distance, piece in enumerate((r0, r1, r2, r3))
    ]

    def copies(index):
        there = at(rows.base(part, index), BLOCK)
        here = at(index * BLOCK, BLOCK, BLOCK)
        return [
            pltpu.make_async_copy(source.at[there], target.at[here], in_sems.at[i, index])
            for i, (source, target) in enumerate(zip(in_refs, (dz_one, d_mixed, soft)))
        ]

    if part:

        def start(index, carry):
            for copy in copies(index):
                copy.start()
            return carry

        lax.fori_loop(0, tiles, start, 0)
    else:
        blocks_in, out_sems = refs[11:15], refs[15]

        def start(index, carry):
            for copy in block_copies(tuple(zip(in_refs, blocks_in)), in_sems, index):
                copy.start()
            return carry

        lax.fori_loop(0, rows.blocks, start, 0)
    for copy in places:
        copy.start()
    placed[length:, :] = jnp.zeros((spare, width), BF16)
    d_proj[...] = jnp.zeros(d_proj.shape, BF16)
    keys[...] = jnp.zeros(keys.shape, F32)
    values[...] = jnp.zeros(values.shape, F32)
    frame_grads[...] = jnp.zeros(frame_grads.shape, F32)
    if not part:
        small[...] = small_two[...]
        grad_out[...] = jnp.zeros(grad_out.shape, F32)
        finish = first_norm_backward(
            rows, in_refs, out_refs, blocks_in, (dz_one, d_mixed, soft), in_sems, out_sems, w_out, gain_one, small, grad_out
        )
    for copy in places:
        copy.wait()

    def project(index, carry):
        here = at(index * BLOCK, BLOCK, BLOCK)
        qkv[here, :] = dot(placed[here, :], w_qkv[...]).astype(BF16)
        return carry

    lax.fori_loop(0, length // BLOCK, project, 0)
    qkv[length:, :] = jnp.zeros((spare, 3 * width), BF16)

    def tile(index, carry):
        frames_at = rows.frames_at(part, index)
        here = at(index * BLOCK, BLOCK, BLOCK)
        if part:
            for copy in copies(index):
                copy.wait()
        limit, column = softmax_parts(rows, part, length)
        inside = BLOCK * index + lax.broadcasted_iota(jnp.int32, (BLOCK, 1), 0)
        inside = inside < (rows.rows_c if part else rows.rows_a)
        frame_grads[frames_at, :] = jnp.where(inside, dz_one[here, :], 0.0)
        for h in range(2):
            low, high = h * head, (h + 1) * head
            query = qkv[frames_at, low:high]
            key = qkv[:length, width + low : width + high]
            value = qkv[:length, 2 * width + low : 2 * width + high]
            upstream = d_mixed[here, low:high]
            upstream = jnp.where(inside, upstream, jnp.zeros_like(upstream))
            shift = jnp.where(inside, soft[here, h : h + 1], -MASKED)
            mean = jnp.where(inside, soft[here, 2 + h : 3 + h], 0.0)
            scores = mask_keys(dot_nt(query, key), column, limit)
            weights = jnp.exp2(scores * (scale * LOG2E) - shift)
            d_weights = dot_nt(upstream, value)
            d_scores = (weights * (d_weights - mean)).astype(BF16)
            d_proj[frames_at, low:high] = (dot(d_scores, key) * scale).astype(BF16)
            keys[:, low:high] += dot_tn(d_scores, query)
            values[:, low:high] += dot_tn(weights.astype(BF16), upstream)
        return carry

    lax.fori_loop(0, tiles, tile, 0)
    d_proj[0:length, width : 2 * width] = (keys[...] * scale).astype(BF16)
    d_proj[0:length, 2 * width : 3 * width] = values[...].astype(BF16)
    for distance, target in enumerate((g0, g1, g_far.at[0], g_far.at[1])):
        here = at((rows.member ^ distance) * quarter, quarter, quarter)
        target[...] = (frame_grads[here, :] + dot_nt(d_proj[here, :], w_qkv[...])).astype(BF16)
    grads = dot_tn(placed[0:length, :], d_proj[0:length, :])
    if part == 0:
        grad_qkv[...] = grads
        lax.fori_loop(0, rows.blocks, finish, 0)
        return
    blocks = refs[11]
    grad_before, grad_out, small, conv_bias = inputs
    grads = (grads + grad_before[...]).astype(BF16)
    for q in range(3):
        blocks[q, :, :] = grads[:, q * width : (q + 1) * width]
    blocks[3, :, :] = grad_out[...].astype(BF16)
    line = lax.broadcasted_iota(jnp.int32, (8, 1), 0)
    for j, target in enumerate(late):
        target[0:width, :] = blocks[rows.member ^ j]
        bias = conv_bias[0:1, j * width : (j + 1) * width]
        tail = jnp.where(line == 6, bias, small[...])
        tail = jnp.concatenate([tail, jnp.zeros((SMALL_ROWS - 8, width), F32)], axis=0)
        target[width : width + SMALL_ROWS, :] = tail.astype(BF16)


def collect(places, lengths, *refs):
    result = refs[-1]
    member = lax.axis_index("tensor")
    whole, shared = plan(lengths)

    def piece(place):
        array, index = place
        return refs[array][...] if index is None else refs[array][index]

    for distance in range(4):
        slot = choose(member ^ distance, whole) % 8
        result[slot] = piece(places[distance][0]).astype(result.dtype)
    for side in range(2):
        second = (member >= 2) == (side == 0)
        slot = jnp.where(second, shared[1], shared[0]) % 8
        total = piece(places[2 * side][1]).astype(F32) + piece(places[2 * side + 1][1]).astype(F32)
        result[slot] = total.astype(result.dtype)


def finish_late(own, p1, p2, p3, *refs):
    grad_qkv, grad_out = refs[:2]
    vectors, blocks = refs[2:-1], refs[-1]
    width = grad_out.shape[0]
    member = lax.axis_index("tensor")
    for distance, piece in enumerate((own, p1, p2, p3)):
        blocks[member ^ distance] = piece[0:width, :].astype(F32)
    for q in range(3):
        grad_qkv[:, q * width : (q + 1) * width] = blocks[q]
    grad_out[...] = blocks[3]
    tail = own[width : width + 16, :].astype(F32)
    for i, vector in enumerate(vectors):
        vector[...] = tail[i : i + 1, :]


def finish_filters(steps, *refs):
    parts, (grad_conv, grad_proj, work) = refs[:-3], refs[-3:]
    where = lax.axis_index("dp")
    depth = grad_conv.shape[0]
    start = 0
    for step, value, other in zip(steps, parts[::2], parts[1::2]):
        half = value.shape[0]
        bit = (where // step) % 2
        work[at(start + bit * half, half), :] = value[...]
        work[at(start + (1 - bit) * half, half), :] = other[...]
        start += 2 * half
    grad_conv[...] = work[0:depth, :].astype(F32)
    grad_proj[...] = work[depth:, :].astype(F32)


def shards(
    frames,
    lengths,
    w_qkv,
    w_out,
    b_out,
    gain_one,
    shift_one,
    w_conv,
    b_conv,
    w_proj,
    b_proj,
    gain_two,
    shift_two,
    cotangent,
):
    count, quarter, width = frames.shape
    length = 4 * quarter
    taps = w_conv.shape[0]
    depth = taps * width
    filters = 4 * w_conv.shape[2]
    padded = length + BLOCK
    space = 2 * length
    limit = 7 * BLOCK
    smem = pl.BlockSpec(memory_space=pltpu.SMEM)
    vmem = pl.BlockSpec(memory_space=pltpu.VMEM)
    anywhere = pl.BlockSpec(memory_space=pl.ANY)
    shape = jax.ShapeDtypeStruct
    dp_size = lax.axis_size("dp")
    dp_place = lax.axis_index("dp")
    b_out, gain_one, shift_one, b_proj, gain_two, shift_two = [
        v[None] for v in (b_out, gain_one, shift_one, b_proj, gain_two, shift_two)
    ]

    def hop(value, distance):
        return lax.ppermute(value, "tensor", [(i, i ^ distance) for i in range(4)])

    def dp_hop(value, distance):
        return lax.ppermute(value, "dp", [(i, i ^ distance) for i in range(dp_size)])

    def after(value, *others):
        return lax.optimization_barrier((value,) + others)[0]

    pack_rows = (depth + width + 64) // 64 * 64
    piece = pack_rows // 4
    pack, *frame_picks, own_piece = pl.pallas_call(
        begin_group,
        out_shape=[shape((pack_rows, width), BF16)]
        + [shape((n, quarter, width), BF16) for n in (2, 2, 3)]
        + [shape((piece, width), BF16)],
        in_specs=[smem] + [vmem] * 4,
        out_specs=[vmem] * 5,
        compiler_params=params(),
        name="begin_group",
    )(lengths, frames, w_conv.reshape(depth, width), w_proj, b_conv[None])
    far0 = hop(own_piece, 2)
    near_pack = hop(pack, 1)
    cot_picks = pl.pallas_call(
        pick,
        out_shape=[shape((n, quarter, width), BF16) for n in (2, 2, 3)],
        in_specs=[smem, vmem],
        out_specs=[vmem] * 3,
        compiler_params=params(),
        name="pick_cotangent",
    )(lengths, after(cotangent, *frame_picks))
    far0, near_pack, *cot_picks = lax.optimization_barrier((far0, near_pack, *cot_picks))
    far_frames = hop(frame_picks[2], 2)
    near_frames = hop(frame_picks[1], 1)
    far1, far2, near_frames = lax.optimization_barrier((dp_hop(far0, 1), dp_hop(far0, 2), near_frames))
    last = [dp_hop(far2[: piece // 2], 1), dp_hop(far1[piece // 2 :], 2)]
    frame_parts = [frame_picks[0], near_frames, far_frames, hop(far_frames[:2], 1)]
    cot_near = hop(after(cot_picks[1], far_frames), 1)
    cot_far = hop(after(cot_picks[2], far_frames), 2)

    rows = length + length // 2
    normed, stats, mixed = pl.pallas_call(
        attention_forward,
        out_shape=(
            shape((space, width), F32),
            shape((space, 128), F32),
            shape((space, width), BF16),
        ),
        in_specs=[smem] + [vmem] * 7,
        out_specs=[anywhere] * 3,
        scratch_shapes=[
            pltpu.VMEM((2, padded, width), BF16),
            pltpu.VMEM((2, padded, 2 * width), BF16),
            pltpu.VMEM((2, 2, length, width), BF16),
            pltpu.VMEM((2, length, width), F32),
            pltpu.VMEM((2, length, 128), F32),
            pltpu.VMEM((2, length, width), BF16),
            pltpu.SemaphoreType.DMA((2, 3, length // BLOCK)),
        ],
        compiler_params=params(),
        cost_estimate=cost(1e6, 1e5),
        name="attention_forward",
    )(after(lengths, near_pack), *near(*frame_parts), w_qkv, w_out, b_out)

    *last, cot_near, cot_far, normed = lax.optimization_barrier((*last, cot_near, cot_far, normed))
    cot_parts = [cot_picks[0], cot_near, cot_far, hop(cot_far[:2], 1)]
    far_pack = jnp.concatenate([far0, far1, far2] + last)
    far_near_pack = hop(far_pack, 1)
    packs = (pack, near_pack, far_pack, far_near_pack)

    chunk_rows = (depth + width) // 2
    block_count = limit // BLOCK
    result = pl.pallas_call(
        feed_forward,
        out_shape=[shape((n, quarter, width), BF16) for n in (2, 2, 4)]
        + [shape((2, 4, chunk_rows // 2, width), BF16)] * 2
        + [
            shape((limit, filters), BF16),
            shape((limit, width), F32),
            shape((depth, filters), BF16),
            shape((8, width), F32),
            shape((8, filters), F32),
        ],
        in_specs=[smem, anywhere] + [vmem] * 4 + [anywhere] * 4 + [vmem] * 5,
        out_specs=[vmem] * 3 + [anywhere] * 5 + [vmem] * 2,
        scratch_shapes=[
            pltpu.VMEM((pack_rows, filters), BF16),
            pltpu.VMEM((limit, width), F32),
            pltpu.VMEM((limit + 2 * HALO, width), F32),
            pltpu.VMEM((limit, depth), BF16),
            pltpu.VMEM((2, BLOCK, filters), F32),
            pltpu.VMEM((BLOCK, filters), F32),
            pltpu.VMEM((limit, filters), BF16),
            pltpu.VMEM((limit, width), BF16),
            pltpu.VMEM((limit, filters), BF16),
            pltpu.VMEM((limit, width), F32),
            pltpu.VMEM((4, depth + width, width), BF16),
            pltpu.VMEM((2, padded, width), BF16),
            pltpu.VMEM((space, width), BF16),
            pltpu.VMEM((space, width), BF16),
            pltpu.VMEM((padded, width), BF16),
            pltpu.SemaphoreType.DMA((FILTER_COPIES,)),
            pltpu.SemaphoreType.DMA((block_count,)),
            pltpu.SemaphoreType.DMA((2, block_count)),
            pltpu.SemaphoreType.DMA((taps + 1, 4, width // (chunk_rows // 10))),
            pltpu.SemaphoreType.DMA((1,)),
        ],
        compiler_params=pltpu.CompilerParams(vmem_limit_bytes=50 * 2**20),
        cost_estimate=cost(1e6, 1e5),
        name="feed_forward",
    )(lengths, normed, *near(*cot_parts, *packs), gain_one, shift_one, b_proj, gain_two, shift_two)
    (out_own, out_near, out_far), kept, sent = result[:3], result[3], result[4]
    d_hidden, dz_two, conv, small_two, conv_bias = result[5:]

    def add(a, b):
        return (a.astype(F32) + b.astype(F32)).astype(BF16)

    def total(*parts):
        return sum(part.astype(F32) for part in parts).astype(BF16)

    def halves(value, step):
        half = value.shape[-2] // 2
        bit = (dp_place // step) % 2
        axis = value.ndim - 2
        parts = value.reshape(value.shape[:-2] + (2, half, width))
        keep = lax.dynamic_index_in_dim(parts, bit, axis, keepdims=False)
        send = lax.dynamic_index_in_dim(parts, 1 - bit, axis, keepdims=False)
        return keep, dp_hop(send, step)

    def joined(value, other, step):
        bit = (dp_place // step) % 2
        return jnp.where(bit == 0, jnp.concatenate([value, other]), jnp.concatenate([other, value]))

    def collected(places, parts, dtype, name):
        return pl.pallas_call(
            functools.partial(collect, places),
            out_shape=shape((count, quarter, width), dtype),
            in_specs=[smem] + [vmem] * len(parts),
            out_specs=vmem,
            compiler_params=params(),
            name=name,
        )(lengths, *near(*parts))

    more = [2**i for i in range(2, 20) if 2**i < dp_size]
    got = hop(sent, 1)
    out_far = hop(out_far, 2)
    out_near = hop(out_near, 1)

    d_first = pl.pallas_call(
        conv_backward,
        out_shape=shape((limit, width), F32),
        in_specs=[smem] + [anywhere] * 3,
        out_specs=anywhere,
        scratch_shapes=[
            pltpu.VMEM((depth, filters), BF16),
            pltpu.VMEM((limit, filters), BF16),
            pltpu.VMEM((limit, width), F32),
            pltpu.VMEM((limit, width), F32),
            pltpu.VMEM((limit + HALO, width), F32),
            pltpu.SemaphoreType.DMA((taps,)),
            pltpu.SemaphoreType.DMA((2, block_count)),
            pltpu.SemaphoreType.DMA((1, block_count)),
        ],
        compiler_params=params(),
        cost_estimate=cost(1e6, 1e5),
        name="conv_backward",
    )(lengths, d_hidden, conv, dz_two)

    def attention_back(part, arrays, inputs, ties):
        late_rows = width + SMALL_ROWS
        if part:
            out_shapes = [shape((late_rows, width), BF16)] * 4
            out_specs = [vmem] * 4
            more_scratch = [pltpu.VMEM((4, width, width), BF16)]
        else:
            out_shapes = [
                shape((width, 3 * width), F32),
                shape((space, width), F32),
                shape((space, width), BF16),
                shape((space, 128), F32),
                shape((width, width), F32),
                shape((8, width), F32),
            ]
            out_specs = [vmem] + [anywhere] * 3 + [vmem] * 2
            more_scratch = [
                pltpu.VMEM((limit, width), F32),
                pltpu.VMEM((limit, width), F32),
                pltpu.VMEM((limit, 128), F32),
                pltpu.VMEM((limit, width), BF16),
                pltpu.SemaphoreType.DMA((3, block_count)),
            ]
        held = length if part else limit
        return pl.pallas_call(
            functools.partial(attention_backward, part),
            out_shape=[shape((quarter, width), BF16)] * 2 + [shape((2, quarter, width), BF16)] + out_shapes,
            in_specs=[smem] + [anywhere] * 4 + [vmem] + [anywhere] * len(arrays) + [vmem] * len(inputs),
            out_specs=[vmem] * 3 + out_specs,
            scratch_shapes=[
                pltpu.VMEM((padded, width), BF16),
                pltpu.VMEM((padded, 3 * width), BF16),
                pltpu.VMEM((padded, 3 * width), BF16),
                pltpu.VMEM((length, width), F32),
                pltpu.VMEM((length, width), F32),
                pltpu.VMEM((padded, width), F32),
                pltpu.VMEM((held, width), F32),
                pltpu.VMEM((held, width), BF16),
                pltpu.VMEM((held, 128), F32),
                pltpu.SemaphoreType.DMA((4,)),
                pltpu.SemaphoreType.DMA((4, block_count)),
            ]
            + more_scratch,
            compiler_params=params(),
            cost_estimate=cost(1e6, 1e5),
            name=f"attention_backward_{'ac'[part]}",
        )(after(lengths, *ties), *frame_parts, w_qkv, *arrays, *inputs)

    got, out_far, out_near = lax.optimization_barrier((got, out_far, out_near, d_first))[:3]
    send_x, send_y = total(kept[1, :2], got[1, :2]), total(kept[1, 2:], got[1, 2:])
    got_x, got_y = dp_hop(send_x, 1), hop(send_y, 2)
    out_beyond = hop(out_far[2:], 1)
    a_own, a_near, a_far, grad_qkv, dz_one, d_mixed, soft, grad_out, small = attention_back(
        0, [d_first, normed, stats, mixed], [w_out, gain_one, small_two], [send_x, send_y]
    )
    got_x, got_y, out_beyond = lax.optimization_barrier((got_x, got_y, out_beyond, grad_qkv))[:3]
    send_x, send_y = total(kept[0, 1], got[0, 1], got_x[1]), total(kept[0, 3], got[0, 3], got_y[1])
    next_x, next_y = hop(send_x, 2), dp_hop(send_y, 2)
    a_far = hop(a_far, 2)
    c_own, c_near, c_far, late0, late1, late2, late3 = attention_back(
        1, [dz_one, d_mixed, soft], [grad_qkv, grad_out, small, conv_bias], [send_x, send_y]
    )
    next_x, next_y = lax.optimization_barrier((next_x, next_y, late0))[:2]
    state = [total(kept[0, 0], got[0, 0], got_x[0], next_x), total(kept[0, 2], got[0, 2], got_y[0], next_y)]

    late_parts = [hop(after(part, *state), d) for d, part in ((1, late1), (2, late2), (3, late3))]
    moving = [halves(state[0], 2), halves(state[1], 1)]
    late = total(late0, *late_parts)
    state = jnp.concatenate([add(keep, after(other, late)) for keep, other in moving])
    c_far = hop(after(c_far, late), 2)
    others = [dp_hop(state, step) for step in more[:1]]
    late_parts = [dp_hop(late, step) for step in (1, 2, 3)]
    output = collected(
        [((0, 0), (0, 1)), ((1, 0), (1, 1)), ((2, 0), (2, 1)), ((3, 0), (3, 1))],
        [after(out_own, late), out_near, out_far, out_beyond],
        BF16,
        "collect_output",
    )
    *others, p1, p2, p3, output, c_far = lax.optimization_barrier((*others, *late_parts, output, c_far))
    late = total(late, p1, p2, p3)
    for other in others:
        state = add(state, other)
    for step in more[1:]:
        state = add(state, dp_hop(state, step))
    state = jnp.split(state, 2)
    backs = [[2, 1], [1, 2]]
    others = [dp_hop(value, back[0]) for value, back in zip(state, backs)]
    near_grads = hop(after(jnp.stack([a_near, c_near, a_far[1], c_far[1]]), late), 1)
    for step in more:
        late = add(late, dp_hop(late, step))
    *others, late, near_grads = lax.optimization_barrier((*others, late, near_grads))
    state = [joined(value, other, back[0]) for value, other, back in zip(state, others, backs)]
    last = [back[-1] for back in backs]
    others = [dp_hop(value, step) for value, step in zip(state, last)]
    blocks = [hop(late[:width], d) for d in (1, 2, 3)]
    d_frames = collected(
        [((0, None), (1, None)), ((2, 0), (2, 1)), ((3, 0), (4, 0)), ((2, 2), (2, 3))],
        [a_own, c_own, near_grads, a_far, c_far],
        F32,
        "collect_grad",
    )
    grad_conv, grad_proj = pl.pallas_call(
        functools.partial(finish_filters, last),
        out_shape=(shape((depth, width), F32), shape((width, width), F32)),
        in_specs=[vmem] * 4,
        out_specs=[vmem] * 2,
        scratch_shapes=[pltpu.VMEM((depth + width, width), BF16)],
        compiler_params=params(),
        name="finish_filters",
    )(*near(*[part for pair in zip(state, others) for part in pair]))
    grad_qkv, grad_out, *vectors = pl.pallas_call(
        finish_late,
        out_shape=[shape((width, 3 * width), F32), shape((width, width), F32)] + [shape((1, width), F32)] * 7,
        in_specs=[vmem] * 4,
        out_specs=[vmem] * 9,
        scratch_shapes=[pltpu.VMEM((4, width, width), F32)],
        compiler_params=params(),
        name="finish_late",
    )(*near(late, *blocks))
    vectors = [v.reshape(width) for v in vectors]
    return (
        output,
        d_frames,
        grad_qkv,
        grad_out,
        vectors[0],
        vectors[1],
        vectors[2],
        grad_conv.reshape(w_conv.shape),
        vectors[6],
        grad_proj,
        vectors[3],
        vectors[4],
        vectors[5],
    )


def solution(mesh):
    return jax.shard_map(
        shards,
        mesh=mesh,
        in_specs=(
            P("dp", "tensor", None),
            P("dp"),
            P(),
            P(),
            P(),
            P(),
            P(),
            P(None, None, "tensor"),
            P("tensor"),
            P("tensor", None),
            P(),
            P(),
            P(),
            P("dp", "tensor", None),
        ),
        out_specs=(
            P("dp", "tensor", None),
            P("dp", "tensor", None),
            P(),
            P(),
            P(),
            P(),
            P(),
            P(None, None, "tensor"),
            P("tensor"),
            P("tensor", None),
            P(),
            P(),
            P(),
        ),
        check_vma=False,
    )
```
